32 devices in a mesh: dp: 4 (over x, core), fsdp: 8 (over z, y).
Axes of the slice: x: 2, y: 2, z: 4, core: 2. Of those that a mesh axis runs over, the one named last changes fastest.
Arguments:
- lookback: bfloat16 [64, 864, 96], P(('dp', 'fsdp')), may hold values from -6 to 6
- bucket_size: int32 [64], P(('dp', 'fsdp')), may hold values from 32 to 864, as said below
- variate_mask: int32 [64, 864], P(('dp', 'fsdp')), may hold values from 0 to 1, as said below
- w_embed: bfloat16 [512, 96], P(('dp', 'fsdp')), may hold values from -0.625 to 0.625
- w_qkv: bfloat16 [1536, 512], P(('dp', 'fsdp')), may hold values from -0.25 to 0.25
- w_out: bfloat16 [512, 512], P(('dp', 'fsdp')), may hold values from -1.5 to 1.5
- w_up: bfloat16 [2048, 512], P(('dp', 'fsdp')), may hold values from -0.25 to 0.25
- w_down: bfloat16 [512, 2048], P(('dp', 'fsdp')), may hold values from -0.125 to 0.125
- up_bias: bfloat16 [2048], P(('dp', 'fsdp')), may hold values from -4 to 4
- biases: bfloat16 [7, 512], P(None, ('dp', 'fsdp')), may hold values from -4 to 4
- gains: bfloat16 [2, 512], P(None, ('dp', 'fsdp')), may hold values from 0.5 to 1.5
- cotangent: bfloat16 [64, 864, 512], P(('dp', 'fsdp')), may hold values from -6 to 6
Outputs:
- layer_out: bfloat16 [64, 864, 512], P(('dp', 'fsdp'))
- lookback_grad: float32 [64, 864, 96], P(('dp', 'fsdp'))
- grad_embed: float32 [512, 96], P(('dp', 'fsdp'))
- grad_qkv: float32 [1536, 512], P(('dp', 'fsdp'))
- grad_out: float32 [512, 512], P(('dp', 'fsdp'))
- grad_up: float32 [2048, 512], P(('dp', 'fsdp'))
- grad_down: float32 [512, 2048], P(('dp', 'fsdp'))
- grad_up_bias: float32 [2048], P(('dp', 'fsdp'))
- grad_biases: float32 [7, 512], P(None, ('dp', 'fsdp'))
- grad_gains: float32 [2, 512], P(None, ('dp', 'fsdp'))
The draws below stay inside these ranges and needn't reach their ends.
Inputs may be any that keep to these rules, and one draw needn't show every extreme that they name: `bucket_size`: each region is cut into windows of either 32 or 864 rows; both kinds of region occur in every draw. `variate_mask`: in a region with bucket 864 the single window's first 321 or first 862 rows are real variates; in a region with bucket 32 every window's first 7 or first 21 rows are; all other rows are padding.
All inputs are finite; a program needn't handle non-finite values.
Results may differ from the reference program's by a relative error of at most 0.013.
The reference program's roundings to bfloat16 on the way count: a program that leaves them out, or rounds other values in their place, can miss the bound.
Values may be sent and summed in bfloat16 or wider, within the bound.
No kernel may reach another device: no remote copies, remote signals or barrier semaphores. Data moves between devices by JAX's collectives and lax.ppermute only.
A program may use at most 128 MiB of HBM per device.

```python
import jax
import jax.numpy as jnp
from jax import lax

D = 512
HEADS = 8
HEAD_DIM = 64
FF = 2048
L_IN = 96
BIG = 864
SMALL = 32
VARS_A = 7
VARS_B = 21
VARS_C = 321
VARS_D = 862
REGIONS = 64


def region_layout(key):
    key = jax.random.fold_in(key, 11)
    kind_key, small_key, big_key, spot_key = jax.random.split(key, 4)
    small_region = jax.random.randint(kind_key, (REGIONS,), 0, 2)
    spot = jax.random.randint(spot_key, (), 0, REGIONS)
    places = jnp.arange(REGIONS)
    small_region = jnp.where(places == spot, 1, small_region)
    small_region = jnp.where(places == (spot + 1) % REGIONS, 0, small_region)
    big_pick = jax.random.randint(big_key, (REGIONS,), 0, 2)
    small_pick = jax.random.randint(small_key, (REGIONS, BIG // SMALL), 0, 2)
    return (small_region, big_pick, small_pick)


def draw_bucket_size(key, part):
    small_region, big_pick, small_pick = region_layout(key)
    return jnp.where(small_region == 1, SMALL, BIG).astype(jnp.int32)


def draw_variate_mask(key, part):
    small_region, big_pick, small_pick = region_layout(key)
    rows = jnp.arange(BIG)
    count_big = jnp.where(big_pick == 1, VARS_D, VARS_C)
    count_small = jnp.where(small_pick == 1, VARS_B, VARS_A)[:, rows // SMALL]
    small_valid = rows[None, :] % SMALL < count_small
    big_valid = rows[None, :] < count_big[:, None]
    return jnp.where(small_region[:, None] == 1, small_valid, big_valid).astype(jnp.int32)


def with_spikes(array, rng, source, target, parts, factor):
    owner, partner = [(jnp.arange(array.shape[position]) // (array.shape[position] // parts)).reshape([-1 if axis == position else 1 for axis in range(array.ndim)]) for position in (source, target)]
    chosen = jax.random.permutation(rng, parts)[partner]
    strong = (owner == chosen) | (owner == (partner + parts // 2) % parts)
    return jnp.where(strong, factor * array, array)


def level_of(key, dims, cuts, smallest, top_value):
    factor_of, own = 1.0, jax.random.fold_in(key, 6)
    for axis_at, blocks in cuts:
        draws = jnp.exp(jax.random.uniform(jax.random.fold_in(own, axis_at), (blocks,), jnp.float32, smallest / len(cuts), top_value / len(cuts)))
        factor_of = factor_of * jnp.repeat(draws, dims[axis_at] // blocks).reshape([-1 if axis == axis_at else 1 for axis in range(len(dims))])
    return factor_of


def gaussian(key, shape, scale, limit, cuts=(), kind=jnp.bfloat16):
    drawn = scale * jax.random.normal(key, shape, jnp.float32)
    if cuts:
        drawn = drawn * level_of(key, shape, cuts, -0.22, 0.18)
    return jnp.clip(drawn, -limit, limit).astype(kind)


def heavy_noise(stream_key, shape, scale, limit, cuts, heavy, kind=jnp.bfloat16):
    array = scale * jax.random.normal(stream_key, shape, jnp.float32)
    if cuts:
        array = array * level_of(stream_key, shape, cuts, -0.22, 0.18)
    return jnp.clip(with_spikes(array, jax.random.fold_in(stream_key, 3), *heavy), -limit, limit).astype(kind)


def setup_inputs(seed: int = 0) -> dict:
    key_list = jax.random.split(jax.random.key(seed), 13)
    return {
        "lookback": gaussian(key_list[0], (REGIONS, BIG, L_IN), 1.0, 6.0, ((0, 32),)),
        "bucket_size": draw_bucket_size(jax.random.fold_in(key_list[12], 71), 0),
        "variate_mask": draw_variate_mask(jax.random.fold_in(key_list[12], 71), 0),
        "w_embed": gaussian(key_list[3], (D, L_IN), L_IN ** -0.5, 0.625, ((0, 32),)),
        "w_qkv": gaussian(key_list[4], (3 * D, D), D ** -0.5, 0.25, ((0, 32),)),
        "w_out": gaussian(key_list[5], (D, D), (D // 32) ** -0.5, 1.5, ((0, 32),)),
        "w_up": gaussian(key_list[6], (FF, D), D ** -0.5, 0.25, ((0, 32),)),
        "w_down": gaussian(key_list[7], (D, FF), FF ** -0.5, 0.125, ((0, 32),)),
        "up_bias": gaussian(key_list[8], (FF,), 0.3, 4.0, ((0, 32),)),
        "biases": gaussian(key_list[9], (7, D), 0.3, 4.0, ((1, 32),)),
        "gains": jnp.clip(1.0 + 0.1 * jax.random.normal(key_list[10], (2, D), jnp.float32), 0.5, 1.5).astype(jnp.bfloat16),
        "cotangent": heavy_noise(key_list[11], (REGIONS, BIG, D), 1.0, 6.0, ((0, 32),), (0, 2, 32, 2.75)),
    }


@jax.custom_vjp
def low(v):
    return lax.optimization_barrier(v.astype(jnp.bfloat16)).astype(jnp.float32)

@jax.custom_vjp
def low_back(v):
    return v

def low_keep(v):
    return (low(v), None)

def low_pass(kept, grad):
    return (grad,)

def back_keep(v):
    return (v, None)

def back_low(kept, grad):
    return (low(grad),)
low.defvjp(low_keep, low_pass)
low_back.defvjp(back_keep, back_low)
norm_eps = 1e-05
masked_score = -1e+30
gelu_coef = 0.7978845608028654

def layer_norm(values, gain, shift):
    center = values - lax.optimization_barrier(jnp.mean(values, axis=-1, keepdims=True))
    spread = lax.optimization_barrier(jnp.mean(center * center, axis=-1, keepdims=True))
    return center * lax.rsqrt(spread + norm_eps) * gain + shift

def gelu_tanh(values):
    return 0.5 * values * (1.0 + jnp.tanh(gelu_coef * (values + 0.044715 * values * values * values)))

def forward(series, w_embed, w_qkv, w_out, w_up, w_down, up_bias, biases, gains, allowed):
    highest = lax.Precision.HIGHEST
    width = w_qkv.shape[1]
    count = series.shape[0]
    embed = low_back(jnp.dot(series, w_embed.T, precision=highest) + biases[0])
    embed_low = low(embed)
    project = jnp.dot(embed_low, w_qkv.T, precision=highest)
    query = low(low_back(project[:, :width] + biases[1])).reshape(count, HEADS, HEAD_DIM)
    keys = low(low_back(project[:, width:2 * width])).reshape(count, HEADS, HEAD_DIM)
    values = low(low_back(project[:, 2 * width:] + biases[2])).reshape(count, HEADS, HEAD_DIM)
    raw = low_back(jnp.einsum('qhd,khd->hqk', query, keys, precision=highest))
    scores = jnp.where(allowed[None], raw * HEAD_DIM ** (-0.5), masked_score)
    top = lax.optimization_barrier(jnp.max(scores, axis=-1, keepdims=True))
    expo = jnp.exp(scores - top)
    probs = low(expo / lax.optimization_barrier(jnp.sum(expo, axis=-1, keepdims=True)))
    mixed = jnp.einsum('hqk,khd->qhd', probs, values, precision=highest).reshape(count, width)
    attn = low(low_back(mixed))
    out_proj = low_back(jnp.dot(attn, w_out.T, precision=highest) + biases[3])
    hidden = layer_norm(embed + out_proj, gains[0], biases[4])
    upper = low_back(jnp.dot(low(hidden), w_up.T, precision=highest) + up_bias)
    active = low(gelu_tanh(upper))
    down = low_back(jnp.dot(active, w_down.T, precision=highest) + biases[5])
    return layer_norm(hidden + down, gains[1], biases[6])

def reference(lookback, bucket_size, variate_mask, w_embed, w_qkv, w_out, w_up, w_down, up_bias, biases, gains, cotangent):
    params = tuple((item.astype(jnp.float32) for item in (w_embed, w_qkv, w_out, w_up, w_down, up_bias, biases, gains)))
    places = jnp.arange(BIG, dtype=jnp.int32)

    def region(totals, pieces):
        series, size_now, valid, grad_in = pieces
        window = places // size_now
        allowed = (window[:, None] == window[None, :]) & (valid[None, :] > 0)

        def apply(series_f, *weights):
            return forward(series_f, *weights, allowed)
        result, back_fn = jax.vjp(apply, series.astype(jnp.float32), *params)
        grads = back_fn(grad_in.astype(jnp.float32) * valid[:, None].astype(jnp.float32))
        totals = tuple((total + grad for total, grad in zip(totals, grads[1:])))
        return (totals, (result.astype(jnp.bfloat16), grads[0]))
    zeros_init = tuple((jnp.zeros_like(item) for item in params))
    totals, (layer_out, lookback_grad) = lax.scan(region, zeros_init, (lookback, bucket_size, variate_mask, cotangent))
    return (layer_out, lookback_grad, totals[0], totals[1], totals[2], totals[3], totals[4], totals[5], totals[6], totals[7])
```

```python
import functools

import jax
import jax.numpy as jnp
from jax import lax
from jax.experimental import pallas as pl
from jax.experimental.pallas import tpu as pltpu
from jax.sharding import PartitionSpec as P

HEADS = 8
HEAD_DIM = 64
PIECES = 32
LANES = 128
TILE = 256
CHUNK = 512
SPAN = 512
AXES = ("dp", "fsdp")

norm_eps = 1e-05
masked_score = -1e30
gelu_coef = 0.7978845608028654

half = jnp.bfloat16
fp32 = jnp.float32

OFFSETS = tuple(
    core * 8 + x * 16 + y + z * 2
    for core in range(2)
    for x in range(2)
    for y in range(2)
    for z in range(4)
)

BIAS_AT = 96
GAIN_AT = 103
UP_AT = 105
UP_COLUMNS = 4


def dot(left, right, left_dim=1, right_dim=0):
    return lax.dot_general(
        left, right, (((left_dim,), (right_dim,)), ((), ())), preferred_element_type=fp32
    )


def params():
    return pltpu.CompilerParams(vmem_limit_bytes=62 * 2**20)


def cost(flops, moved):
    return pl.CostEstimate(flops=int(flops), bytes_accessed=int(moved), transcendentals=0)


VMEM = pl.BlockSpec(memory_space=pltpu.VMEM)
SMEM = pl.BlockSpec(memory_space=pltpu.SMEM)
ANY = pl.BlockSpec(memory_space=pl.ANY)


def piece_copies(me, refs, sem, place):
    copies = []
    at = 0
    for ref in refs:
        for i in range(ref.shape[0]):
            owner = jnp.bitwise_xor(me, OFFSETS[at])
            for source, target in place(ref.at[i], owner):
                copies.append(pltpu.make_async_copy(source, target, sem))
            at += 1
    return copies


def rows_of(owner, count):
    return pl.ds(pl.multiple_of(owner * count, 16), count)


def owners(me):
    return [jnp.bitwise_xor(me, offset) for offset in OFFSETS]


def across(column, lanes=LANES):
    return jnp.broadcast_to(column.astype(fp32), (column.shape[0], lanes))


def prepare_kernel(small, bucket_ref, mask_ref, lb_ref, ct_ref, series_ref, masked_ref, qf_ref, kf_ref):
    regions, rows = mask_ref.shape
    padded = qf_ref.shape[2]
    lags, width = lb_ref.shape[1], ct_ref.shape[2]
    last = rows // small - 1
    spare = padded - rows
    number = lax.broadcasted_iota(jnp.int32, (HEAD_DIM, padded), 0) - 16
    place = lax.broadcasted_iota(jnp.int32, (HEAD_DIM, padded), 1)
    counted = (number >= 0) & (number <= last)
    below = lax.broadcasted_iota(jnp.int32, (LANES - lags, padded), 0)
    for r in range(regions):
        lanes = slice(r * padded, (r + 1) * padded)
        valid = jnp.concatenate([mask_ref[r : r + 1, :].astype(fp32), jnp.zeros((1, spare), fp32)], axis=1)
        turned = jnp.concatenate([ct_ref[r].T, jnp.zeros((width, spare), half)], axis=1)
        masked_ref[:, lanes] = (turned.astype(fp32) * valid).astype(half)
        values = jnp.concatenate([lb_ref[r], jnp.zeros((lags, spare), half)], axis=1)
        series_ref[:lags, lanes] = values
        series_ref[lags:, lanes] = jnp.where(below == 0, 1.0, 0.0).astype(half)
        bucket = bucket_ref[r]
        window = jnp.floor((place.astype(fp32) + 0.5) / bucket.astype(fp32)).astype(jnp.int32)
        window = jnp.minimum(window, last)
        qf_ref[r] = (
            jnp.where(counted & (window != number), masked_score, 0.0) + jnp.where(number == last + 1, 1.0, 0.0)
        ).astype(half)
        kf_ref[r] = (
            jnp.where(counted & (window == number), 1.0, 0.0)
            + jnp.where((number >= -16) & (number < -13), 1.0, 0.0)
            + jnp.where(number == last + 1, jnp.where(valid > 0, 0.0, masked_score), 0.0)
        ).astype(half)


def prepare(bucket_size, variate_mask, lookback_t, cotangent, padded, small):
    regions, rows, width = cotangent.shape
    tokens = regions * padded
    feature = jax.ShapeDtypeStruct((regions, HEAD_DIM, padded), half)
    return pl.pallas_call(
        functools.partial(prepare_kernel, small),
        in_specs=[SMEM, VMEM, VMEM, VMEM],
        out_specs=[VMEM] * 4,
        out_shape=[
            jax.ShapeDtypeStruct((LANES, tokens), half),
            jax.ShapeDtypeStruct((width, tokens), half),
            feature,
            feature,
        ],
        compiler_params=params(),
        cost_estimate=cost(1e7, 8e6),
    )(bucket_size, variate_mask, lookback_t, cotangent)


def build_first(raw, w1):
    turned = raw[:, LANES:].astype(fp32).T
    for owner in range(PIECES):
        at = slice(owner * 16, owner * 16 + 16)
        short = turned[:16, at]
        w1[at, :] = jnp.concatenate(
            [raw[at, :BIAS_AT].astype(fp32), short[:, :9], jnp.zeros((16, LANES - BIAS_AT - 9), fp32)], axis=1
        ).astype(half)
    return turned


def scores_of(query, keys, query_f, key_f, rows):
    padded = query_f.shape[1]
    keys_t = jnp.concatenate([keys, key_f], axis=0).T[:rows]
    query_a = jnp.concatenate([query, query_f], axis=0)
    return [dot(keys_t, query_a[:, s : min(s + TILE, padded)]) for s in range(0, padded, TILE)]


def mix(scores, values, rows, store):
    values_a = jnp.concatenate([values[:, :rows], jnp.ones((16, rows), half)], axis=0)
    for i, score in enumerate(scores):
        top = jnp.max(score, axis=0, keepdims=True)
        expo = jnp.exp(score - top).astype(half)
        mixed = dot(values_a, expo)
        total = mixed[HEAD_DIM : HEAD_DIM + 1]
        lanes = slice(i * TILE, i * TILE + score.shape[1])
        store(lanes, (mixed[:HEAD_DIM] * (1.0 / total)).astype(half), top + jnp.log(total))


def heads_forward(count, read, query_f, key_f, rows, store):
    ahead = scores_of(read(0, 0), read(0, 1), query_f, key_f, rows)
    for i in range(count):
        scores = ahead
        if i + 1 < count:
            ahead = scores_of(read(i + 1, 0), read(i + 1, 1), query_f, key_f, rows)
        mix(scores, read(i, 2), rows, functools.partial(store, i))


def project_kernel(n_a, per_step, rows, regions, me_ref, *refs):
    a_refs, refs = refs[:n_a], refs[n_a:]
    series_ref, qf_ref, kf_ref, qkv_ref, emb_ref, attn_ref, log_ref, w1, turned_ref, wqkv_t, *refs = refs
    raw, wqkv, qkv_s, emb_s, sem, sem_out = refs
    step, steps = pl.program_id(0), pl.num_programs(0)
    padded = qf_ref.shape[2]
    width = emb_s.shape[0]
    outs = [
        pltpu.make_async_copy(qkv_s, qkv_ref, sem_out.at[0]),
        pltpu.make_async_copy(emb_s, emb_ref, sem_out.at[1]),
    ]

    @pl.when(step == 0)
    def _():
        def place(piece, owner):
            return [
                (piece.at[:, pl.ds(j * width, width)], wqkv.at[pl.ds(pl.multiple_of(owner * 48 + j * 16, 16), 16)])
                for j in range(3)
            ] + [(piece.at[:, pl.ds(3 * width, 2 * LANES)], raw.at[rows_of(owner, 16)])]

        copies = piece_copies(me_ref[0], a_refs, sem, place)
        for copy in copies:
            copy.start()
        for copy in copies:
            copy.wait()
        turned_ref[...] = build_first(raw, w1)
        bias_q = across(w1[:, BIAS_AT + 1 : BIAS_AT + 2], padded)
        bias_v = across(w1[:, BIAS_AT + 2 : BIAS_AT + 3], padded)
        for r in range(regions):
            lanes = slice(r * padded, (r + 1) * padded)
            low = dot(w1[...], series_ref[:, lanes]).astype(half)
            emb_s[:, lanes] = low
            for part in range(3):
                value = dot(wqkv[part * width : (part + 1) * width], low)
                if part == 0:
                    value = (value + bias_q) * HEAD_DIM**-0.5
                elif part == 2:
                    value = value + bias_v
                qkv_s[part * width : (part + 1) * width, lanes] = value.astype(half)
        for copy in outs:
            copy.start()
        wqkv_t[...] = wqkv[...].T

    region = step // (HEADS // per_step)
    first = lax.rem(step, HEADS // per_step) * per_step
    lanes = pl.ds(pl.multiple_of(region * padded, LANES), padded)

    def read(i, part):
        at = pl.multiple_of((first + i) * HEAD_DIM, HEAD_DIM)
        return qkv_s[pl.ds(part * width + at, HEAD_DIM), lanes]

    def store(i, lanes, mixed, log):
        attn_ref[i * HEAD_DIM : (i + 1) * HEAD_DIM, lanes] = mixed
        log_ref[0, i : i + 1, lanes] = log

    heads_forward(per_step, read, qf_ref[0], kf_ref[0], rows, store)

    @pl.when(step == steps - 1)
    def _():
        for copy in outs:
            copy.wait()


def head_blocks(padded, per_step, first=0):
    groups = HEADS // per_step

    def heads(part=0):
        return pl.BlockSpec(
            (per_step * HEAD_DIM, padded), lambda t: (part * groups + (t + first) % groups, (t + first) // groups)
        )

    feature = pl.BlockSpec((1, HEAD_DIM, padded), lambda t: ((t + first) // groups, 0, 0))
    log = pl.BlockSpec((1, per_step, padded), lambda t: (t + first, 0, 0))
    return heads, feature, log


def project(me, a_bufs, series, query_f, key_f, rows, width, per_step, steps):
    regions, _, padded = query_f.shape
    tokens = regions * padded
    heads, feature, log = head_blocks(padded, per_step)
    total_steps = regions * HEADS // per_step
    return pl.pallas_call(
        functools.partial(project_kernel, len(a_bufs), per_step, rows, regions),
        grid=(steps,),
        in_specs=[SMEM] + [ANY] * len(a_bufs) + [VMEM, feature, feature],
        out_specs=[ANY, ANY, heads(), log, VMEM, VMEM, VMEM],
        out_shape=[
            jax.ShapeDtypeStruct((3 * width, tokens), half),
            jax.ShapeDtypeStruct((width, tokens), half),
            jax.ShapeDtypeStruct((width, tokens), half),
            jax.ShapeDtypeStruct((total_steps, per_step, padded), fp32),
            jax.ShapeDtypeStruct((width, LANES), half),
            jax.ShapeDtypeStruct((LANES, width), fp32),
            jax.ShapeDtypeStruct((width, 3 * width), half),
        ],
        scratch_shapes=[
            pltpu.VMEM((width, 2 * LANES), half),
            pltpu.VMEM((3 * width, width), half),
            pltpu.VMEM((3 * width, tokens), half),
            pltpu.VMEM((width, tokens), half),
            pltpu.SemaphoreType.DMA,
            pltpu.SemaphoreType.DMA((2,)),
        ],
        compiler_params=params(),
        cost_estimate=cost(2e10, 1.5e7),
    )(me, *a_bufs, series, query_f, key_f)


def attend_kernel(per_step, rows, q_ref, k_ref, v_ref, qf_ref, kf_ref, *refs):
    attn_ref, log_ref = refs[-2:]

    def read(i, part):
        return (q_ref, k_ref, v_ref)[part][i * HEAD_DIM : (i + 1) * HEAD_DIM, :]

    def store(i, lanes, mixed, log):
        attn_ref[i * HEAD_DIM : (i + 1) * HEAD_DIM, lanes] = mixed
        log_ref[0, i : i + 1, lanes] = log

    heads_forward(per_step, read, qf_ref[0], kf_ref[0], rows, store)


def attend(qkv, attn, logs, query_f, key_f, rows, per_step, first):
    padded = query_f.shape[2]
    heads, feature, log = head_blocks(padded, per_step, first)
    return pl.pallas_call(
        functools.partial(attend_kernel, per_step, rows),
        grid=(logs.shape[0] - first,),
        in_specs=[heads(0), heads(1), heads(2), feature, feature, ANY, ANY],
        out_specs=[heads(), log],
        out_shape=[jax.ShapeDtypeStruct(attn.shape, half), jax.ShapeDtypeStruct(logs.shape, fp32)],
        input_output_aliases={5: 0, 6: 1},
        compiler_params=params(),
        cost_estimate=cost(1e10, 1e7),
    )(qkv, qkv, qkv, query_f, key_f, attn, logs)


NAMES = ("b3", "g0", "b4", "b5", "g1", "b6")
COLUMNS = {"b3": 99, "g0": 103, "b4": 100, "b5": 101, "g1": 104, "b6": 102}


def fold(value):
    total = value[:, :LANES]
    for s in range(LANES, value.shape[1], LANES):
        total = total + value[:, s : s + LANES]
    return total


def mean(value):
    return jnp.mean(value, axis=0, keepdims=True)


def feed_kernel(n_b, rows, regions, me_ref, *refs):
    b_refs, refs = refs[:n_b], refs[n_b:]
    w1_ref, turned_ref, series_ref, attn_ref, ct_ref, out_ref, gattn_ref, gres_ref, keep_ref, send_ref, small_ref, *refs = refs
    w_out, w_out_t, w_up, w_up_t, w_down, w_down_t, up_b, col, attn_s, ct_s, *refs = refs
    act_s, slope_s, gdown_s, hid_s, gproj_s, gattn_s, flow, norm_s, lo_s, acc, acc_up, sem_in, sem_w, sem_out, sem_g = refs
    width, units = w_up_t.shape
    chunks = units // CHUNK
    padded = attn_s.shape[1] // regions
    me = me_ref[0]
    lanes = [slice(r * padded, (r + 1) * padded) for r in range(regions)]

    loads = [
        (
            pltpu.make_async_copy(attn_ref.at[:, pl.ds(r * padded, padded)], attn_s.at[:, pl.ds(r * padded, padded)], sem_in.at[2 * r]),
            pltpu.make_async_copy(ct_ref.at[:, pl.ds(r * padded, padded)], ct_s.at[:, pl.ds(r * padded, padded)], sem_in.at[2 * r + 1]),
        )
        for r in range(regions)
    ]
    loads[0][0].start()
    groups = ([], [], [])
    at = 0
    owner_of = owners(me)
    for ref in b_refs:
        for i in range(ref.shape[0]):
            owner, piece = owner_of[at], ref.at[i]
            groups[0].append(pltpu.make_async_copy(piece.at[:, pl.ds(0, width)], w_out.at[rows_of(owner, 16)], sem_w.at[0]))
            for j in range(4):
                groups[1].append(
                    pltpu.make_async_copy(
                        piece.at[:, pl.ds((1 + j) * width, width)],
                        w_up.at[pl.ds(pl.multiple_of(owner * 64 + j * 16, 16), 16)],
                        sem_w.at[1],
                    )
                )
            groups[2].append(pltpu.make_async_copy(piece.at[:, pl.ds(5 * width, units)], w_down.at[rows_of(owner, 16)], sem_w.at[2]))
            at += 1
    for group in groups:
        for copy in group:
            copy.start()
    for first, second in loads:
        if first is not loads[0][0]:
            first.start()
        second.start()

    for i, name in enumerate(NAMES):
        col[i] = across(w1_ref[:, COLUMNS[name] : COLUMNS[name] + 1])
    for owner in range(PIECES):
        up_b[owner * 64 : owner * 64 + 64, :] = jnp.broadcast_to(
            turned_ref[:64, owner * 16 + 9 : owner * 16 + 10], (64, LANES)
        )

    def wide(value, size=padded):
        return jnp.concatenate([value] * (size // LANES), axis=1)

    def column(name):
        return wide(col[NAMES.index(name)])

    def add_to(r, name, value):
        i = NAMES.index(name)
        acc[i] = fold(value) if r == 0 else acc[i] + fold(value)

    rates = [None] * regions
    outs = []

    def leave(source, target):
        copy = pltpu.make_async_copy(source, target, sem_out.at[len(outs)])
        copy.start()
        outs.append(copy)

    def enter(r):
        loads[r][0].wait()
        embed = dot(w1_ref[...], series_ref[:, lanes[r]])
        resid = embed + (dot(w_out[...], attn_s[:, lanes[r]]) + column("b3"))
        center = resid - mean(resid)
        rates[r] = lax.rsqrt(mean(center * center) + norm_eps)
        norm = center * rates[r]
        norm_s[:, lanes[r]] = norm
        hidden = norm * column("g0") + column("b4")
        flow[:, lanes[r]] = hidden
        hid_s[:, lanes[r]] = hidden.astype(half)

    def up(r, c):
        part = slice(c * CHUNK, (c + 1) * CHUNK)
        upper = dot(w_up[part, :], hid_s[:, lanes[r]]) + wide(up_b[part, :])
        square = upper * upper
        turned = 0.5 + 0.5 * jnp.tanh(upper * (gelu_coef + (gelu_coef * 0.044715) * square))
        act = upper * turned
        slope = turned + act * (1.0 - turned) * (2.0 * gelu_coef + (6.0 * gelu_coef * 0.044715) * square)
        slope_s[part, lanes[r]] = slope.astype(half)
        act_s[part, lanes[r]] = act.astype(half)

    def down(r):
        flow[:, lanes[r]] = flow[:, lanes[r]] + (dot(w_down[...], act_s[:, lanes[r]]) + column("b5"))

    def turn(r):
        resid = flow[:, lanes[r]]
        center = resid - mean(resid)
        rate = lax.rsqrt(mean(center * center) + norm_eps)
        norm = center * rate
        lo_s[r * padded : (r + 1) * padded, :] = (norm * column("g1") + column("b6")).astype(half).T
        leave(lo_s.at[pl.ds(r * padded, rows)], out_ref.at[r])
        loads[r][1].wait()
        grad = ct_s[:, lanes[r]].astype(fp32)
        add_to(r, "b6", grad)
        add_to(r, "g1", grad * norm)
        grad = grad * column("g1")
        grad = rate * (grad - mean(grad) - norm * mean(grad * norm))
        add_to(r, "b5", grad)
        flow[:, lanes[r]] = grad
        gdown_s[:, lanes[r]] = grad.astype(half)

    def up_back(r, c):
        part = slice(c * CHUNK, (c + 1) * CHUNK)
        grad = slope_s[part, lanes[r]].astype(fp32) * dot(w_down_t[part, :], gdown_s[:, lanes[r]])
        acc_up[part, :] = fold(grad) if r == 0 else acc_up[part, :] + fold(grad)
        slope_s[part, lanes[r]] = grad.astype(half)

    def back(r):
        flow[:, lanes[r]] = flow[:, lanes[r]] + dot(w_up_t[...], slope_s[:, lanes[r]])

    def leave_norm(r):
        grad = flow[:, lanes[r]]
        norm = norm_s[:, lanes[r]]
        add_to(r, "b4", grad)
        add_to(r, "g0", grad * norm)
        grad = grad * column("g0")
        grad = rates[r] * (grad - mean(grad) - norm * mean(grad * norm))
        add_to(r, "b3", grad)
        flow[:, lanes[r]] = grad
        low = grad.astype(half)
        gproj_s[:, lanes[r]] = low
        gattn_s[:, lanes[r]] = dot(w_out_t[...], low).astype(half)
        leave(flow.at[:, pl.ds(r * padded, padded)], gres_ref.at[:, pl.ds(r * padded, padded)])
        leave(gattn_s.at[:, pl.ds(r * padded, padded)], gattn_ref.at[:, pl.ds(r * padded, padded)])

    for copy in groups[0]:
        copy.wait()
    enter(0)
    for copy in groups[1]:
        copy.wait()
    for r in range(regions):
        up(r, 0)
        if r == 0:
            for copy in groups[2]:
                copy.wait()
            w_out_t[...] = w_out[...].T
            w_down_t[...] = w_down[...].T
            w_up_t[...] = w_up[...].T
        up(r, 1)
        if r + 1 < regions:
            enter(r + 1)
        if r > 0:
            turn(r - 1)
        for c in range(2, chunks):
            up(r, c)
        down(r)
    for r in range(regions):
        up_back(r, 0)
        up_back(r, 1)
        if r == 0:
            turn(regions - 1)
        else:
            leave_norm(r - 1)
        for c in range(2, chunks):
            up_back(r, c)
        back(r)
    for c in range(chunks):
        part = slice(c * CHUNK, (c + 1) * CHUNK)
        w_down[:, part] = dot(gdown_s[...], act_s[part, :], 1, 1).astype(half)
    leave_norm(regions - 1)
    w_up[...] = dot(slope_s[...], hid_s[...], 1, 1).astype(half)
    w_out[...] = dot(gproj_s[...], attn_s[...], 1, 1).astype(half)
    copies = []
    for r, owner in enumerate(owner_of):
        target = (keep_ref if r < PIECES // 2 else send_ref).at[r % (PIECES // 2)]
        copies.append(pltpu.make_async_copy(w_out.at[rows_of(owner, 16)], target.at[:, pl.ds(0, width)], sem_g))
        for j in range(4):
            copies.append(
                pltpu.make_async_copy(
                    w_up.at[pl.ds(pl.multiple_of(owner * 64 + j * 16, 16), 16)],
                    target.at[:, pl.ds((1 + j) * width, width)],
                    sem_g,
                )
            )
        copies.append(pltpu.make_async_copy(w_down.at[rows_of(owner, 16)], target.at[:, pl.ds(5 * width, units)], sem_g))
    for copy in copies:
        copy.start()
    total = jnp.zeros((width, LANES), fp32)
    lane = lax.broadcasted_iota(jnp.int32, (width, LANES), 1)
    for i, name in enumerate(NAMES):
        total = total + jnp.where(lane == COLUMNS[name], jnp.sum(acc[i], axis=1, keepdims=True), 0.0)
    up_sum = jnp.sum(acc_up[...], axis=1, keepdims=True).reshape(PIECES, UP_COLUMNS, 16, 1)
    for c in range(UP_COLUMNS):
        total = total + jnp.where(lane == UP_AT + c, up_sum[:, c].reshape(width, 1), 0.0)
    small_ref[...] = total
    for copy in copies:
        copy.wait()
    for copy in outs:
        copy.wait()


def feed(me, b_bufs, w1, turned, series, attn, cotangent, regions, rows, units):
    width, tokens = attn.shape
    half_set = jax.ShapeDtypeStruct((PIECES // 2, 16, 5 * width + units), half)
    low_all = pltpu.VMEM((width, tokens), half)
    return pl.pallas_call(
        functools.partial(feed_kernel, len(b_bufs), rows, regions),
        in_specs=[SMEM] + [ANY] * len(b_bufs) + [VMEM, VMEM, VMEM, ANY, ANY],
        out_specs=[ANY] * 5 + [VMEM],
        out_shape=[
            jax.ShapeDtypeStruct((regions, rows, width), half),
            jax.ShapeDtypeStruct((width, tokens), half),
            jax.ShapeDtypeStruct((width, tokens), fp32),
            half_set,
            half_set,
            jax.ShapeDtypeStruct((width, LANES), fp32),
        ],
        scratch_shapes=[
            pltpu.VMEM((width, width), half),
            pltpu.VMEM((width, width), half),
            pltpu.VMEM((units, width), half),
            pltpu.VMEM((width, units), half),
            pltpu.VMEM((width, units), half),
            pltpu.VMEM((units, width), half),
            pltpu.VMEM((units, LANES), fp32),
            pltpu.VMEM((len(NAMES), width, LANES), fp32),
            low_all,
            low_all,
            pltpu.VMEM((units, tokens), half),
            pltpu.VMEM((units, tokens), half),
            low_all,
            low_all,
            low_all,
            low_all,
            pltpu.VMEM((width, tokens), fp32),
            pltpu.VMEM((width, tokens), fp32),
            pltpu.VMEM((tokens, width), half),
            pltpu.VMEM((len(NAMES), width, LANES), fp32),
            pltpu.VMEM((units, LANES), fp32),
            pltpu.SemaphoreType.DMA((2 * regions,)),
            pltpu.SemaphoreType.DMA((3,)),
            pltpu.SemaphoreType.DMA((3 * regions,)),
            pltpu.SemaphoreType.DMA,
        ],
        compiler_params=params(),
        cost_estimate=cost(4e10, 2e7),
    )(me, *b_bufs, w1, turned, series, attn, cotangent)


def heads_back(per_step, rows, refs, store):
    q_ref, k_ref, v_ref, attn_ref, gattn_ref, log_ref, qf_ref, kf_ref = refs
    padded = qf_ref.shape[2]
    query_f, key_f = qf_ref[0], kf_ref[0]
    blocks = [(s, min(TILE, rows - s)) for s in range(0, rows, TILE)]
    filler = jnp.zeros((13, padded), fp32)

    def in_three(row):
        first = row.astype(half).astype(fp32)
        left = row - first
        second = left.astype(half).astype(fp32)
        return jnp.concatenate([first, second, left - second, filler], axis=0).astype(half)

    for i in range(per_step):
        head = slice(i * HEAD_DIM, (i + 1) * HEAD_DIM)
        query, keys, values, grad = q_ref[head, :], k_ref[head, :], v_ref[head, :], gattn_ref[head, :]
        inner = jnp.sum(grad.astype(fp32) * attn_ref[head, :].astype(fp32), axis=0, keepdims=True)
        query_a = jnp.concatenate([query, in_three(-log_ref[0, i : i + 1, :]), query_f[16:]], axis=0).T
        grad_a = jnp.concatenate([grad, in_three(-inner), jnp.zeros((48, padded), half)], axis=0).T
        keys_a = jnp.concatenate([keys, key_f], axis=0)
        values_a = jnp.concatenate([values, key_f], axis=0)
        grad_keys = grad_values = None
        grad_query = []
        for s, n in blocks:
            probs = jnp.exp(dot(query_a[s : s + n], keys_a))
            raw = (probs * dot(grad_a[s : s + n], values_a)).astype(half)
            more_v = dot(grad[:, s : s + n], probs.astype(half))
            more_k = dot(query[:, s : s + n], raw)
            grad_values = more_v if grad_values is None else grad_values + more_v
            grad_keys = more_k if grad_keys is None else grad_keys + more_k
            grad_query.append((dot(keys, raw, 1, 1) * HEAD_DIM**-0.5).astype(half))
        grad_query.append(jnp.zeros((HEAD_DIM, padded - rows), half))
        store(i, (jnp.concatenate(grad_query, axis=1), grad_keys.astype(half), grad_values.astype(half)))


def attend_back_kernel(per_step, rows, *refs):
    grad_ref = refs[8]

    def store(i, three):
        for part, value in enumerate(three):
            grad_ref[0, part, i * HEAD_DIM : (i + 1) * HEAD_DIM, :] = value

    heads_back(per_step, rows, refs[:8], store)


def finish_kernel(per_step, rows, first, me_ref, *refs):
    ins = refs[:8]
    done_ref, emb_ref, gres_ref, series_ref, wqkv_t_ref, w1_ref, small_ref, keep_ref, send_ref, lbg_ref, *refs = refs[8:]
    grad_s, emb_s, gres_s, wqkv_t, g_qkv, g_one, sem, sem_out = refs
    step, steps = pl.program_id(0), pl.num_programs(0)
    width, tokens = emb_s.shape
    regions, lags, _ = lbg_ref.shape
    padded = tokens // regions
    groups = HEADS // per_step
    height = per_step * HEAD_DIM
    brought = [
        pltpu.make_async_copy(emb_ref, emb_s, sem),
        pltpu.make_async_copy(gres_ref, gres_s, sem),
        pltpu.make_async_copy(wqkv_t_ref, wqkv_t, sem),
    ]
    for t in range(first):
        for part in range(3):
            brought.append(
                pltpu.make_async_copy(
                    done_ref.at[t, part],
                    grad_s.at[
                        pl.ds(part * width + (t % groups) * height, height), pl.ds(t // groups * padded, padded)
                    ],
                    sem,
                )
            )

    @pl.when(step == 0)
    def _():
        for copy in brought:
            copy.start()

    now = step + first
    lanes = pl.ds(pl.multiple_of(now // groups * padded, LANES), padded)
    rows_at = lax.rem(now, groups) * height

    def store(i, three):
        for part, value in enumerate(three):
            at = pl.multiple_of(part * width + rows_at + i * HEAD_DIM, HEAD_DIM)
            grad_s[pl.ds(at, HEAD_DIM), lanes] = value

    heads_back(per_step, rows, ins, store)

    @pl.when(step == steps - 1)
    def _():
        for copy in brought:
            copy.wait()
        owner_of = owners(me_ref[0])
        for part in range(3):
            at = slice(part * width, (part + 1) * width)
            g_qkv[at, :] = dot(grad_s[at, :], emb_s[...], 1, 1).astype(half)
        copies = []
        for r, owner in enumerate(owner_of):
            target = (keep_ref if r < PIECES // 2 else send_ref).at[r % (PIECES // 2)]
            for j in range(3):
                copies.append(
                    pltpu.make_async_copy(
                        g_qkv.at[pl.ds(pl.multiple_of(owner * 48 + j * 16, 16), 16)],
                        target.at[:, pl.ds(j * width, width)],
                        sem_out.at[0],
                    )
                )
        for copy in copies:
            copy.start()
        series = series_ref[...]
        total = small_ref[...]
        lane = lax.broadcasted_iota(jnp.int32, total.shape, 1)
        for i, part in enumerate((0, 2)):
            bias = dot(grad_s[part * width : (part + 1) * width, :], series, 1, 1)
            total = total + jnp.where(lane == BIAS_AT + 1 + i, bias[:, BIAS_AT : BIAS_AT + 1], 0.0)
        for r in range(regions):
            part = slice(r * padded, (r + 1) * padded)
            low = (gres_s[:, part] + dot(wqkv_t[...], grad_s[:, part])).astype(half)
            total = total + dot(low, series_ref[:, part], 1, 1)
            lbg_ref[r] = dot(w1_ref[...], low, 0, 0)[:lags, :rows]
        g_one[...] = total.astype(half)
        more = []
        for r, owner in enumerate(owner_of):
            target = (keep_ref if r < PIECES // 2 else send_ref).at[r % (PIECES // 2)]
            more.append(
                pltpu.make_async_copy(
                    g_one.at[rows_of(owner, 16)], target.at[:, pl.ds(3 * width, LANES)], sem_out.at[1]
                )
            )
        for copy in more:
            copy.start()
        for copy in copies:
            copy.wait()
        for copy in more:
            copy.wait()


def back_operands(qkv, attn, grad_attn, logs, query_f, key_f, per_step, first):
    heads, feature, log = head_blocks(query_f.shape[2], per_step, first)
    specs = [heads(0), heads(1), heads(2), heads(), heads(), log, feature, feature]
    return specs, (qkv, qkv, qkv, attn, grad_attn, logs, query_f, key_f)


def attend_back(qkv, attn, grad_attn, logs, query_f, key_f, rows, per_step, steps):
    padded = query_f.shape[2]
    specs, operands = back_operands(qkv, attn, grad_attn, logs, query_f, key_f, per_step, 0)
    shape = (3, per_step * HEAD_DIM, padded)
    return pl.pallas_call(
        functools.partial(attend_back_kernel, per_step, rows),
        grid=(steps,),
        in_specs=specs,
        out_specs=pl.BlockSpec((1, *shape), lambda t: (t, 0, 0, 0)),
        out_shape=jax.ShapeDtypeStruct((steps, *shape), half),
        compiler_params=params(),
        cost_estimate=cost(2e10, 1e7),
    )(*operands)


def finish(me, qkv, attn, grad_attn, logs, query_f, key_f, done, embed_low, grad_resid, series, wqkv_t, w1, small, rows, lags, per_step):
    regions, _, padded = query_f.shape
    width, tokens = attn.shape
    first = done.shape[0]
    specs, operands = back_operands(qkv, attn, grad_attn, logs, query_f, key_f, per_step, first)
    half_set = jax.ShapeDtypeStruct((PIECES // 2, 16, 3 * width + LANES), half)
    return pl.pallas_call(
        functools.partial(finish_kernel, per_step, rows, first),
        grid=(logs.shape[0] - first,),
        in_specs=[SMEM] + specs + [ANY, ANY, ANY, VMEM, ANY, VMEM, VMEM],
        out_specs=[ANY, ANY, VMEM],
        out_shape=[half_set, half_set, jax.ShapeDtypeStruct((regions, lags, rows), fp32)],
        scratch_shapes=[
            pltpu.VMEM((3 * width, tokens), half),
            pltpu.VMEM((width, tokens), half),
            pltpu.VMEM((width, tokens), fp32),
            pltpu.VMEM((width, 3 * width), half),
            pltpu.VMEM((3 * width, width), half),
            pltpu.VMEM((width, LANES), half),
            pltpu.SemaphoreType.DMA,
            pltpu.SemaphoreType.DMA((2,)),
        ],
        compiler_params=params(),
        cost_estimate=cost(4e10, 2e7),
    )(me, *operands, done, embed_low, grad_resid, series, wqkv_t, w1, small)


def send(value, offset):
    return lax.ppermute(value, AXES, [(i, i ^ offset) for i in range(PIECES)])


def after(value, *others):
    return lax.optimization_barrier((value, *others))[0]


def along_z(piece):
    return jnp.stack([piece] + [send(piece, 2 * s) for s in range(1, 4)])


def along_plane(value):
    return [value] + [send(value, offset) for offset in (1, 16, 17)]


def along_core(plane):
    return plane + [send(part, 8) for part in plane]


def add(*terms):
    return sum(term.astype(fp32) for term in terms)


def sum_plane(low):
    got = [send(low[4 * i : 4 * i + 4], offset) for i, offset in ((1, 1), (2, 16), (3, 17))]
    return [low[:4]] + got


def sum_z(low):
    return [low[0]] + [send(low[s], 2 * s) for s in range(1, 4)]


def side_by_side(value):
    return [value[s : s + 16] for s in range(0, value.shape[0], 16)]


def stacked(value, width):
    return jnp.concatenate([value[:, s : s + width] for s in range(0, value.shape[1], width)], axis=0)


def short_block(biases, gains, up_bias):
    block = jnp.concatenate([biases, gains], axis=0)
    block = jnp.pad(block, ((0, 0), (0, LANES - block.shape[1])))
    up = jnp.pad(up_bias.reshape(1, -1), ((0, 6), (0, LANES - up_bias.shape[0])))
    return jnp.concatenate([block, up], axis=0)


def first_piece(w_embed, short, w_qkv):
    w_embed = jnp.pad(w_embed, ((0, 0), (0, LANES - w_embed.shape[1])))
    return jnp.concatenate([*side_by_side(w_qkv), w_embed, short], axis=1)


def second_piece(w_out, w_up, w_down):
    return jnp.concatenate([w_out, *side_by_side(w_up), w_down], axis=1)


def unpack_one(packed, lags):
    up = packed[:, UP_AT : UP_AT + UP_COLUMNS].reshape(-1, 16, UP_COLUMNS).transpose(0, 2, 1).reshape(-1)
    return packed[:, :lags], packed[:, BIAS_AT:GAIN_AT].T, packed[:, GAIN_AT:UP_AT].T, up


def body(
    ours,
    lookback,
    bucket_size,
    variate_mask,
    w_embed,
    w_qkv,
    w_out,
    w_up,
    w_down,
    up_bias,
    biases,
    gains,
    cotangent,
):
    regions, rows, lags = lookback.shape
    width = w_qkv.shape[1]
    units = w_down.shape[1]
    padded = -(-rows // LANES) * LANES
    per_step = 4
    steps = regions * HEADS // per_step
    lookback_t = lookback.transpose(0, 2, 1)
    series, masked, query_f, key_f = prepare(bucket_size, variate_mask, lookback_t, cotangent, padded, 32)

    if ours:
        index = lax.axis_index(AXES).astype(jnp.int32)
        z_a = along_z(first_piece(w_embed, short_block(biases, gains, up_bias), w_qkv))
        z_b = along_z(second_piece(w_out, w_up, w_down))
        plane_a = along_plane(after(z_a, series))
        plane_b = along_plane(after(z_b, z_a))
        a_bufs = along_core(plane_a)
    else:
        index = jnp.zeros((), jnp.int32)

        def whole(value, axis=0):
            return lax.all_gather(value, AXES, axis=axis, tiled=True)

        def cut(value, axis=0):
            shape = value.shape[:axis] + (PIECES, value.shape[axis] // PIECES) + value.shape[axis + 1 :]
            return jnp.moveaxis(value.reshape(shape), axis, 0)

        short = jax.vmap(short_block)(cut(whole(biases, 1), 1), cut(whole(gains, 1), 1), cut(whole(up_bias)))
        a_bufs = [jax.vmap(first_piece)(cut(whole(w_embed)), short, cut(whole(w_qkv)))]
        b_bufs = [jax.vmap(second_piece)(cut(whole(w_out)), cut(whole(w_up)), cut(whole(w_down)))]
    me = index.reshape(1)

    qkv, embed_low, attn, logs, w1, turned, wqkv_t = project(
        me, a_bufs, series, query_f, key_f, rows, width, per_step, steps - 1
    )
    if ours:
        b_bufs = along_core([after(part, logs) for part in plane_b])
    attn, logs = attend(qkv, attn, logs, query_f, key_f, rows, per_step, steps - 1)
    layer_out, grad_attn, grad_resid, keep_b, send_b, sums = feed(
        me, b_bufs, w1, turned, series, attn, masked, regions, rows, units
    )
    if ours:
        core_b = send(send_b, 8)
    done = attend_back(qkv, attn, grad_attn, logs, query_f, key_f, rows, per_step, 1)
    if ours:
        low_b = add(keep_b, after(core_b, done)).astype(half)
        parts_b = sum_plane(low_b)
        done = after(done, low_b)
    keep_a, send_a, lookback_grad = finish(
        me, qkv, attn, grad_attn, logs, query_f, key_f, done, embed_low, grad_resid, series, wqkv_t, w1, sums, rows, lags, per_step
    )
    lookback_grad = lookback_grad.transpose(0, 2, 1)

    def parts_of(grad_a, grad_b):
        w_qkv_part = stacked(grad_a[:, : 3 * width], width)
        return w_qkv_part, grad_a[:, 3 * width :], grad_b[:, :width], stacked(grad_b[:, width : 5 * width], width), grad_b[:, 5 * width :]

    if ours:
        core_a = send(send_a, 8)
        low_b = add(*[after(part, keep_a) for part in parts_b]).astype(half)
        z_parts_b = sum_z(low_b)
        low_a = add(keep_a, core_a).astype(half)
        low_a = add(*sum_plane(low_a)).astype(half)
        grad_b = add(*[after(part, low_a) for part in z_parts_b])
        grad_a = add(*sum_z(low_a))
        grad_qkv, packed, grad_out, grad_up, grad_down = parts_of(grad_a, grad_b)
        grad_embed, grad_biases, grad_gains, grad_up_bias = unpack_one(packed, lags)
    else:
        def shared(value, axis=0):
            return lax.psum_scatter(value, AXES, scatter_dimension=axis, tiled=True)

        order = jnp.argsort(jnp.array(OFFSETS, jnp.int32))
        grad_a = jnp.concatenate([keep_a, send_a], axis=0).astype(fp32)[order]
        grad_b = jnp.concatenate([keep_b, send_b], axis=0).astype(fp32)[order]
        whole_parts = [value.reshape(-1, value.shape[-1]) for value in jax.vmap(parts_of)(grad_a, grad_b)]
        grad_embed, grad_biases, grad_gains, grad_up_bias = unpack_one(whole_parts[1], lags)
        grad_qkv, grad_out, grad_up, grad_down = (shared(whole_parts[i]) for i in (0, 2, 3, 4))
        grad_embed, grad_up_bias = shared(grad_embed), shared(grad_up_bias)
        grad_biases, grad_gains = shared(grad_biases, 1), shared(grad_gains, 1)
    return (
        layer_out,
        lookback_grad,
        grad_embed,
        grad_qkv,
        grad_out,
        grad_up,
        grad_down,
        grad_up_bias,
        grad_biases,
        grad_gains,
    )


def solution(mesh):
    one = P(AXES)
    rows = P(AXES, None)
    blocks = P(AXES, None, None)
    columns = P(None, AXES)
    in_specs = (blocks, one, rows, rows, rows, rows, rows, rows, one, columns, columns, blocks)
    out_specs = (blocks, blocks, rows, rows, rows, rows, rows, one, columns, columns)
    ours = tuple(mesh.shape[axis] for axis in AXES) == (4, 8)
    return jax.shard_map(
        functools.partial(body, ours), mesh=mesh, in_specs=in_specs, out_specs=out_specs, check_vma=False
    )
```

```python
import functools

import jax
import jax.numpy as jnp
from jax import lax
from jax.experimental import pallas as pl
from jax.experimental.pallas import tpu as pltpu
from jax.sharding import PartitionSpec as P

HEADS = 8
HEAD_DIM = 64
PIECES = 32
LANES = 128
TILE = 256
CHUNK = 512
SPAN = 512
AXES = ("dp", "fsdp")

norm_eps = 1e-05
masked_score = -1e30
gelu_coef = 0.7978845608028654

half = jnp.bfloat16
fp32 = jnp.float32

OFFSETS = tuple(
    core * 8 + x * 16 + y + z * 2
    for core in range(2)
    for x in range(2)
    for y in range(2)
    for z in range(4)
)

BIAS_AT = 96
GAIN_AT = 103
UP_AT = 105
UP_COLUMNS = 4


def dot(left, right, left_dim=1, right_dim=0):
    return lax.dot_general(
        left, right, (((left_dim,), (right_dim,)), ((), ())), preferred_element_type=fp32
    )


def params():
    return pltpu.CompilerParams(vmem_limit_bytes=62 * 2**20)


def cost(flops, moved):
    return pl.CostEstimate(flops=int(flops), bytes_accessed=int(moved), transcendentals=0)


VMEM = pl.BlockSpec(memory_space=pltpu.VMEM)
SMEM = pl.BlockSpec(memory_space=pltpu.SMEM)
ANY = pl.BlockSpec(memory_space=pl.ANY)


def piece_copies(me, refs, sem, place):
    copies = []
    at = 0
    for ref in refs:
        for i in range(ref.shape[0]):
            owner = jnp.bitwise_xor(me, OFFSETS[at])
            for source, target in place(ref.at[i], owner):
                copies.append(pltpu.make_async_copy(source, target, sem))
            at += 1
    return copies


def rows_of(owner, count):
    return pl.ds(pl.multiple_of(owner * count, 16), count)


def owners(me):
    return [jnp.bitwise_xor(me, offset) for offset in OFFSETS]


def across(column, lanes=LANES):
    return jnp.broadcast_to(column.astype(fp32), (column.shape[0], lanes))


def prepare_kernel(small, bucket_ref, mask_ref, lb_ref, ct_ref, series_ref, masked_ref, qf_ref, kf_ref):
    regions, rows = mask_ref.shape
    padded = qf_ref.shape[2]
    lags, width = lb_ref.shape[1], ct_ref.shape[2]
    last = rows // small - 1
    spare = padded - rows
    number = lax.broadcasted_iota(jnp.int32, (HEAD_DIM, padded), 0) - 16
    place = lax.broadcasted_iota(jnp.int32, (HEAD_DIM, padded), 1)
    counted = (number >= 0) & (number <= last)
    below = lax.broadcasted_iota(jnp.int32, (LANES - lags, padded), 0)
    for r in range(regions):
        lanes = slice(r * padded, (r + 1) * padded)
        valid = jnp.concatenate([mask_ref[r : r + 1, :].astype(fp32), jnp.zeros((1, spare), fp32)], axis=1)
        turned = jnp.concatenate([ct_ref[r].T, jnp.zeros((width, spare), half)], axis=1)
        masked_ref[:, lanes] = (turned.astype(fp32) * valid).astype(half)
        values = jnp.concatenate([lb_ref[r], jnp.zeros((lags, spare), half)], axis=1)
        series_ref[:lags, lanes] = values
        series_ref[lags:, lanes] = jnp.where(below == 0, 1.0, 0.0).astype(half)
        bucket = bucket_ref[r]
        window = jnp.floor((place.astype(fp32) + 0.5) / bucket.astype(fp32)).astype(jnp.int32)
        window = jnp.minimum(window, last)
        qf_ref[r] = (
            jnp.where(counted & (window != number), masked_score, 0.0) + jnp.where(number == last + 1, 1.0, 0.0)
        ).astype(half)
        kf_ref[r] = (
            jnp.where(counted & (window == number), 1.0, 0.0)
            + jnp.where((number >= -16) & (number < -13), 1.0, 0.0)
            + jnp.where(number == last + 1, jnp.where(valid > 0, 0.0, masked_score), 0.0)
        ).astype(half)


def prepare(bucket_size, variate_mask, lookback_t, cotangent, padded, small):
    regions, rows, width = cotangent.shape
    tokens = regions * padded
    feature = jax.ShapeDtypeStruct((regions, HEAD_DIM, padded), half)
    return pl.pallas_call(
        functools.partial(prepare_kernel, small),
        in_specs=[SMEM, VMEM, VMEM, VMEM],
        out_specs=[VMEM] * 4,
        out_shape=[
            jax.ShapeDtypeStruct((LANES, tokens), half),
            jax.ShapeDtypeStruct((width, tokens), half),
            feature,
            feature,
        ],
        compiler_params=params(),
        cost_estimate=cost(1e7, 8e6),
    )(bucket_size, variate_mask, lookback_t, cotangent)


def short_block(biases, gains, up_bias):
    width = biases.shape[1]
    up_bias = up_bias.reshape(1, -1)
    return jnp.concatenate(
        [
            jnp.concatenate([biases, jnp.zeros((7, LANES - width), biases.dtype)], axis=1),
            jnp.concatenate([gains, jnp.zeros((2, LANES - width), biases.dtype)], axis=1),
            jnp.concatenate([up_bias, jnp.zeros((1, LANES - up_bias.shape[1]), biases.dtype)], axis=1),
            jnp.zeros((6, LANES), biases.dtype),
        ],
        axis=0,
    )


def side_by_side(value):
    return [value[s : s + 16] for s in range(0, value.shape[0], 16)]


def first_piece(w_embed, short, w_qkv):
    spare = jnp.zeros((w_embed.shape[0], LANES - w_embed.shape[1]), half)
    return jnp.concatenate([*side_by_side(w_qkv), w_embed, spare, short], axis=1)


def second_piece(w_out, w_up, w_down):
    return jnp.concatenate([w_out, *side_by_side(w_up), w_down], axis=1)


def pack_kernel(embed_ref, qkv_ref, out_ref, up_ref, down_ref, up_bias_ref, bias_ref, gain_ref, first_ref, second_ref):
    width = qkv_ref.shape[1]
    for j in range(3):
        first_ref[:, j * width : (j + 1) * width] = qkv_ref[j * 16 : (j + 1) * 16, :]
    spare = jnp.zeros((16, LANES - embed_ref.shape[1]), half)
    first_ref[:, 3 * width : 3 * width + LANES] = jnp.concatenate([embed_ref[...], spare], axis=1)
    short = short_block(bias_ref[...].astype(fp32), gain_ref[...].astype(fp32), up_bias_ref[...].astype(fp32))
    first_ref[:, 3 * width + LANES :] = short.astype(half)
    second_ref[:, :width] = out_ref[...]
    for j in range(4):
        second_ref[:, (1 + j) * width : (2 + j) * width] = up_ref[j * 16 : (j + 1) * 16, :]
    second_ref[:, 5 * width :] = down_ref[...]


def pack(w_embed, w_qkv, w_out, w_up, w_down, up_bias, biases, gains):
    width, units = w_out.shape[1], w_down.shape[1]
    return pl.pallas_call(
        pack_kernel,
        in_specs=[VMEM] * 8,
        out_specs=[VMEM] * 2,
        out_shape=[
            jax.ShapeDtypeStruct((16, 3 * width + 2 * LANES), half),
            jax.ShapeDtypeStruct((16, 5 * width + units), half),
        ],
    )(w_embed, w_qkv, w_out, w_up, w_down, up_bias.reshape(1, -1), biases, gains)


def unpack_first_kernel(*refs):
    parts, (qkv_ref, embed_ref, up_ref, bias_ref, gain_ref) = refs[:4], refs[4:]
    total = sum(ref[...].astype(fp32) for ref in parts)
    width = qkv_ref.shape[1]
    for j in range(3):
        qkv_ref[j * 16 : (j + 1) * 16, :] = total[:, j * width : (j + 1) * width]
    rest = total[:, 3 * width :]
    embed_ref[...] = rest[:, : embed_ref.shape[1]]
    turned = rest.T
    bias_ref[...] = turned[BIAS_AT:GAIN_AT, :]
    gain_ref[...] = turned[GAIN_AT:UP_AT, :]
    up_ref[...] = jnp.concatenate([turned[UP_AT + c : UP_AT + c + 1, :] for c in range(UP_COLUMNS)], axis=1)


def unpack_first(parts, width, lags):
    qkv, embed, up, bias, gain = pl.pallas_call(
        unpack_first_kernel,
        in_specs=[VMEM] * 4,
        out_specs=[VMEM] * 5,
        out_shape=[
            jax.ShapeDtypeStruct((48, width), fp32),
            jax.ShapeDtypeStruct((16, lags), fp32),
            jax.ShapeDtypeStruct((1, 16 * UP_COLUMNS), fp32),
            jax.ShapeDtypeStruct((7, 16), fp32),
            jax.ShapeDtypeStruct((2, 16), fp32),
        ],
    )(*parts)
    return qkv, embed, up.reshape(-1), bias, gain


def unpack_second_kernel(*refs):
    parts, (out_ref, up_ref, down_ref) = refs[:4], refs[4:]
    width = out_ref.shape[1]

    def total(columns):
        return sum(ref[:, columns].astype(fp32) for ref in parts)

    out_ref[...] = total(slice(0, width))
    for j in range(4):
        up_ref[j * 16 : (j + 1) * 16, :] = total(slice((1 + j) * width, (2 + j) * width))
    down_ref[...] = total(slice(5 * width, None))


def unpack_second(parts, width, units):
    return pl.pallas_call(
        unpack_second_kernel,
        in_specs=[VMEM] * 4,
        out_specs=[VMEM] * 3,
        out_shape=[
            jax.ShapeDtypeStruct((16, width), fp32),
            jax.ShapeDtypeStruct((64, width), fp32),
            jax.ShapeDtypeStruct((16, units), fp32),
        ],
    )(*parts)


def build_first(raw, w1):
    turned = raw[:, LANES:].astype(fp32).T
    for owner in range(PIECES):
        at = slice(owner * 16, owner * 16 + 16)
        short = turned[:16, at]
        w1[at, :] = jnp.concatenate(
            [raw[at, :BIAS_AT].astype(fp32), short[:, :9], jnp.zeros((16, LANES - BIAS_AT - 9), fp32)], axis=1
        ).astype(half)
    return turned


def scores_of(query, keys, query_f, key_f, rows):
    padded = query_f.shape[1]
    keys_t = jnp.concatenate([keys, key_f], axis=0).T[:rows]
    query_a = jnp.concatenate([query, query_f], axis=0)
    return [dot(keys_t, query_a[:, s : min(s + TILE, padded)]) for s in range(0, padded, TILE)]


def mix(scores, values, rows, store):
    values_a = jnp.concatenate([values[:, :rows], jnp.ones((16, rows), half)], axis=0)
    for i, score in enumerate(scores):
        top = jnp.max(score, axis=0, keepdims=True)
        expo = jnp.exp(score - top).astype(half)
        mixed = dot(values_a, expo)
        total = mixed[HEAD_DIM : HEAD_DIM + 1]
        lanes = slice(i * TILE, i * TILE + score.shape[1])
        store(lanes, (mixed[:HEAD_DIM] * (1.0 / total)).astype(half), top + jnp.log(total))


def heads_forward(count, read, query_f, key_f, rows, store):
    ahead = scores_of(read(0, 0), read(0, 1), query_f, key_f, rows)
    for i in range(count):
        scores = ahead
        if i + 1 < count:
            ahead = scores_of(read(i + 1, 0), read(i + 1, 1), query_f, key_f, rows)
        mix(scores, read(i, 2), rows, functools.partial(store, i))


def project_kernel(n_a, per_step, rows, regions, me_ref, *refs):
    a_refs, refs = refs[:n_a], refs[n_a:]
    series_ref, qf_ref, kf_ref, qkv_ref, emb_ref, attn_ref, log_ref, w1, turned_ref, wqkv_t, *refs = refs
    raw, wqkv, qkv_s, emb_s, sem, sem_out = refs
    step, steps = pl.program_id(0), pl.num_programs(0)
    padded = qf_ref.shape[2]
    width = emb_s.shape[0]
    outs = [
        pltpu.make_async_copy(qkv_s, qkv_ref, sem_out.at[0]),
        pltpu.make_async_copy(emb_s, emb_ref, sem_out.at[1]),
    ]

    @pl.when(step == 0)
    def _():
        def place(piece, owner):
            return [
                (piece.at[:, pl.ds(j * width, width)], wqkv.at[pl.ds(pl.multiple_of(owner * 48 + j * 16, 16), 16)])
                for j in range(3)
            ] + [(piece.at[:, pl.ds(3 * width, 2 * LANES)], raw.at[rows_of(owner, 16)])]

        copies = piece_copies(me_ref[0], a_refs, sem, place)
        for copy in copies:
            copy.start()
        for copy in copies:
            copy.wait()
        turned_ref[...] = build_first(raw, w1)
        bias_q = across(w1[:, BIAS_AT + 1 : BIAS_AT + 2], padded)
        bias_v = across(w1[:, BIAS_AT + 2 : BIAS_AT + 3], padded)
        for r in range(regions):
            lanes = slice(r * padded, (r + 1) * padded)
            low = dot(w1[...], series_ref[:, lanes]).astype(half)
            emb_s[:, lanes] = low
            for part in range(3):
                value = dot(wqkv[part * width : (part + 1) * width], low)
                if part == 0:
                    value = (value + bias_q) * HEAD_DIM**-0.5
                elif part == 2:
                    value = value + bias_v
                qkv_s[part * width : (part + 1) * width, lanes] = value.astype(half)
        for copy in outs:
            copy.start()
        wqkv_t[...] = wqkv[...].T

    region = step // (HEADS // per_step)
    first = lax.rem(step, HEADS // per_step) * per_step
    lanes = pl.ds(pl.multiple_of(region * padded, LANES), padded)

    def read(i, part):
        at = pl.multiple_of((first + i) * HEAD_DIM, HEAD_DIM)
        return qkv_s[pl.ds(part * width + at, HEAD_DIM), lanes]

    def store(i, lanes, mixed, log):
        attn_ref[i * HEAD_DIM : (i + 1) * HEAD_DIM, lanes] = mixed
        log_ref[0, i : i + 1, lanes] = log

    heads_forward(per_step, read, qf_ref[0], kf_ref[0], rows, store)

    @pl.when(step == steps - 1)
    def _():
        for copy in outs:
            copy.wait()


def head_blocks(padded, per_step, first=0):
    groups = HEADS // per_step

    def heads(part=0):
        return pl.BlockSpec(
            (per_step * HEAD_DIM, padded), lambda t: (part * groups + (t + first) % groups, (t + first) // groups)
        )

    feature = pl.BlockSpec((1, HEAD_DIM, padded), lambda t: ((t + first) // groups, 0, 0))
    log = pl.BlockSpec((1, per_step, padded), lambda t: (t + first, 0, 0))
    return heads, feature, log


def project(me, a_bufs, series, query_f, key_f, rows, width, per_step, steps):
    regions, _, padded = query_f.shape
    tokens = regions * padded
    heads, feature, log = head_blocks(padded, per_step)
    total_steps = regions * HEADS // per_step
    return pl.pallas_call(
        functools.partial(project_kernel, len(a_bufs), per_step, rows, regions),
        grid=(steps,),
        in_specs=[SMEM] + [ANY] * len(a_bufs) + [VMEM, feature, feature],
        out_specs=[ANY, ANY, heads(), log, VMEM, VMEM, VMEM],
        out_shape=[
            jax.ShapeDtypeStruct((3 * width, tokens), half),
            jax.ShapeDtypeStruct((width, tokens), half),
            jax.ShapeDtypeStruct((width, tokens), half),
            jax.ShapeDtypeStruct((total_steps, per_step, padded), fp32),
            jax.ShapeDtypeStruct((width, LANES), half),
            jax.ShapeDtypeStruct((LANES, width), fp32),
            jax.ShapeDtypeStruct((width, 3 * width), half),
        ],
        scratch_shapes=[
            pltpu.VMEM((width, 2 * LANES), half),
            pltpu.VMEM((3 * width, width), half),
            pltpu.VMEM((3 * width, tokens), half),
            pltpu.VMEM((width, tokens), half),
            pltpu.SemaphoreType.DMA,
            pltpu.SemaphoreType.DMA((2,)),
        ],
        compiler_params=params(),
        cost_estimate=cost(2e10, 1.5e7),
    )(me, *a_bufs, series, query_f, key_f)


def attend_kernel(per_step, rows, q_ref, k_ref, v_ref, qf_ref, kf_ref, *refs):
    attn_ref, log_ref = refs[-2:]

    def read(i, part):
        return (q_ref, k_ref, v_ref)[part][i * HEAD_DIM : (i + 1) * HEAD_DIM, :]

    def store(i, lanes, mixed, log):
        attn_ref[i * HEAD_DIM : (i + 1) * HEAD_DIM, lanes] = mixed
        log_ref[0, i : i + 1, lanes] = log

    heads_forward(per_step, read, qf_ref[0], kf_ref[0], rows, store)


def attend(qkv, attn, logs, query_f, key_f, rows, per_step, first):
    padded = query_f.shape[2]
    heads, feature, log = head_blocks(padded, per_step, first)
    return pl.pallas_call(
        functools.partial(attend_kernel, per_step, rows),
        grid=(logs.shape[0] - first,),
        in_specs=[heads(0), heads(1), heads(2), feature, feature, ANY, ANY],
        out_specs=[heads(), log],
        out_shape=[jax.ShapeDtypeStruct(attn.shape, half), jax.ShapeDtypeStruct(logs.shape, fp32)],
        input_output_aliases={5: 0, 6: 1},
        compiler_params=params(),
        cost_estimate=cost(1e10, 1e7),
    )(qkv, qkv, qkv, query_f, key_f, attn, logs)


NAMES = ("b3", "g0", "b4", "b5", "g1", "b6")
COLUMNS = {"b3": 99, "g0": 103, "b4": 100, "b5": 101, "g1": 104, "b6": 102}


def fold(value):
    total = value[:, :LANES]
    for s in range(LANES, value.shape[1], LANES):
        total = total + value[:, s : s + LANES]
    return total


def mean(value):
    return jnp.mean(value, axis=0, keepdims=True)


def feed_kernel(n_b, rows, regions, parts, me_ref, *refs):
    b_refs, refs = refs[:n_b], refs[n_b:]
    w1_ref, turned_ref, series_ref, attn_ref, ct_ref, out_ref, gattn_ref, gres_ref, keep_ref, send_ref, small_ref, *refs = refs
    w_out, w_out_t, w_up, w_up_t, w_down, w_down_t, up_b, col, attn_s, ct_s, *refs = refs
    act_s, slope_s, gdown_s, hid_s, gproj_s, gattn_s, flow, norm_s, lo_s, acc, acc_up, sem_in, sem_w, sem_out, sem_g = refs
    width, units = w_up_t.shape
    chunks = units // CHUNK
    padded = attn_s.shape[1] // regions
    count = len(parts)
    me = me_ref[0]
    lanes = [slice(s, s + n) for s, n in parts]

    loads = [
        (
            pltpu.make_async_copy(attn_ref.at[:, pl.ds(s, n)], attn_s.at[:, pl.ds(s, n)], sem_in.at[2 * i]),
            pltpu.make_async_copy(ct_ref.at[:, pl.ds(s, n)], ct_s.at[:, pl.ds(s, n)], sem_in.at[2 * i + 1]),
        )
        for i, (s, n) in enumerate(parts)
    ]
    loads[0][0].start()
    groups = ([], [], [])
    at = 0
    owner_of = owners(me)
    for ref in b_refs:
        for i in range(ref.shape[0]):
            owner, piece = owner_of[at], ref.at[i]
            groups[0].append(pltpu.make_async_copy(piece.at[:, pl.ds(0, width)], w_out.at[rows_of(owner, 16)], sem_w.at[0]))
            for j in range(4):
                groups[1].append(
                    pltpu.make_async_copy(
                        piece.at[:, pl.ds((1 + j) * width, width)],
                        w_up.at[pl.ds(pl.multiple_of(owner * 64 + j * 16, 16), 16)],
                        sem_w.at[1],
                    )
                )
            groups[2].append(pltpu.make_async_copy(piece.at[:, pl.ds(5 * width, units)], w_down.at[rows_of(owner, 16)], sem_w.at[2]))
            at += 1
    for group in groups:
        for copy in group:
            copy.start()
    for first, second in loads:
        if first is not loads[0][0]:
            first.start()
        second.start()

    for i, name in enumerate(NAMES):
        col[i] = across(w1_ref[:, COLUMNS[name] : COLUMNS[name] + 1])
    for owner in range(PIECES):
        up_b[owner * 64 : owner * 64 + 64, :] = jnp.broadcast_to(
            turned_ref[:64, owner * 16 + 9 : owner * 16 + 10], (64, LANES)
        )

    def wide(value, size):
        return jnp.concatenate([value] * (size // LANES), axis=1)

    def column(r, name):
        return wide(col[NAMES.index(name)], parts[r][1])

    def add_to(r, name, value):
        i = NAMES.index(name)
        acc[i] = fold(value) if r == 0 else acc[i] + fold(value)

    rates = [None] * count
    outs = []

    def leave(source, target):
        copy = pltpu.make_async_copy(source, target, sem_out.at[len(outs)])
        copy.start()
        outs.append(copy)

    def enter(r):
        loads[r][0].wait()
        embed = dot(w1_ref[...], series_ref[:, lanes[r]])
        resid = embed + (dot(w_out[...], attn_s[:, lanes[r]]) + column(r, "b3"))
        center = resid - mean(resid)
        rates[r] = lax.rsqrt(mean(center * center) + norm_eps)
        norm = center * rates[r]
        norm_s[:, lanes[r]] = norm
        hidden = norm * column(r, "g0") + column(r, "b4")
        flow[:, lanes[r]] = hidden
        hid_s[:, lanes[r]] = hidden.astype(half)

    def up(r, c):
        part = slice(c * CHUNK, (c + 1) * CHUNK)
        upper = dot(w_up[part, :], hid_s[:, lanes[r]]) + wide(up_b[part, :], parts[r][1])
        square = upper * upper
        turned = 0.5 + 0.5 * jnp.tanh(upper * (gelu_coef + (gelu_coef * 0.044715) * square))
        act = upper * turned
        slope = turned + act * (1.0 - turned) * (2.0 * gelu_coef + (6.0 * gelu_coef * 0.044715) * square)
        slope_s[part, lanes[r]] = slope.astype(half)
        act_s[part, lanes[r]] = act.astype(half)

    def down(r):
        flow[:, lanes[r]] = flow[:, lanes[r]] + (dot(w_down[...], act_s[:, lanes[r]]) + column(r, "b5"))

    def turn(r):
        resid = flow[:, lanes[r]]
        center = resid - mean(resid)
        rate = lax.rsqrt(mean(center * center) + norm_eps)
        norm = center * rate
        lo_s[lanes[r], :] = (norm * column(r, "g1") + column(r, "b6")).astype(half).T
        loads[r][1].wait()
        grad = ct_s[:, lanes[r]].astype(fp32)
        add_to(r, "b6", grad)
        add_to(r, "g1", grad * norm)
        grad = grad * column(r, "g1")
        grad = rate * (grad - mean(grad) - norm * mean(grad * norm))
        add_to(r, "b5", grad)
        flow[:, lanes[r]] = grad
        gdown_s[:, lanes[r]] = grad.astype(half)

    def up_back(r, c):
        part = slice(c * CHUNK, (c + 1) * CHUNK)
        grad = slope_s[part, lanes[r]].astype(fp32) * dot(w_down_t[part, :], gdown_s[:, lanes[r]])
        acc_up[part, :] = fold(grad) if r == 0 else acc_up[part, :] + fold(grad)
        slope_s[part, lanes[r]] = grad.astype(half)

    def back(r):
        flow[:, lanes[r]] = flow[:, lanes[r]] + dot(w_up_t[...], slope_s[:, lanes[r]])

    def leave_norm(r):
        grad = flow[:, lanes[r]]
        norm = norm_s[:, lanes[r]]
        add_to(r, "b4", grad)
        add_to(r, "g0", grad * norm)
        grad = grad * column(r, "g0")
        grad = rates[r] * (grad - mean(grad) - norm * mean(grad * norm))
        add_to(r, "b3", grad)
        flow[:, lanes[r]] = grad
        low = grad.astype(half)
        gproj_s[:, lanes[r]] = low
        gattn_s[:, lanes[r]] = dot(w_out_t[...], low).astype(half)
        at = pl.ds(*parts[r])
        leave(flow.at[:, at], gres_ref.at[:, at])
        leave(gattn_s.at[:, at], gattn_ref.at[:, at])

    for copy in groups[0]:
        copy.wait()
    enter(0)
    for copy in groups[1]:
        copy.wait()
    for r in range(count):
        up(r, 0)
        if r == 0:
            for copy in groups[2]:
                copy.wait()
            w_out_t[...] = w_out[...].T
            w_down_t[...] = w_down[...].T
            w_up_t[...] = w_up[...].T
        up(r, 1)
        if r + 1 < count:
            enter(r + 1)
        if r > 0:
            turn(r - 1)
        for c in range(2, chunks):
            up(r, c)
        down(r)
    for r in range(count):
        up_back(r, 0)
        up_back(r, 1)
        if r == 0:
            turn(count - 1)
            for region in range(regions):
                leave(lo_s.at[pl.ds(region * padded, rows)], out_ref.at[region])
        else:
            leave_norm(r - 1)
        for c in range(2, chunks):
            up_back(r, c)
        back(r)
    leave_norm(count - 1)
    targets = [(keep_ref if r < PIECES // 2 else send_ref).at[r % (PIECES // 2)] for r in range(PIECES)]
    copies = []

    def give(source, column, size):
        copies.append(pltpu.make_async_copy(source, target.at[:, pl.ds(column, size)], sem_g))
        copies[-1].start()

    w_up[...] = dot(slope_s[...], hid_s[...], 1, 1).astype(half)
    for owner, target in zip(owner_of, targets):
        for j in range(4):
            give(w_up.at[pl.ds(pl.multiple_of(owner * 64 + j * 16, 16), 16)], (1 + j) * width, width)
    w_out[...] = dot(gproj_s[...], attn_s[...], 1, 1).astype(half)
    w_down[...] = dot(gdown_s[...], act_s[...], 1, 1).astype(half)
    for owner, target in zip(owner_of, targets):
        give(w_out.at[rows_of(owner, 16)], 0, width)
        give(w_down.at[rows_of(owner, 16)], 5 * width, units)
    total = jnp.zeros((width, LANES), fp32)
    lane = lax.broadcasted_iota(jnp.int32, (width, LANES), 1)
    for i, name in enumerate(NAMES):
        total = total + jnp.where(lane == COLUMNS[name], jnp.sum(acc[i], axis=1, keepdims=True), 0.0)
    up_sum = jnp.sum(acc_up[...], axis=1, keepdims=True).reshape(PIECES, UP_COLUMNS, 16, 1)
    for c in range(UP_COLUMNS):
        total = total + jnp.where(lane == UP_AT + c, up_sum[:, c].reshape(width, 1), 0.0)
    small_ref[...] = total
    for copy in copies:
        copy.wait()
    for copy in outs:
        copy.wait()


def feed(me, b_bufs, w1, turned, series, attn, cotangent, regions, rows, units):
    width, tokens = attn.shape
    half_set = jax.ShapeDtypeStruct((PIECES // 2, 16, 5 * width + units), half)
    low_all = pltpu.VMEM((width, tokens), half)
    parts = ((0, tokens // 2 // TILE * TILE), (tokens // 2 // TILE * TILE, tokens - tokens // 2 // TILE * TILE))
    return pl.pallas_call(
        functools.partial(feed_kernel, len(b_bufs), rows, regions, parts),
        in_specs=[SMEM] + [ANY] * len(b_bufs) + [VMEM, VMEM, VMEM, ANY, ANY],
        out_specs=[ANY] * 5 + [VMEM],
        out_shape=[
            jax.ShapeDtypeStruct((regions, rows, width), half),
            jax.ShapeDtypeStruct((width, tokens), half),
            jax.ShapeDtypeStruct((width, tokens), fp32),
            half_set,
            half_set,
            jax.ShapeDtypeStruct((width, LANES), fp32),
        ],
        scratch_shapes=[
            pltpu.VMEM((width, width), half),
            pltpu.VMEM((width, width), half),
            pltpu.VMEM((units, width), half),
            pltpu.VMEM((width, units), half),
            pltpu.VMEM((width, units), half),
            pltpu.VMEM((units, width), half),
            pltpu.VMEM((units, LANES), fp32),
            pltpu.VMEM((len(NAMES), width, LANES), fp32),
            low_all,
            low_all,
            pltpu.VMEM((units, tokens), half),
            pltpu.VMEM((units, tokens), half),
            low_all,
            low_all,
            low_all,
            low_all,
            pltpu.VMEM((width, tokens), fp32),
            pltpu.VMEM((width, tokens), fp32),
            pltpu.VMEM((tokens, width), half),
            pltpu.VMEM((len(NAMES), width, LANES), fp32),
            pltpu.VMEM((units, LANES), fp32),
            pltpu.SemaphoreType.DMA((2 * len(parts),)),
            pltpu.SemaphoreType.DMA((3,)),
            pltpu.SemaphoreType.DMA((regions + 2 * len(parts),)),
            pltpu.SemaphoreType.DMA,
        ],
        compiler_params=params(),
        cost_estimate=cost(4e10, 2e7),
    )(me, *b_bufs, w1, turned, series, attn, cotangent)


def heads_back(per_step, rows, refs, store, beside=None):
    q_ref, k_ref, v_ref, attn_ref, gattn_ref, log_ref, qf_ref, kf_ref = refs
    padded = qf_ref.shape[2]
    query_f, key_f = qf_ref[0], kf_ref[0]
    blocks = [(s, min(TILE, rows - s)) for s in range(0, rows, TILE)]
    filler = jnp.zeros((13, padded), fp32)

    def in_three(row):
        first = row.astype(half).astype(fp32)
        left = row - first
        second = left.astype(half).astype(fp32)
        return jnp.concatenate([first, second, left - second, filler], axis=0).astype(half)

    for i in range(per_step):
        head = slice(i * HEAD_DIM, (i + 1) * HEAD_DIM)
        query, keys, values, grad = q_ref[head, :], k_ref[head, :], v_ref[head, :], gattn_ref[head, :]
        inner = jnp.sum(grad.astype(fp32) * attn_ref[head, :].astype(fp32), axis=0, keepdims=True)
        query_a = jnp.concatenate([query, in_three(-log_ref[0, i : i + 1, :]), query_f[16:]], axis=0).T
        grad_a = jnp.concatenate([grad, in_three(-inner), jnp.zeros((48, padded), half)], axis=0).T
        keys_a = jnp.concatenate([keys, key_f], axis=0)
        values_a = jnp.concatenate([values, key_f], axis=0)
        grad_keys = grad_values = None
        grad_query = []
        for s, n in blocks:
            probs = jnp.exp(dot(query_a[s : s + n], keys_a))
            raw = (probs * dot(grad_a[s : s + n], values_a)).astype(half)
            more_v = dot(grad[:, s : s + n], probs.astype(half))
            more_k = dot(query[:, s : s + n], raw)
            grad_values = more_v if grad_values is None else grad_values + more_v
            grad_keys = more_k if grad_keys is None else grad_keys + more_k
            grad_query.append((dot(keys, raw, 1, 1) * HEAD_DIM**-0.5).astype(half))
        grad_query.append(jnp.zeros((HEAD_DIM, padded - rows), half))
        store(i, (jnp.concatenate(grad_query, axis=1), grad_keys.astype(half), grad_values.astype(half)))
        if beside is not None:
            beside(i)


def attend_back_kernel(per_step, rows, *refs):
    grad_ref = refs[8]

    def store(i, three):
        for part, value in enumerate(three):
            grad_ref[0, part, i * HEAD_DIM : (i + 1) * HEAD_DIM, :] = value

    heads_back(per_step, rows, refs[:8], store)


def attend_back_add_kernel(per_step, rows, *refs):
    ins, (keep_ref, got_ref, grad_ref), quarter_refs = refs[:8], refs[8:11], refs[11:15]
    keep_s, got_s, low_s, sem_in, sem_out = refs[15:]
    loads = [
        [
            pltpu.make_async_copy(source.at[pl.ds(4 * i, 4)], target.at[pl.ds(4 * i, 4)], sem_in.at[i, j])
            for j, (source, target) in enumerate(((keep_ref, keep_s), (got_ref, got_s)))
        ]
        for i in range(4)
    ]
    outs = [
        pltpu.make_async_copy(low_s.at[pl.ds(4 * i, 4)], quarter_refs[i], sem_out.at[i]) for i in range(4)
    ]
    for pair in loads:
        for copy in pair:
            copy.start()

    def store(i, three):
        for part, value in enumerate(three):
            grad_ref[0, part, i * HEAD_DIM : (i + 1) * HEAD_DIM, :] = value

    def beside(i):
        for copy in loads[i]:
            copy.wait()
        at = slice(4 * i, 4 * i + 4)
        low_s[at] = (keep_s[at].astype(fp32) + got_s[at].astype(fp32)).astype(half)
        outs[i].start()

    heads_back(per_step, rows, ins, store, beside)
    for copy in outs:
        copy.wait()


def finish_kernel(per_step, rows, counts, me_ref, *refs):
    ins, done_refs, refs = refs[:8], refs[8 : 8 + len(counts)], refs[8 + len(counts) :]
    first = sum(counts)
    emb_ref, gres_ref, series_ref, wqkv_t_ref, w1_ref, small_ref, keep_ref, send_ref, lbg_ref, *refs = refs
    grad_s, emb_s, gres_s, wqkv_t, g_qkv, g_one, sem, sem_out = refs
    step, steps = pl.program_id(0), pl.num_programs(0)
    width, tokens = emb_s.shape
    regions, lags, _ = lbg_ref.shape
    padded = tokens // regions
    groups = HEADS // per_step
    height = per_step * HEAD_DIM
    brought = [
        pltpu.make_async_copy(emb_ref, emb_s, sem),
        pltpu.make_async_copy(gres_ref, gres_s, sem),
        pltpu.make_async_copy(wqkv_t_ref, wqkv_t, sem),
    ]
    done = [ref.at[t] for ref in done_refs for t in range(ref.shape[0])]
    for t in range(first):
        for part in range(3):
            brought.append(
                pltpu.make_async_copy(
                    done[t].at[part],
                    grad_s.at[
                        pl.ds(part * width + (t % groups) * height, height), pl.ds(t // groups * padded, padded)
                    ],
                    sem,
                )
            )

    @pl.when(step == 0)
    def _():
        for copy in brought:
            copy.start()

    now = step + first
    lanes = pl.ds(pl.multiple_of(now // groups * padded, LANES), padded)
    rows_at = lax.rem(now, groups) * height

    def store(i, three):
        for part, value in enumerate(three):
            at = pl.multiple_of(part * width + rows_at + i * HEAD_DIM, HEAD_DIM)
            grad_s[pl.ds(at, HEAD_DIM), lanes] = value

    heads_back(per_step, rows, ins, store)

    @pl.when(step == steps - 1)
    def _():
        for copy in brought:
            copy.wait()
        owner_of = owners(me_ref[0])
        for part in range(3):
            at = slice(part * width, (part + 1) * width)
            g_qkv[at, :] = dot(grad_s[at, :], emb_s[...], 1, 1).astype(half)
        copies = []
        for r, owner in enumerate(owner_of):
            target = (keep_ref if r < PIECES // 2 else send_ref).at[r % (PIECES // 2)]
            for j in range(3):
                copies.append(
                    pltpu.make_async_copy(
                        g_qkv.at[pl.ds(pl.multiple_of(owner * 48 + j * 16, 16), 16)],
                        target.at[:, pl.ds(j * width, width)],
                        sem_out.at[0],
                    )
                )
        for copy in copies:
            copy.start()
        total = small_ref[...]
        lane = lax.broadcasted_iota(jnp.int32, total.shape, 1)
        for i, part in enumerate((0, 2)):
            bias = fold(grad_s[part * width : (part + 1) * width, :].astype(fp32))
            total = total + jnp.where(lane == BIAS_AT + 1 + i, jnp.sum(bias, axis=1, keepdims=True), 0.0)
        low = (gres_s[...] + dot(wqkv_t[...], grad_s[...])).astype(half)
        total = total + dot(low, series_ref[...], 1, 1)
        for r in range(regions):
            lbg_ref[r] = dot(w1_ref[...], low[:, r * padded : (r + 1) * padded], 0, 0)[:lags, :rows]
        g_one[...] = total.astype(half)
        more = []
        for r, owner in enumerate(owner_of):
            target = (keep_ref if r < PIECES // 2 else send_ref).at[r % (PIECES // 2)]
            more.append(
                pltpu.make_async_copy(
                    g_one.at[rows_of(owner, 16)], target.at[:, pl.ds(3 * width, LANES)], sem_out.at[1]
                )
            )
        for copy in more:
            copy.start()
        for copy in copies:
            copy.wait()
        for copy in more:
            copy.wait()


def back_operands(qkv, attn, grad_attn, logs, query_f, key_f, per_step, first):
    heads, feature, log = head_blocks(query_f.shape[2], per_step, first)
    specs = [heads(0), heads(1), heads(2), heads(), heads(), log, feature, feature]
    return specs, (qkv, qkv, qkv, attn, grad_attn, logs, query_f, key_f)


def attend_back(qkv, attn, grad_attn, logs, query_f, key_f, rows, per_step, first, steps, pair=None):
    padded = query_f.shape[2]
    specs, operands = back_operands(qkv, attn, grad_attn, logs, query_f, key_f, per_step, first)
    shape = (3, per_step * HEAD_DIM, padded)
    grad_spec = pl.BlockSpec((1, *shape), lambda t: (t, 0, 0, 0))
    grad_shape = jax.ShapeDtypeStruct((steps, *shape), half)
    if pair is None:
        return pl.pallas_call(
            functools.partial(attend_back_kernel, per_step, rows),
            grid=(steps,),
            in_specs=specs,
            out_specs=grad_spec,
            out_shape=grad_shape,
            compiler_params=params(),
            cost_estimate=cost(2e10, 1e7),
        )(*operands)
    whole = pair[0].shape
    quarter = jax.ShapeDtypeStruct((4, *whole[1:]), half)
    grad, *quarters = pl.pallas_call(
        functools.partial(attend_back_add_kernel, per_step, rows),
        grid=(1,),
        in_specs=specs + [ANY, ANY],
        out_specs=[grad_spec] + [ANY] * 4,
        out_shape=[grad_shape] + [quarter] * 4,
        scratch_shapes=[pltpu.VMEM(whole, half)] * 3
        + [pltpu.SemaphoreType.DMA((4, 2)), pltpu.SemaphoreType.DMA((4,))],
        compiler_params=params(),
        cost_estimate=cost(2e10, 1e7),
    )(*operands, *pair)
    return grad, quarters


def finish(me, qkv, attn, grad_attn, logs, query_f, key_f, done, embed_low, grad_resid, series, wqkv_t, w1, small, rows, lags, per_step):
    regions, _, padded = query_f.shape
    width, tokens = attn.shape
    counts = tuple(value.shape[0] for value in done)
    first = sum(counts)
    specs, operands = back_operands(qkv, attn, grad_attn, logs, query_f, key_f, per_step, first)
    half_set = jax.ShapeDtypeStruct((PIECES // 2, 16, 3 * width + LANES), half)
    return pl.pallas_call(
        functools.partial(finish_kernel, per_step, rows, counts),
        grid=(logs.shape[0] - first,),
        in_specs=[SMEM] + specs + [ANY] * len(done) + [ANY, ANY, VMEM, ANY, VMEM, VMEM],
        out_specs=[ANY, ANY, VMEM],
        out_shape=[half_set, half_set, jax.ShapeDtypeStruct((regions, lags, rows), fp32)],
        scratch_shapes=[
            pltpu.VMEM((3 * width, tokens), half),
            pltpu.VMEM((width, tokens), half),
            pltpu.VMEM((width, tokens), fp32),
            pltpu.VMEM((width, 3 * width), half),
            pltpu.VMEM((3 * width, width), half),
            pltpu.VMEM((width, LANES), half),
            pltpu.SemaphoreType.DMA,
            pltpu.SemaphoreType.DMA((2,)),
        ],
        compiler_params=params(),
        cost_estimate=cost(4e10, 2e7),
    )(me, *operands, *done, embed_low, grad_resid, series, wqkv_t, w1, small)


def send(value, offset):
    return lax.ppermute(value, AXES, [(i, i ^ offset) for i in range(PIECES)])


def after(value, *others):
    return lax.optimization_barrier((value, *others))[0]


def along_z(piece):
    return jnp.stack([piece] + [send(piece, 2 * s) for s in range(1, 4)])


def along_plane(value):
    return [value] + [send(value, offset) for offset in (1, 16, 17)]


def along_core(plane):
    return plane + [send(part, 8) for part in plane]


def add(*terms):
    return sum(term.astype(fp32) for term in terms)


def quarters(low):
    return [low[4 * i : 4 * i + 4] for i in range(4)]


def add_core(keep, got):
    return [add(*pair).astype(half) for pair in zip(quarters(keep), quarters(got))]


def sum_plane(lows):
    return [lows[0]] + [send(low, offset) for low, offset in zip(lows[1:], (1, 16, 17))]


def add_plane(parts):
    return [add(*[part[s] for part in parts]).astype(half) for s in range(4)]


def sum_z(lows):
    return [lows[0]] + [send(lows[s], 2 * s) for s in range(1, 4)]


def stacked(value, width):
    return jnp.concatenate([value[:, s : s + width] for s in range(0, value.shape[1], width)], axis=0)


def unpack_one(packed, lags):
    up = packed[:, UP_AT : UP_AT + UP_COLUMNS].reshape(-1, 16, UP_COLUMNS).transpose(0, 2, 1).reshape(-1)
    return packed[:, :lags], packed[:, BIAS_AT:GAIN_AT].T, packed[:, GAIN_AT:UP_AT].T, up


def body(
    ours,
    lookback,
    bucket_size,
    variate_mask,
    w_embed,
    w_qkv,
    w_out,
    w_up,
    w_down,
    up_bias,
    biases,
    gains,
    cotangent,
):
    regions, rows, lags = lookback.shape
    width = w_qkv.shape[1]
    units = w_down.shape[1]
    padded = -(-rows // LANES) * LANES
    per_step = 4
    steps = regions * HEADS // per_step
    lookback_t = lookback.transpose(0, 2, 1)
    series, masked, query_f, key_f = prepare(bucket_size, variate_mask, lookback_t, cotangent, padded, 32)

    if ours:
        index = lax.axis_index(AXES).astype(jnp.int32)
        piece_a, piece_b = pack(w_embed, w_qkv, w_out, w_up, w_down, up_bias, biases, gains)
        z_a = after(along_z(piece_a), series)
        z_b = along_z(piece_b)
        plane_a = along_plane(z_a)
        plane_b = along_plane(after(z_b, z_a))
        a_bufs = along_core(plane_a)
    else:
        index = jnp.zeros((), jnp.int32)

        def whole(value, axis=0):
            return lax.all_gather(value, AXES, axis=axis, tiled=True)

        def cut(value, axis=0):
            shape = value.shape[:axis] + (PIECES, value.shape[axis] // PIECES) + value.shape[axis + 1 :]
            return jnp.moveaxis(value.reshape(shape), axis, 0)

        early = jnp.array(OFFSETS)
        short = jax.vmap(short_block)(cut(whole(biases, 1), 1), cut(whole(gains, 1), 1), cut(whole(up_bias)))
        a_bufs = [jax.vmap(first_piece)(cut(whole(w_embed)), short, cut(whole(w_qkv)))[early]]
        b_bufs = [jax.vmap(second_piece)(cut(whole(w_out)), cut(whole(w_up)), cut(whole(w_down)))[early]]
    me = index.reshape(1)

    qkv, embed_low, attn, logs, w1, turned, wqkv_t = project(
        me, a_bufs, series, query_f, key_f, rows, width, per_step, steps - 1
    )
    if ours:
        b_bufs = along_core([after(part, logs) for part in plane_b])
    attn, logs = attend(qkv, attn, logs, query_f, key_f, rows, per_step, steps - 1)
    layer_out, grad_attn, grad_resid, keep_b, send_b, sums = feed(
        me, b_bufs, w1, turned, series, attn, masked, regions, rows, units
    )
    if ours:
        core_b = send(send_b, 8)
    done = [attend_back(qkv, attn, grad_attn, logs, query_f, key_f, rows, per_step, 0, 1)]
    if ours:
        pair = (keep_b, after(core_b, *done))
        grad, lows_b = attend_back(qkv, attn, grad_attn, logs, query_f, key_f, rows, per_step, 1, 1, pair)
        done.append(grad)
        parts_b = sum_plane(lows_b)
    keep_a, send_a, lookback_grad = finish(
        me, qkv, attn, grad_attn, logs, query_f, key_f, done, embed_low, grad_resid, series, wqkv_t, w1, sums, rows, lags, per_step
    )
    lookback_grad = lookback_grad.transpose(0, 2, 1)

    def parts_of(grad_a, grad_b):
        w_qkv_part = stacked(grad_a[:, : 3 * width], width)
        return w_qkv_part, grad_a[:, 3 * width :], grad_b[:, :width], stacked(grad_b[:, width : 5 * width], width), grad_b[:, 5 * width :]

    if ours:
        core_a = send(send_a, 8)
        parts_b = sum_z(add_plane([after(part, keep_a) for part in parts_b]))
        lows_a = add_core(keep_a, after(core_a, parts_b[0]))
        lows_a = add_plane(sum_plane(lows_a))
        grad_out, grad_up, grad_down = unpack_second([after(part, *lows_a) for part in parts_b], width, units)
        parts_a = sum_z(lows_a)
        grad_qkv, grad_embed, grad_up_bias, grad_biases, grad_gains = unpack_first(parts_a, width, lags)
    else:
        def shared(value, axis=0):
            return lax.psum_scatter(value, AXES, scatter_dimension=axis, tiled=True)

        order = jnp.argsort(jnp.array(OFFSETS, jnp.int32))
        grad_a = jnp.concatenate([keep_a, send_a], axis=0).astype(fp32)[order]
        grad_b = jnp.concatenate([keep_b, send_b], axis=0).astype(fp32)[order]
        whole_parts = [value.reshape(-1, value.shape[-1]) for value in jax.vmap(parts_of)(grad_a, grad_b)]
        grad_embed, grad_biases, grad_gains, grad_up_bias = unpack_one(whole_parts[1], lags)
        grad_qkv, grad_out, grad_up, grad_down = (shared(whole_parts[i]) for i in (0, 2, 3, 4))
        grad_embed, grad_up_bias = shared(grad_embed), shared(grad_up_bias)
        grad_biases, grad_gains = shared(grad_biases, 1), shared(grad_gains, 1)
    return (
        layer_out,
        lookback_grad,
        grad_embed,
        grad_qkv,
        grad_out,
        grad_up,
        grad_down,
        grad_up_bias,
        grad_biases,
        grad_gains,
    )


def solution(mesh):
    one = P(AXES)
    rows = P(AXES, None)
    blocks = P(AXES, None, None)
    columns = P(None, AXES)
    in_specs = (blocks, one, rows, rows, rows, rows, rows, rows, one, columns, columns, blocks)
    out_specs = (blocks, blocks, rows, rows, rows, rows, rows, one, columns, columns)
    ours = tuple(mesh.shape[axis] for axis in AXES) == (4, 8)
    return jax.shard_map(
        functools.partial(body, ours), mesh=mesh, in_specs=in_specs, out_specs=out_specs, check_vma=False
    )
```

```python
import functools

import jax
import jax.numpy as jnp
from jax import lax
from jax.experimental import pallas as pl
from jax.experimental.pallas import tpu as pltpu
from jax.sharding import PartitionSpec as P

HEADS = 8
HEAD_DIM = 64
PIECES = 32
LANES = 128
TILE = 256
CHUNK = 512
SPAN = 512
AXES = ("dp", "fsdp")

norm_eps = 1e-05
masked_score = -1e30
gelu_coef = 0.7978845608028654

half = jnp.bfloat16
fp32 = jnp.float32

OFFSETS = tuple(
    core * 8 + x * 16 + y + z * 2
    for core in range(2)
    for x in range(2)
    for y in range(2)
    for z in range(4)
)

BIAS_AT = 96
GAIN_AT = 103
UP_AT = 105
UP_COLUMNS = 4


def dot(left, right, left_dim=1, right_dim=0):
    return lax.dot_general(
        left, right, (((left_dim,), (right_dim,)), ((), ())), preferred_element_type=fp32
    )


def params(mebibytes=62):
    return pltpu.CompilerParams(vmem_limit_bytes=mebibytes * 2**20)


def cost(flops, moved):
    return pl.CostEstimate(flops=int(flops), bytes_accessed=int(moved), transcendentals=0)


VMEM = pl.BlockSpec(memory_space=pltpu.VMEM)
SMEM = pl.BlockSpec(memory_space=pltpu.SMEM)
ANY = pl.BlockSpec(memory_space=pl.ANY)


def piece_copies(me, refs, sem, place):
    copies = []
    at = 0
    for ref in refs:
        for i in range(ref.shape[0]):
            owner = jnp.bitwise_xor(me, OFFSETS[at])
            for source, target in place(ref.at[i], owner):
                copies.append(pltpu.make_async_copy(source, target, sem))
            at += 1
    return copies


def rows_of(owner, count):
    return pl.ds(pl.multiple_of(owner * count, 16), count)


def owners(me):
    return [jnp.bitwise_xor(me, offset) for offset in OFFSETS]


def across(column, lanes=LANES):
    return jnp.broadcast_to(column.astype(fp32), (column.shape[0], lanes))


def prepare_kernel(small, bucket_ref, mask_ref, lb_ref, ct_ref, series_ref, masked_ref, qf_ref, kf_ref):
    regions, rows = mask_ref.shape
    padded = qf_ref.shape[2]
    lags, width = lb_ref.shape[1], ct_ref.shape[2]
    last = rows // small - 1
    spare = padded - rows
    number = lax.broadcasted_iota(jnp.int32, (HEAD_DIM, padded), 0) - 16
    place = lax.broadcasted_iota(jnp.int32, (HEAD_DIM, padded), 1)
    counted = (number >= 0) & (number <= last)
    below = lax.broadcasted_iota(jnp.int32, (LANES - lags, padded), 0)
    for r in range(regions):
        lanes = slice(r * padded, (r + 1) * padded)
        valid = jnp.concatenate([mask_ref[r : r + 1, :].astype(fp32), jnp.zeros((1, spare), fp32)], axis=1)
        turned = jnp.concatenate([ct_ref[r].T, jnp.zeros((width, spare), half)], axis=1)
        masked_ref[:, lanes] = (turned.astype(fp32) * valid).astype(half)
        values = jnp.concatenate([lb_ref[r], jnp.zeros((lags, spare), half)], axis=1)
        series_ref[:lags, lanes] = values
        series_ref[lags:, lanes] = jnp.where(below == 0, 1.0, 0.0).astype(half)
        bucket = bucket_ref[r]
        window = jnp.floor((place.astype(fp32) + 0.5) / bucket.astype(fp32)).astype(jnp.int32)
        window = jnp.minimum(window, last)
        qf_ref[r] = (
            jnp.where(counted & (window != number), masked_score, 0.0) + jnp.where(number == last + 1, 1.0, 0.0)
        ).astype(half)
        kf_ref[r] = (
            jnp.where(counted & (window == number), 1.0, 0.0)
            + jnp.where((number >= -16) & (number < -13), 1.0, 0.0)
            + jnp.where(number == last + 1, jnp.where(valid > 0, 0.0, masked_score), 0.0)
        ).astype(half)


def prepare(bucket_size, variate_mask, lookback_t, cotangent, padded, small):
    regions, rows, width = cotangent.shape
    tokens = regions * padded
    feature = jax.ShapeDtypeStruct((regions, HEAD_DIM, padded), half)
    return pl.pallas_call(
        functools.partial(prepare_kernel, small),
        in_specs=[SMEM, VMEM, VMEM, VMEM],
        out_specs=[VMEM] * 4,
        out_shape=[
            jax.ShapeDtypeStruct((LANES, tokens), half),
            jax.ShapeDtypeStruct((width, tokens), half),
            feature,
            feature,
        ],
        compiler_params=params(),
        cost_estimate=cost(1e7, 8e6),
    )(bucket_size, variate_mask, lookback_t, cotangent)


def short_block(biases, gains, up_bias):
    width = biases.shape[1]
    up_bias = up_bias.reshape(1, -1)
    return jnp.concatenate(
        [
            jnp.concatenate([biases, jnp.zeros((7, LANES - width), biases.dtype)], axis=1),
            jnp.concatenate([gains, jnp.zeros((2, LANES - width), biases.dtype)], axis=1),
            jnp.concatenate([up_bias, jnp.zeros((1, LANES - up_bias.shape[1]), biases.dtype)], axis=1),
            jnp.zeros((6, LANES), biases.dtype),
        ],
        axis=0,
    )


def side_by_side(value):
    return [value[s : s + 16] for s in range(0, value.shape[0], 16)]


def first_piece(w_embed, short, w_qkv):
    spare = jnp.zeros((w_embed.shape[0], LANES - w_embed.shape[1]), half)
    return jnp.concatenate([*side_by_side(w_qkv), w_embed, spare, short], axis=1)


def second_piece(w_out, w_up, w_down):
    return jnp.concatenate([w_out, *side_by_side(w_up), w_down], axis=1)


def pack_kernel(embed_ref, qkv_ref, out_ref, up_ref, down_ref, up_bias_ref, bias_ref, gain_ref, first_ref, second_ref):
    width = qkv_ref.shape[1]
    for j in range(3):
        first_ref[:, j * width : (j + 1) * width] = qkv_ref[j * 16 : (j + 1) * 16, :]
    spare = jnp.zeros((16, LANES - embed_ref.shape[1]), half)
    first_ref[:, 3 * width : 3 * width + LANES] = jnp.concatenate([embed_ref[...], spare], axis=1)
    short = short_block(bias_ref[...].astype(fp32), gain_ref[...].astype(fp32), up_bias_ref[...].astype(fp32))
    first_ref[:, 3 * width + LANES :] = short.astype(half)
    second_ref[:, :width] = out_ref[...]
    for j in range(4):
        second_ref[:, (1 + j) * width : (2 + j) * width] = up_ref[j * 16 : (j + 1) * 16, :]
    second_ref[:, 5 * width :] = down_ref[...]


def pack(w_embed, w_qkv, w_out, w_up, w_down, up_bias, biases, gains):
    width, units = w_out.shape[1], w_down.shape[1]
    return pl.pallas_call(
        pack_kernel,
        in_specs=[VMEM] * 8,
        out_specs=[VMEM] * 2,
        out_shape=[
            jax.ShapeDtypeStruct((16, 3 * width + 2 * LANES), half),
            jax.ShapeDtypeStruct((16, 5 * width + units), half),
        ],
    )(w_embed, w_qkv, w_out, w_up, w_down, up_bias.reshape(1, -1), biases, gains)


def brought(refs, places, sem):
    copies = [pltpu.make_async_copy(ref, place, sem.at[i]) for i, (ref, place) in enumerate(zip(refs, places))]
    for copy in copies:
        copy.start()
    for copy in copies:
        copy.wait()
    return lambda columns: sum(place[:, columns].astype(fp32) for place in places)


def unpack_first_kernel(*refs):
    parts, (qkv_ref, embed_ref, up_ref, bias_ref, gain_ref), places, sem = refs[:4], refs[4:9], refs[9:13], refs[13]
    total = brought(parts, places, sem)(slice(None))
    width = qkv_ref.shape[1]
    for j in range(3):
        qkv_ref[j * 16 : (j + 1) * 16, :] = total[:, j * width : (j + 1) * width]
    rest = total[:, 3 * width :]
    embed_ref[...] = rest[:, : embed_ref.shape[1]]
    turned = rest.T
    bias_ref[...] = turned[BIAS_AT:GAIN_AT, :]
    gain_ref[...] = turned[GAIN_AT:UP_AT, :]
    up_ref[...] = jnp.concatenate([turned[UP_AT + c : UP_AT + c + 1, :] for c in range(UP_COLUMNS)], axis=1)


def unpack_first(parts, width, lags):
    qkv, embed, up, bias, gain = pl.pallas_call(
        unpack_first_kernel,
        in_specs=[ANY] * 4,
        out_specs=[VMEM] * 5,
        out_shape=[
            jax.ShapeDtypeStruct((48, width), fp32),
            jax.ShapeDtypeStruct((16, lags), fp32),
            jax.ShapeDtypeStruct((1, 16 * UP_COLUMNS), fp32),
            jax.ShapeDtypeStruct((7, 16), fp32),
            jax.ShapeDtypeStruct((2, 16), fp32),
        ],
        scratch_shapes=[pltpu.VMEM(part.shape, half) for part in parts] + [pltpu.SemaphoreType.DMA((4,))],
    )(*parts)
    return qkv, embed, up.reshape(-1), bias, gain


def unpack_second_kernel(*refs):
    parts, (out_ref, up_ref, down_ref), places, sem = refs[:4], refs[4:7], refs[7:11], refs[11]
    width = out_ref.shape[1]
    total = brought(parts, places, sem)
    out_ref[...] = total(slice(0, width))
    for j in range(4):
        up_ref[j * 16 : (j + 1) * 16, :] = total(slice((1 + j) * width, (2 + j) * width))
    down_ref[...] = total(slice(5 * width, None))


def unpack_second(parts, width, units):
    return pl.pallas_call(
        unpack_second_kernel,
        in_specs=[ANY] * 4,
        out_specs=[VMEM] * 3,
        out_shape=[
            jax.ShapeDtypeStruct((16, width), fp32),
            jax.ShapeDtypeStruct((64, width), fp32),
            jax.ShapeDtypeStruct((16, units), fp32),
        ],
        scratch_shapes=[pltpu.VMEM(part.shape, half) for part in parts] + [pltpu.SemaphoreType.DMA((4,))],
    )(*parts)


def build_first(raw, w1):
    turned = raw[:, LANES:].astype(fp32).T
    for owner in range(PIECES):
        at = slice(owner * 16, owner * 16 + 16)
        short = turned[:16, at]
        w1[at, :] = jnp.concatenate(
            [raw[at, :BIAS_AT].astype(fp32), short[:, :9], jnp.zeros((16, LANES - BIAS_AT - 9), fp32)], axis=1
        ).astype(half)
    return turned


def scores_of(query, keys, query_f, key_f, rows):
    padded = query_f.shape[1]
    keys_t = jnp.concatenate([keys, key_f], axis=0).T[:rows]
    query_a = jnp.concatenate([query, query_f], axis=0)
    return [dot(keys_t, query_a[:, s : min(s + TILE, padded)]) for s in range(0, padded, TILE)]


def mix(scores, values, rows, store):
    values_a = jnp.concatenate([values[:, :rows], jnp.ones((16, rows), half)], axis=0)
    for i, score in enumerate(scores):
        top = jnp.max(score, axis=0, keepdims=True)
        expo = jnp.exp(score - top).astype(half)
        mixed = dot(values_a, expo)
        total = mixed[HEAD_DIM : HEAD_DIM + 1]
        lanes = slice(i * TILE, i * TILE + score.shape[1])
        store(lanes, (mixed[:HEAD_DIM] * (1.0 / total)).astype(half), top + jnp.log(total))


def heads_forward(count, read, query_f, key_f, rows, store):
    ahead = scores_of(read(0, 0), read(0, 1), query_f, key_f, rows)
    for i in range(count):
        scores = ahead
        if i + 1 < count:
            ahead = scores_of(read(i + 1, 0), read(i + 1, 1), query_f, key_f, rows)
        mix(scores, read(i, 2), rows, functools.partial(store, i))


def project_kernel(n_a, per_step, rows, regions, me_ref, *refs):
    a_refs, refs = refs[:n_a], refs[n_a:]
    series_ref, qf_ref, kf_ref, qkv_ref, emb_ref, attn_ref, log_ref, w1, turned_ref, wqkv_t, *refs = refs
    raw, wqkv, qkv_s, emb_s, sem, sem_out = refs
    step, steps = pl.program_id(0), pl.num_programs(0)
    padded = qf_ref.shape[2]
    width = emb_s.shape[0]
    outs = [
        pltpu.make_async_copy(qkv_s, qkv_ref, sem_out.at[0]),
        pltpu.make_async_copy(emb_s, emb_ref, sem_out.at[1]),
    ]

    @pl.when(step == 0)
    def _():
        def place(piece, owner):
            return [
                (piece.at[:, pl.ds(j * width, width)], wqkv.at[pl.ds(pl.multiple_of(owner * 48 + j * 16, 16), 16)])
                for j in range(3)
            ] + [(piece.at[:, pl.ds(3 * width, 2 * LANES)], raw.at[rows_of(owner, 16)])]

        copies = piece_copies(me_ref[0], a_refs, sem, place)
        for copy in copies:
            copy.start()
        for copy in copies:
            copy.wait()
        turned_ref[...] = build_first(raw, w1)
        bias_q = across(w1[:, BIAS_AT + 1 : BIAS_AT + 2], padded)
        bias_v = across(w1[:, BIAS_AT + 2 : BIAS_AT + 3], padded)
        for r in range(regions):
            lanes = slice(r * padded, (r + 1) * padded)
            low = dot(w1[...], series_ref[:, lanes]).astype(half)
            emb_s[:, lanes] = low
            for part in range(3):
                value = dot(wqkv[part * width : (part + 1) * width], low)
                if part == 0:
                    value = (value + bias_q) * HEAD_DIM**-0.5
                elif part == 2:
                    value = value + bias_v
                qkv_s[part * width : (part + 1) * width, lanes] = value.astype(half)
        for copy in outs:
            copy.start()
        wqkv_t[...] = wqkv[...].T

    region = step // (HEADS // per_step)
    first = lax.rem(step, HEADS // per_step) * per_step
    lanes = pl.ds(pl.multiple_of(region * padded, LANES), padded)

    def read(i, part):
        at = pl.multiple_of((first + i) * HEAD_DIM, HEAD_DIM)
        return qkv_s[pl.ds(part * width + at, HEAD_DIM), lanes]

    def store(i, lanes, mixed, log):
        attn_ref[i * HEAD_DIM : (i + 1) * HEAD_DIM, lanes] = mixed
        log_ref[i, :, lanes] = log

    heads_forward(per_step, read, qf_ref[0], kf_ref[0], rows, store)

    @pl.when(step == steps - 1)
    def _():
        for copy in outs:
            copy.wait()


def head_blocks(padded, per_step, first=0):
    groups = HEADS // per_step

    def heads(part=0):
        return pl.BlockSpec(
            (per_step * HEAD_DIM, padded), lambda t: (part * groups + (t + first) % groups, (t + first) // groups)
        )

    feature = pl.BlockSpec((1, HEAD_DIM, padded), lambda t: ((t + first) // groups, 0, 0))
    log = pl.BlockSpec((per_step, 1, padded), lambda t: (t + first, 0, 0))
    return heads, feature, log


def project(me, a_bufs, series, query_f, key_f, rows, width, per_step, steps):
    regions, _, padded = query_f.shape
    tokens = regions * padded
    heads, feature, log = head_blocks(padded, per_step)
    return pl.pallas_call(
        functools.partial(project_kernel, len(a_bufs), per_step, rows, regions),
        grid=(steps,),
        in_specs=[SMEM] + [ANY] * len(a_bufs) + [VMEM, feature, feature],
        out_specs=[ANY, ANY, heads(), log, VMEM, VMEM, VMEM],
        out_shape=[
            jax.ShapeDtypeStruct((3 * width, tokens), half),
            jax.ShapeDtypeStruct((width, tokens), half),
            jax.ShapeDtypeStruct((width, tokens), half),
            jax.ShapeDtypeStruct((regions * HEADS, 1, padded), fp32),
            jax.ShapeDtypeStruct((width, LANES), half),
            jax.ShapeDtypeStruct((LANES, width), fp32),
            jax.ShapeDtypeStruct((width, 3 * width), half),
        ],
        scratch_shapes=[
            pltpu.VMEM((width, 2 * LANES), half),
            pltpu.VMEM((3 * width, width), half),
            pltpu.VMEM((3 * width, tokens), half),
            pltpu.VMEM((width, tokens), half),
            pltpu.SemaphoreType.DMA,
            pltpu.SemaphoreType.DMA((2,)),
        ],
        compiler_params=params(),
        cost_estimate=cost(2e10, 1.5e7),
    )(me, *a_bufs, series, query_f, key_f)


def attend_kernel(per_step, rows, q_ref, k_ref, v_ref, qf_ref, kf_ref, *refs):
    attn_ref, log_ref = refs[-2:]

    def read(i, part):
        return (q_ref, k_ref, v_ref)[part][i * HEAD_DIM : (i + 1) * HEAD_DIM, :]

    def store(i, lanes, mixed, log):
        attn_ref[i * HEAD_DIM : (i + 1) * HEAD_DIM, lanes] = mixed
        log_ref[i, :, lanes] = log

    heads_forward(per_step, read, qf_ref[0], kf_ref[0], rows, store)


def attend(qkv, attn, logs, query_f, key_f, rows, per_step, first):
    padded = query_f.shape[2]
    heads, feature, log = head_blocks(padded, per_step, first)
    return pl.pallas_call(
        functools.partial(attend_kernel, per_step, rows),
        grid=(logs.shape[0] // per_step - first,),
        in_specs=[heads(0), heads(1), heads(2), feature, feature, ANY, ANY],
        out_specs=[heads(), log],
        out_shape=[jax.ShapeDtypeStruct(attn.shape, half), jax.ShapeDtypeStruct(logs.shape, fp32)],
        input_output_aliases={5: 0, 6: 1},
        compiler_params=params(),
        cost_estimate=cost(1e10, 1e7),
    )(qkv, qkv, qkv, query_f, key_f, attn, logs)


NAMES = ("b3", "g0", "b4", "b5", "g1", "b6")
COLUMNS = {"b3": 99, "g0": 103, "b4": 100, "b5": 101, "g1": 104, "b6": 102}


def fold(value):
    total = value[:, :LANES]
    for s in range(LANES, value.shape[1], LANES):
        total = total + value[:, s : s + LANES]
    return total


def mean(value):
    return jnp.mean(value, axis=0, keepdims=True)


def feed_kernel(n_b, rows, regions, parts, me_ref, *refs):
    b_refs, refs = refs[:n_b], refs[n_b:]
    w1_hbm, turned_hbm, series_hbm, attn_ref, ct_ref, out_ref, gattn_ref, gres_ref, keep_ref, send_ref, small_hbm, *refs = refs
    w1_ref, turned_ref, series_ref, small_ref, *refs = refs
    w_out, w_out_t, w_up, w_up_t, w_down, w_down_t, up_b, col, attn_s, ct_s, *refs = refs
    act_s, slope_s, gdown_s, hid_s, gproj_s, gattn_s, flow, norm_s, lo_s, acc, acc_up, sem_in, sem_w, sem_out, sem_g = refs
    width, units = w_up_t.shape
    chunks = units // CHUNK
    padded = attn_s.shape[1] // regions
    count = len(parts)
    me = me_ref[0]
    lanes = [slice(s, s + n) for s, n in parts]

    loads = [
        (
            pltpu.make_async_copy(attn_ref.at[:, pl.ds(s, n)], attn_s.at[:, pl.ds(s, n)], sem_in.at[2 * i]),
            pltpu.make_async_copy(ct_ref.at[:, pl.ds(s, n)], ct_s.at[:, pl.ds(s, n)], sem_in.at[2 * i + 1]),
        )
        for i, (s, n) in enumerate(parts)
    ]
    short = [
        pltpu.make_async_copy(source, target, sem_w.at[3])
        for source, target in ((w1_hbm, w1_ref), (turned_hbm, turned_ref), (series_hbm, series_ref))
    ]
    for copy in short:
        copy.start()
    loads[0][0].start()
    groups = ([], [], [])
    at = 0
    owner_of = owners(me)
    for ref in b_refs:
        for i in range(ref.shape[0]):
            owner, piece = owner_of[at], ref.at[i]
            groups[0].append(pltpu.make_async_copy(piece.at[:, pl.ds(0, width)], w_out.at[rows_of(owner, 16)], sem_w.at[0]))
            for j in range(4):
                groups[1].append(
                    pltpu.make_async_copy(
                        piece.at[:, pl.ds((1 + j) * width, width)],
                        w_up.at[pl.ds(pl.multiple_of(owner * 64 + j * 16, 16), 16)],
                        sem_w.at[1],
                    )
                )
            groups[2].append(pltpu.make_async_copy(piece.at[:, pl.ds(5 * width, units)], w_down.at[rows_of(owner, 16)], sem_w.at[2]))
            at += 1
    for copy in groups[0]:
        copy.start()

    for copy in short:
        copy.wait()
    for i, name in enumerate(NAMES):
        col[i] = across(w1_ref[:, COLUMNS[name] : COLUMNS[name] + 1])
    for owner in range(PIECES):
        up_b[owner * 64 : owner * 64 + 64, :] = jnp.broadcast_to(
            turned_ref[:64, owner * 16 + 9 : owner * 16 + 10], (64, LANES)
        )

    def wide(value, size):
        return jnp.concatenate([value] * (size // LANES), axis=1)

    def column(r, name):
        return wide(col[NAMES.index(name)], parts[r][1])

    def add_to(r, name, value):
        i = NAMES.index(name)
        acc[i] = fold(value) if r == 0 else acc[i] + fold(value)

    rates = [None] * count
    outs = []

    def leave(source, target):
        copy = pltpu.make_async_copy(source, target, sem_out.at[len(outs)])
        copy.start()
        outs.append(copy)

    def enter(r):
        loads[r][0].wait()
        embed = dot(w1_ref[...], series_ref[:, lanes[r]])
        resid = embed + (dot(w_out[...], attn_s[:, lanes[r]]) + column(r, "b3"))
        center = resid - mean(resid)
        rates[r] = lax.rsqrt(mean(center * center) + norm_eps)
        norm = center * rates[r]
        norm_s[:, lanes[r]] = norm
        hidden = norm * column(r, "g0") + column(r, "b4")
        flow[:, lanes[r]] = hidden
        hid_s[:, lanes[r]] = hidden.astype(half)

    def up(r, c):
        part = slice(c * CHUNK, (c + 1) * CHUNK)
        upper = dot(w_up[part, :], hid_s[:, lanes[r]]) + wide(up_b[part, :], parts[r][1])
        square = upper * upper
        turned = 0.5 + 0.5 * jnp.tanh(upper * (gelu_coef + (gelu_coef * 0.044715) * square))
        act = upper * turned
        slope = turned + act * (1.0 - turned) * (2.0 * gelu_coef + (6.0 * gelu_coef * 0.044715) * square)
        slope_s[part, lanes[r]] = slope.astype(half)
        act_s[part, lanes[r]] = act.astype(half)

    def down(r):
        flow[:, lanes[r]] = flow[:, lanes[r]] + (dot(w_down[...], act_s[:, lanes[r]]) + column(r, "b5"))

    def turn(r):
        resid = flow[:, lanes[r]]
        center = resid - mean(resid)
        rate = lax.rsqrt(mean(center * center) + norm_eps)
        norm = center * rate
        lo_s[lanes[r], :] = (norm * column(r, "g1") + column(r, "b6")).astype(half).T
        loads[r][1].wait()
        grad = ct_s[:, lanes[r]].astype(fp32)
        add_to(r, "b6", grad)
        add_to(r, "g1", grad * norm)
        grad = grad * column(r, "g1")
        grad = rate * (grad - mean(grad) - norm * mean(grad * norm))
        add_to(r, "b5", grad)
        flow[:, lanes[r]] = grad
        gdown_s[:, lanes[r]] = grad.astype(half)

    def up_back(r, c):
        part = slice(c * CHUNK, (c + 1) * CHUNK)
        grad = slope_s[part, lanes[r]].astype(fp32) * dot(w_down_t[part, :], gdown_s[:, lanes[r]])
        acc_up[part, :] = fold(grad) if r == 0 else acc_up[part, :] + fold(grad)
        slope_s[part, lanes[r]] = grad.astype(half)

    def back(r):
        flow[:, lanes[r]] = flow[:, lanes[r]] + dot(w_up_t[...], slope_s[:, lanes[r]])

    def leave_norm(r):
        grad = flow[:, lanes[r]]
        norm = norm_s[:, lanes[r]]
        add_to(r, "b4", grad)
        add_to(r, "g0", grad * norm)
        grad = grad * column(r, "g0")
        grad = rates[r] * (grad - mean(grad) - norm * mean(grad * norm))
        add_to(r, "b3", grad)
        flow[:, lanes[r]] = grad
        low = grad.astype(half)
        gproj_s[:, lanes[r]] = low
        gattn_s[:, lanes[r]] = dot(w_out_t[...], low).astype(half)
        at = pl.ds(*parts[r])
        leave(flow.at[:, at], gres_ref.at[:, at])
        leave(gattn_s.at[:, at], gattn_ref.at[:, at])

    for copy in groups[0]:
        copy.wait()
    for group in groups[1:]:
        for copy in group:
            copy.start()
    for first, second in loads:
        if first is not loads[0][0]:
            first.start()
        second.start()
    enter(0)
    for copy in groups[1]:
        copy.wait()
    for r in range(count):
        up(r, 0)
        if r == 0:
            for copy in groups[2]:
                copy.wait()
            w_out_t[...] = w_out[...].T
            w_down_t[...] = w_down[...].T
            w_up_t[...] = w_up[...].T
        up(r, 1)
        if r + 1 < count:
            enter(r + 1)
        if r > 0:
            turn(r - 1)
        for c in range(2, chunks):
            up(r, c)
        down(r)
    for r in range(count):
        up_back(r, 0)
        up_back(r, 1)
        if r == 0:
            turn(count - 1)
            for region in range(regions):
                leave(lo_s.at[pl.ds(region * padded, rows)], out_ref.at[region])
        else:
            leave_norm(r - 1)
        for c in range(2, chunks):
            up_back(r, c)
        back(r)
    leave_norm(count - 1)
    targets = [(keep_ref if r < PIECES // 2 else send_ref).at[r % (PIECES // 2)] for r in range(PIECES)]
    copies = []

    def give(source, column, size):
        copies.append(pltpu.make_async_copy(source, target.at[:, pl.ds(column, size)], sem_g))
        copies[-1].start()

    w_up[...] = dot(slope_s[...], hid_s[...], 1, 1).astype(half)
    for owner, target in zip(owner_of, targets):
        for j in range(4):
            give(w_up.at[pl.ds(pl.multiple_of(owner * 64 + j * 16, 16), 16)], (1 + j) * width, width)
    w_out[...] = dot(gproj_s[...], attn_s[...], 1, 1).astype(half)
    w_down[...] = dot(gdown_s[...], act_s[...], 1, 1).astype(half)
    for owner, target in zip(owner_of, targets):
        give(w_out.at[rows_of(owner, 16)], 0, width)
        give(w_down.at[rows_of(owner, 16)], 5 * width, units)
    total = jnp.zeros((width, LANES), fp32)
    lane = lax.broadcasted_iota(jnp.int32, (width, LANES), 1)
    for i, name in enumerate(NAMES):
        total = total + jnp.where(lane == COLUMNS[name], jnp.sum(acc[i], axis=1, keepdims=True), 0.0)
    up_sum = jnp.sum(acc_up[...], axis=1, keepdims=True).reshape(PIECES, UP_COLUMNS, 16, 1)
    for c in range(UP_COLUMNS):
        total = total + jnp.where(lane == UP_AT + c, up_sum[:, c].reshape(width, 1), 0.0)
    small_ref[...] = total
    leave(small_ref, small_hbm)
    for copy in copies:
        copy.wait()
    for copy in outs:
        copy.wait()


def feed(me, b_bufs, w1, turned, series, attn, cotangent, regions, rows, units):
    width, tokens = attn.shape
    half_set = jax.ShapeDtypeStruct((PIECES // 2, 16, 5 * width + units), half)
    low_all = pltpu.VMEM((width, tokens), half)
    parts = ((0, tokens // 2 // TILE * TILE), (tokens // 2 // TILE * TILE, tokens - tokens // 2 // TILE * TILE))
    return pl.pallas_call(
        functools.partial(feed_kernel, len(b_bufs), rows, regions, parts),
        in_specs=[SMEM] + [ANY] * len(b_bufs) + [ANY] * 5,
        out_specs=[ANY] * 6,
        out_shape=[
            jax.ShapeDtypeStruct((regions, rows, width), half),
            jax.ShapeDtypeStruct((width, tokens), half),
            jax.ShapeDtypeStruct((width, tokens), fp32),
            half_set,
            half_set,
            jax.ShapeDtypeStruct((width, LANES), fp32),
        ],
        scratch_shapes=[
            pltpu.VMEM(w1.shape, half),
            pltpu.VMEM(turned.shape, fp32),
            pltpu.VMEM(series.shape, half),
            pltpu.VMEM((width, LANES), fp32),
            pltpu.VMEM((width, width), half),
            pltpu.VMEM((width, width), half),
            pltpu.VMEM((units, width), half),
            pltpu.VMEM((width, units), half),
            pltpu.VMEM((width, units), half),
            pltpu.VMEM((units, width), half),
            pltpu.VMEM((units, LANES), fp32),
            pltpu.VMEM((len(NAMES), width, LANES), fp32),
            low_all,
            low_all,
            pltpu.VMEM((units, tokens), half),
            pltpu.VMEM((units, tokens), half),
            low_all,
            low_all,
            low_all,
            low_all,
            pltpu.VMEM((width, tokens), fp32),
            pltpu.VMEM((width, tokens), fp32),
            pltpu.VMEM((tokens, width), half),
            pltpu.VMEM((len(NAMES), width, LANES), fp32),
            pltpu.VMEM((units, LANES), fp32),
            pltpu.SemaphoreType.DMA((2 * len(parts),)),
            pltpu.SemaphoreType.DMA((4,)),
            pltpu.SemaphoreType.DMA((regions + 2 * len(parts) + 1,)),
            pltpu.SemaphoreType.DMA,
        ],
        compiler_params=params(),
        cost_estimate=cost(4e10, 2e7),
    )(me, *b_bufs, w1, turned, series, attn, cotangent)


def heads_back(per_step, rows, refs, store):
    q_ref, k_ref, v_ref, attn_ref, gattn_ref, log_ref, qf_ref, kf_ref = refs
    padded = qf_ref.shape[2]
    query_f, key_f = qf_ref[0], kf_ref[0]
    blocks = [(s, min(TILE, rows - s)) for s in range(0, rows, TILE)]
    filler = jnp.zeros((13, padded), fp32)

    def in_three(row):
        first = row.astype(half).astype(fp32)
        left = row - first
        second = left.astype(half).astype(fp32)
        return jnp.concatenate([first, second, left - second, filler], axis=0).astype(half)

    for i in range(per_step):
        head = slice(i * HEAD_DIM, (i + 1) * HEAD_DIM)
        query, keys, values, grad = q_ref[head, :], k_ref[head, :], v_ref[head, :], gattn_ref[head, :]
        inner = jnp.sum(grad.astype(fp32) * attn_ref[head, :].astype(fp32), axis=0, keepdims=True)
        query_a = jnp.concatenate([query, in_three(-log_ref[i]), query_f[16:]], axis=0).T
        grad_a = jnp.concatenate([grad, in_three(-inner), jnp.zeros((48, padded), half)], axis=0).T
        keys_a = jnp.concatenate([keys, key_f], axis=0)
        values_a = jnp.concatenate([values, key_f], axis=0)
        grad_keys = grad_values = None
        grad_query = []
        for s, n in blocks:
            probs = jnp.exp(dot(query_a[s : s + n], keys_a))
            raw = (probs * dot(grad_a[s : s + n], values_a)).astype(half)
            more_v = dot(grad[:, s : s + n], probs.astype(half))
            more_k = dot(query[:, s : s + n], raw)
            grad_values = more_v if grad_values is None else grad_values + more_v
            grad_keys = more_k if grad_keys is None else grad_keys + more_k
            grad_query.append((dot(keys, raw, 1, 1) * HEAD_DIM**-0.5).astype(half))
        grad_query.append(jnp.zeros((HEAD_DIM, padded - rows), half))
        store(i, (jnp.concatenate(grad_query, axis=1), grad_keys.astype(half), grad_values.astype(half)))


def attend_back_kernel(per_step, rows, *refs):
    grad_ref = refs[8]

    def store(i, three):
        for part, value in enumerate(three):
            grad_ref[0, part, i * HEAD_DIM : (i + 1) * HEAD_DIM, :] = value

    heads_back(per_step, rows, refs[:8], store)


def finish_kernel(per_step, rows, counts, me_ref, *refs):
    ins, done_refs, refs = refs[:8], refs[8 : 8 + len(counts)], refs[8 + len(counts) :]
    first = sum(counts)
    emb_ref, gres_ref, series_ref, wqkv_t_ref, w1_ref, small_ref, keep_ref, send_ref, lbg_hbm, lbg_ref, *refs = refs
    grad_s, emb_s, gres_s, wqkv_t, g_qkv, g_one, sem, sem_out = refs
    step, steps = pl.program_id(0), pl.num_programs(0)
    width, tokens = emb_s.shape
    regions, lags, _ = lbg_ref.shape
    padded = tokens // regions
    groups = HEADS // per_step
    height = per_step * HEAD_DIM
    brought = [
        pltpu.make_async_copy(emb_ref, emb_s, sem),
        pltpu.make_async_copy(gres_ref, gres_s, sem),
        pltpu.make_async_copy(wqkv_t_ref, wqkv_t, sem),
    ]
    done = [ref.at[t] for ref in done_refs for t in range(ref.shape[0])]
    for t in range(first):
        for part in range(3):
            brought.append(
                pltpu.make_async_copy(
                    done[t].at[part],
                    grad_s.at[
                        pl.ds(part * width + (t % groups) * height, height), pl.ds(t // groups * padded, padded)
                    ],
                    sem,
                )
            )

    @pl.when(step == 0)
    def _():
        for copy in brought:
            copy.start()

    now = step + first
    lanes = pl.ds(pl.multiple_of(now // groups * padded, LANES), padded)
    rows_at = lax.rem(now, groups) * height

    def store(i, three):
        for part, value in enumerate(three):
            at = pl.multiple_of(part * width + rows_at + i * HEAD_DIM, HEAD_DIM)
            grad_s[pl.ds(at, HEAD_DIM), lanes] = value

    heads_back(per_step, rows, ins, store)

    @pl.when(step == steps - 1)
    def _():
        for copy in brought:
            copy.wait()
        owner_of = owners(me_ref[0])
        for part in range(3):
            at = slice(part * width, (part + 1) * width)
            g_qkv[at, :] = dot(grad_s[at, :], emb_s[...], 1, 1).astype(half)
        copies = []
        for r, owner in enumerate(owner_of):
            target = (keep_ref if r < PIECES // 2 else send_ref).at[r % (PIECES // 2)]
            for j in range(3):
                copies.append(
                    pltpu.make_async_copy(
                        g_qkv.at[pl.ds(pl.multiple_of(owner * 48 + j * 16, 16), 16)],
                        target.at[:, pl.ds(j * width, width)],
                        sem_out.at[0],
                    )
                )
        for copy in copies:
            copy.start()
        total = small_ref[...]
        lane = lax.broadcasted_iota(jnp.int32, total.shape, 1)
        for i, part in enumerate((0, 2)):
            bias = fold(grad_s[part * width : (part + 1) * width, :].astype(fp32))
            total = total + jnp.where(lane == BIAS_AT + 1 + i, jnp.sum(bias, axis=1, keepdims=True), 0.0)
        low = (gres_s[...] + dot(wqkv_t[...], grad_s[...])).astype(half)
        total = total + dot(low, series_ref[...], 1, 1)
        for r in range(regions):
            lbg_ref[r] = dot(w1_ref[...], low[:, r * padded : (r + 1) * padded], 0, 0)[:lags, :rows]
        lbg_out = pltpu.make_async_copy(lbg_ref, lbg_hbm, sem_out.at[2])
        lbg_out.start()
        g_one[...] = total.astype(half)
        more = []
        for r, owner in enumerate(owner_of):
            target = (keep_ref if r < PIECES // 2 else send_ref).at[r % (PIECES // 2)]
            more.append(
                pltpu.make_async_copy(
                    g_one.at[rows_of(owner, 16)], target.at[:, pl.ds(3 * width, LANES)], sem_out.at[1]
                )
            )
        for copy in more:
            copy.start()
        for copy in copies:
            copy.wait()
        for copy in more:
            copy.wait()
        lbg_out.wait()


def back_operands(qkv, attn, grad_attn, logs, query_f, key_f, per_step, first):
    heads, feature, log = head_blocks(query_f.shape[2], per_step, first)
    specs = [heads(0), heads(1), heads(2), heads(), heads(), log, feature, feature]
    return specs, (qkv, qkv, qkv, attn, grad_attn, logs, query_f, key_f)


def attend_back(qkv, attn, grad_attn, logs, query_f, key_f, rows, per_step, first, steps):
    padded = query_f.shape[2]
    specs, operands = back_operands(qkv, attn, grad_attn, logs, query_f, key_f, per_step, first)
    shape = (3, per_step * HEAD_DIM, padded)
    grad_spec = pl.BlockSpec((1, *shape), lambda t: (t, 0, 0, 0))
    grad_shape = jax.ShapeDtypeStruct((steps, *shape), half)
    return pl.pallas_call(
        functools.partial(attend_back_kernel, per_step, rows),
        grid=(steps,),
        in_specs=specs,
        out_specs=grad_spec,
        out_shape=grad_shape,
        compiler_params=params(60),
        cost_estimate=cost(2e10, 1e7),
    )(*operands)


def finish(me, qkv, attn, grad_attn, logs, query_f, key_f, done, embed_low, grad_resid, series, wqkv_t, w1, small, rows, lags, per_step):
    regions, _, padded = query_f.shape
    width, tokens = attn.shape
    counts = tuple(value.shape[0] for value in done)
    first = sum(counts)
    specs, operands = back_operands(qkv, attn, grad_attn, logs, query_f, key_f, per_step, first)
    half_set = jax.ShapeDtypeStruct((PIECES // 2, 16, 3 * width + LANES), half)
    return pl.pallas_call(
        functools.partial(finish_kernel, per_step, rows, counts),
        grid=(logs.shape[0] // per_step - first,),
        in_specs=[SMEM] + specs + [ANY] * len(done) + [ANY, ANY, VMEM, ANY, VMEM, VMEM],
        out_specs=[ANY, ANY, ANY],
        out_shape=[half_set, half_set, jax.ShapeDtypeStruct((regions, lags, rows), fp32)],
        scratch_shapes=[
            pltpu.VMEM((regions, lags, rows), fp32),
            pltpu.VMEM((3 * width, tokens), half),
            pltpu.VMEM((width, tokens), half),
            pltpu.VMEM((width, tokens), fp32),
            pltpu.VMEM((width, 3 * width), half),
            pltpu.VMEM((3 * width, width), half),
            pltpu.VMEM((width, LANES), half),
            pltpu.SemaphoreType.DMA,
            pltpu.SemaphoreType.DMA((3,)),
        ],
        compiler_params=params(),
        cost_estimate=cost(4e10, 2e7),
    )(me, *operands, *done, embed_low, grad_resid, series, wqkv_t, w1, small)


def send(value, offset):
    return lax.ppermute(value, AXES, [(i, i ^ offset) for i in range(PIECES)])


def after(value, *others):
    return lax.optimization_barrier((value, *others))[0]


def along_z(piece):
    return jnp.stack([piece] + [send(piece, 2 * s) for s in range(1, 4)])


def along_plane(value):
    return [value] + [send(value, offset) for offset in (1, 16, 17)]


def along_core(plane):
    return plane + [send(part, 8) for part in plane]


def add(*terms):
    return sum(term.astype(fp32) for term in terms)


def quarters(low):
    return [low[4 * i : 4 * i + 4] for i in range(4)]


def add_core(keep, got):
    return [add(*pair).astype(half) for pair in zip(quarters(keep), quarters(got))]


def sum_plane(lows):
    return [lows[0]] + [send(low, offset) for low, offset in zip(lows[1:], (1, 16, 17))]


def add_plane(parts):
    return [add(*[part[s] for part in parts]).astype(half) for s in range(4)]


def sum_z(lows):
    return [lows[0]] + [send(lows[s], 2 * s) for s in range(1, 4)]


def stacked(value, width):
    return jnp.concatenate([value[:, s : s + width] for s in range(0, value.shape[1], width)], axis=0)


def unpack_one(packed, lags):
    up = packed[:, UP_AT : UP_AT + UP_COLUMNS].reshape(-1, 16, UP_COLUMNS).transpose(0, 2, 1).reshape(-1)
    return packed[:, :lags], packed[:, BIAS_AT:GAIN_AT].T, packed[:, GAIN_AT:UP_AT].T, up


def body(
    ours,
    lookback,
    bucket_size,
    variate_mask,
    w_embed,
    w_qkv,
    w_out,
    w_up,
    w_down,
    up_bias,
    biases,
    gains,
    cotangent,
):
    regions, rows, lags = lookback.shape
    width = w_qkv.shape[1]
    units = w_down.shape[1]
    padded = -(-rows // LANES) * LANES
    per_step = 4
    steps = regions * HEADS // per_step
    per_step_f = 2
    steps_f = regions * HEADS // per_step_f
    lookback_t = lookback.transpose(0, 2, 1)
    series, masked, query_f, key_f = prepare(bucket_size, variate_mask, lookback_t, cotangent, padded, 32)

    if ours:
        index = lax.axis_index(AXES).astype(jnp.int32)
        piece_a, piece_b = pack(w_embed, w_qkv, w_out, w_up, w_down, up_bias, biases, gains)
        z_a = after(along_z(piece_a), series)
        z_b = along_z(piece_b)
        plane_a = along_plane(z_a)
        plane_b = along_plane(after(z_b, z_a))
        a_bufs = along_core(plane_a)
    else:
        index = jnp.zeros((), jnp.int32)

        def whole(value, axis=0):
            return lax.all_gather(value, AXES, axis=axis, tiled=True)

        def cut(value, axis=0):
            shape = value.shape[:axis] + (PIECES, value.shape[axis] // PIECES) + value.shape[axis + 1 :]
            return jnp.moveaxis(value.reshape(shape), axis, 0)

        early = jnp.array(OFFSETS)
        short = jax.vmap(short_block)(cut(whole(biases, 1), 1), cut(whole(gains, 1), 1), cut(whole(up_bias)))
        a_bufs = [jax.vmap(first_piece)(cut(whole(w_embed)), short, cut(whole(w_qkv)))[early]]
        b_bufs = [jax.vmap(second_piece)(cut(whole(w_out)), cut(whole(w_up)), cut(whole(w_down)))[early]]
    me = index.reshape(1)

    qkv, embed_low, attn, logs, w1, turned, wqkv_t = project(
        me, a_bufs, series, query_f, key_f, rows, width, per_step_f, steps_f - 1
    )
    if ours:
        b_bufs = along_core(plane_b[:1]) + along_core([after(part, logs) for part in plane_b[1:]])
        b_bufs = [b_bufs[0], *b_bufs[2:5], b_bufs[1], *b_bufs[5:]]
    attn, logs = attend(qkv, attn, logs, query_f, key_f, rows, per_step_f, steps_f - 1)
    layer_out, grad_attn, grad_resid, keep_b, send_b, sums = feed(
        me, b_bufs, w1, turned, series, attn, masked, regions, rows, units
    )
    if ours:
        core_b = send(send_b, 8)
    done = [attend_back(qkv, attn, grad_attn, logs, query_f, key_f, rows, per_step, 0, steps - 2)]
    if ours:
        lows_b = add_core(keep_b, after(core_b, *done))
        parts_b = sum_plane(lows_b)
        grad_attn = after(grad_attn, *lows_b)
    keep_a, send_a, lookback_grad = finish(
        me, qkv, attn, grad_attn, logs, query_f, key_f, done, embed_low, grad_resid, series, wqkv_t, w1, sums, rows, lags, per_step
    )
    lookback_grad = lookback_grad.transpose(0, 2, 1)

    def parts_of(grad_a, grad_b):
        w_qkv_part = stacked(grad_a[:, : 3 * width], width)
        return w_qkv_part, grad_a[:, 3 * width :], grad_b[:, :width], stacked(grad_b[:, width : 5 * width], width), grad_b[:, 5 * width :]

    if ours:
        core_a = send(send_a, 8)
        parts_b = sum_z(add_plane([after(part, keep_a) for part in parts_b]))
        lows_a = add_core(keep_a, after(core_a, parts_b[0]))
        lows_a = add_plane(sum_plane(lows_a))
        grad_out, grad_up, grad_down = unpack_second([after(part, *lows_a) for part in parts_b], width, units)
        parts_a = sum_z(lows_a)
        grad_qkv, grad_embed, grad_up_bias, grad_biases, grad_gains = unpack_first(parts_a, width, lags)
    else:
        def shared(value, axis=0):
            return lax.psum_scatter(value, AXES, scatter_dimension=axis, tiled=True)

        order = jnp.argsort(jnp.array(OFFSETS, jnp.int32))
        grad_a = jnp.concatenate([keep_a, send_a], axis=0).astype(fp32)[order]
        grad_b = jnp.concatenate([keep_b, send_b], axis=0).astype(fp32)[order]
        whole_parts = [value.reshape(-1, value.shape[-1]) for value in jax.vmap(parts_of)(grad_a, grad_b)]
        grad_embed, grad_biases, grad_gains, grad_up_bias = unpack_one(whole_parts[1], lags)
        grad_qkv, grad_out, grad_up, grad_down = (shared(whole_parts[i]) for i in (0, 2, 3, 4))
        grad_embed, grad_up_bias = shared(grad_embed), shared(grad_up_bias)
        grad_biases, grad_gains = shared(grad_biases, 1), shared(grad_gains, 1)
    return (
        layer_out,
        lookback_grad,
        grad_embed,
        grad_qkv,
        grad_out,
        grad_up,
        grad_down,
        grad_up_bias,
        grad_biases,
        grad_gains,
    )


def solution(mesh):
    one = P(AXES)
    rows = P(AXES, None)
    blocks = P(AXES, None, None)
    columns = P(None, AXES)
    in_specs = (blocks, one, rows, rows, rows, rows, rows, rows, one, columns, columns, blocks)
    out_specs = (blocks, blocks, rows, rows, rows, rows, rows, one, columns, columns)
    ours = tuple(mesh.shape[axis] for axis in AXES) == (4, 8)
    return jax.shard_map(
        functools.partial(body, ours), mesh=mesh, in_specs=in_specs, out_specs=out_specs, check_vma=False
    )
```

```python
import functools

import jax
import jax.numpy as jnp
from jax import lax
from jax.experimental import pallas as pl
from jax.experimental.pallas import tpu as pltpu
from jax.sharding import PartitionSpec as P

HEADS = 8
HEAD_DIM = 64
PIECES = 32
LANES = 128
TILE = 256
CHUNK = 512
SPAN = 512
AXES = ("dp", "fsdp")

norm_eps = 1e-05
masked_score = -1e30
gelu_coef = 0.7978845608028654

half = jnp.bfloat16
fp32 = jnp.float32

OFFSETS = tuple(
    core * 8 + x * 16 + y + z * 2
    for core in range(2)
    for x in range(2)
    for y in range(2)
    for z in range(4)
)

BIAS_AT = 96
GAIN_AT = 103
UP_AT = 105
UP_COLUMNS = 4


def dot(left, right, left_dim=1, right_dim=0):
    return lax.dot_general(
        left, right, (((left_dim,), (right_dim,)), ((), ())), preferred_element_type=fp32
    )


def params(mebibytes=62):
    return pltpu.CompilerParams(vmem_limit_bytes=mebibytes * 2**20)


def cost(flops, moved):
    return pl.CostEstimate(flops=int(flops), bytes_accessed=int(moved), transcendentals=0)


VMEM = pl.BlockSpec(memory_space=pltpu.VMEM)
SMEM = pl.BlockSpec(memory_space=pltpu.SMEM)
ANY = pl.BlockSpec(memory_space=pl.ANY)


def piece_copies(me, refs, sem, place):
    copies = []
    at = 0
    for ref in refs:
        for i in range(ref.shape[0]):
            owner = jnp.bitwise_xor(me, OFFSETS[at])
            for source, target in place(ref.at[i], owner):
                copies.append(pltpu.make_async_copy(source, target, sem))
            at += 1
    return copies


def rows_of(owner, count):
    return pl.ds(pl.multiple_of(owner * count, 16), count)


def owners(me):
    return [jnp.bitwise_xor(me, offset) for offset in OFFSETS]


def across(column, lanes=LANES):
    return jnp.broadcast_to(column.astype(fp32), (column.shape[0], lanes))


def prepare_kernel(small, bucket_ref, mask_ref, lb_ref, ct_ref, series_ref, masked_ref, qf_ref, kf_ref):
    regions, rows = mask_ref.shape
    padded = qf_ref.shape[2]
    lags, width = lb_ref.shape[1], ct_ref.shape[2]
    last = rows // small - 1
    spare = padded - rows
    number = lax.broadcasted_iota(jnp.int32, (HEAD_DIM, padded), 0) - 16
    place = lax.broadcasted_iota(jnp.int32, (HEAD_DIM, padded), 1)
    counted = (number >= 0) & (number <= last)
    below = lax.broadcasted_iota(jnp.int32, (LANES - lags, padded), 0)
    for r in range(regions):
        lanes = slice(r * padded, (r + 1) * padded)
        valid = jnp.concatenate([mask_ref[r : r + 1, :].astype(fp32), jnp.zeros((1, spare), fp32)], axis=1)
        turned = jnp.concatenate([ct_ref[r].T, jnp.zeros((width, spare), half)], axis=1)
        masked_ref[:, lanes] = (turned.astype(fp32) * valid).astype(half)
        values = jnp.concatenate([lb_ref[r], jnp.zeros((lags, spare), half)], axis=1)
        series_ref[:lags, lanes] = values
        series_ref[lags:, lanes] = jnp.where(below == 0, 1.0, 0.0).astype(half)
        bucket = bucket_ref[r]
        window = jnp.floor((place.astype(fp32) + 0.5) / bucket.astype(fp32)).astype(jnp.int32)
        window = jnp.minimum(window, last)
        qf_ref[r] = (
            jnp.where(counted & (window != number), masked_score, 0.0) + jnp.where(number == last + 1, 1.0, 0.0)
        ).astype(half)
        kf_ref[r] = (
            jnp.where(counted & (window == number), 1.0, 0.0)
            + jnp.where((number >= -16) & (number < -13), 1.0, 0.0)
            + jnp.where(number == last + 1, jnp.where(valid > 0, 0.0, masked_score), 0.0)
        ).astype(half)


def prepare(bucket_size, variate_mask, lookback_t, cotangent, padded, small):
    regions, rows, width = cotangent.shape
    tokens = regions * padded
    feature = jax.ShapeDtypeStruct((regions, HEAD_DIM, padded), half)
    return pl.pallas_call(
        functools.partial(prepare_kernel, small),
        in_specs=[SMEM, VMEM, VMEM, VMEM],
        out_specs=[VMEM] * 4,
        out_shape=[
            jax.ShapeDtypeStruct((LANES, tokens), half),
            jax.ShapeDtypeStruct((width, tokens), half),
            feature,
            feature,
        ],
        compiler_params=params(),
        cost_estimate=cost(1e7, 8e6),
    )(bucket_size, variate_mask, lookback_t, cotangent)


def short_block(biases, gains, up_bias):
    width = biases.shape[1]
    up_bias = up_bias.reshape(1, -1)
    return jnp.concatenate(
        [
            jnp.concatenate([biases, jnp.zeros((7, LANES - width), biases.dtype)], axis=1),
            jnp.concatenate([gains, jnp.zeros((2, LANES - width), biases.dtype)], axis=1),
            jnp.concatenate([up_bias, jnp.zeros((1, LANES - up_bias.shape[1]), biases.dtype)], axis=1),
            jnp.zeros((6, LANES), biases.dtype),
        ],
        axis=0,
    )


def side_by_side(value):
    return [value[s : s + 16] for s in range(0, value.shape[0], 16)]


def first_piece(w_embed, short, w_qkv):
    spare = jnp.zeros((w_embed.shape[0], LANES - w_embed.shape[1]), half)
    return jnp.concatenate([*side_by_side(w_qkv), w_embed, spare, short], axis=1)


def second_piece(w_out, w_up, w_down):
    return jnp.concatenate([w_out, *side_by_side(w_up), w_down], axis=1)


def pack_kernel(embed_ref, qkv_ref, out_ref, up_ref, down_ref, up_bias_ref, bias_ref, gain_ref, first_ref, second_ref):
    width = qkv_ref.shape[1]
    for j in range(3):
        first_ref[:, j * width : (j + 1) * width] = qkv_ref[j * 16 : (j + 1) * 16, :]
    spare = jnp.zeros((16, LANES - embed_ref.shape[1]), half)
    first_ref[:, 3 * width : 3 * width + LANES] = jnp.concatenate([embed_ref[...], spare], axis=1)
    short = short_block(bias_ref[...].astype(fp32), gain_ref[...].astype(fp32), up_bias_ref[...].astype(fp32))
    first_ref[:, 3 * width + LANES :] = short.astype(half)
    second_ref[:, :width] = out_ref[...]
    for j in range(4):
        second_ref[:, (1 + j) * width : (2 + j) * width] = up_ref[j * 16 : (j + 1) * 16, :]
    second_ref[:, 5 * width :] = down_ref[...]


def pack(w_embed, w_qkv, w_out, w_up, w_down, up_bias, biases, gains):
    width, units = w_out.shape[1], w_down.shape[1]
    return pl.pallas_call(
        pack_kernel,
        in_specs=[VMEM] * 8,
        out_specs=[VMEM] * 2,
        out_shape=[
            jax.ShapeDtypeStruct((16, 3 * width + 2 * LANES), half),
            jax.ShapeDtypeStruct((16, 5 * width + units), half),
        ],
    )(w_embed, w_qkv, w_out, w_up, w_down, up_bias.reshape(1, -1), biases, gains)


def brought(refs, places, sem):
    copies = [pltpu.make_async_copy(ref, place, sem.at[i]) for i, (ref, place) in enumerate(zip(refs, places))]
    for copy in copies:
        copy.start()
    for copy in copies:
        copy.wait()
    return lambda columns: sum(place[:, columns].astype(fp32) for place in places)


def unpack_first_kernel(*refs):
    parts, (qkv_ref, embed_ref, up_ref, bias_ref, gain_ref), places, sem = refs[:4], refs[4:9], refs[9:13], refs[13]
    total = brought(parts, places, sem)(slice(None))
    width = qkv_ref.shape[1]
    for j in range(3):
        qkv_ref[j * 16 : (j + 1) * 16, :] = total[:, j * width : (j + 1) * width]
    rest = total[:, 3 * width :]
    embed_ref[...] = rest[:, : embed_ref.shape[1]]
    turned = rest.T
    bias_ref[...] = turned[BIAS_AT:GAIN_AT, :]
    gain_ref[...] = turned[GAIN_AT:UP_AT, :]
    up_ref[...] = jnp.concatenate([turned[UP_AT + c : UP_AT + c + 1, :] for c in range(UP_COLUMNS)], axis=1)


def unpack_first(parts, width, lags):
    qkv, embed, up, bias, gain = pl.pallas_call(
        unpack_first_kernel,
        in_specs=[ANY] * 4,
        out_specs=[VMEM] * 5,
        out_shape=[
            jax.ShapeDtypeStruct((48, width), fp32),
            jax.ShapeDtypeStruct((16, lags), fp32),
            jax.ShapeDtypeStruct((1, 16 * UP_COLUMNS), fp32),
            jax.ShapeDtypeStruct((7, 16), fp32),
            jax.ShapeDtypeStruct((2, 16), fp32),
        ],
        scratch_shapes=[pltpu.VMEM(part.shape, half) for part in parts] + [pltpu.SemaphoreType.DMA((4,))],
    )(*parts)
    return qkv, embed, up.reshape(-1), bias, gain


def unpack_second_kernel(*refs):
    parts, (out_ref, up_ref, down_ref), places, sem = refs[:4], refs[4:7], refs[7:11], refs[11]
    width = out_ref.shape[1]
    total = brought(parts, places, sem)
    out_ref[...] = total(slice(0, width))
    for j in range(4):
        up_ref[j * 16 : (j + 1) * 16, :] = total(slice((1 + j) * width, (2 + j) * width))
    down_ref[...] = total(slice(5 * width, None))


def unpack_second(parts, width, units):
    return pl.pallas_call(
        unpack_second_kernel,
        in_specs=[ANY] * 4,
        out_specs=[VMEM] * 3,
        out_shape=[
            jax.ShapeDtypeStruct((16, width), fp32),
            jax.ShapeDtypeStruct((64, width), fp32),
            jax.ShapeDtypeStruct((16, units), fp32),
        ],
        scratch_shapes=[pltpu.VMEM(part.shape, half) for part in parts] + [pltpu.SemaphoreType.DMA((4,))],
    )(*parts)


def build_first(raw, w1):
    turned = raw[:, LANES:].astype(fp32).T
    for owner in range(PIECES):
        at = slice(owner * 16, owner * 16 + 16)
        short = turned[:16, at]
        w1[at, :] = jnp.concatenate(
            [raw[at, :BIAS_AT].astype(fp32), short[:, :9], jnp.zeros((16, LANES - BIAS_AT - 9), fp32)], axis=1
        ).astype(half)
    return turned


def scores_of(query, keys, query_f, key_f, rows):
    padded = query_f.shape[1]
    keys_t = jnp.concatenate([keys, key_f], axis=0).T[:rows]
    query_a = jnp.concatenate([query, query_f], axis=0)
    return [dot(keys_t, query_a[:, s : min(s + TILE, padded)]) for s in range(0, padded, TILE)]


def mix(scores, values, rows, store):
    values_a = jnp.concatenate([values[:, :rows], jnp.ones((16, rows), half)], axis=0)
    for i, score in enumerate(scores):
        top = jnp.max(score, axis=0, keepdims=True)
        expo = jnp.exp(score - top).astype(half)
        mixed = dot(values_a, expo)
        total = mixed[HEAD_DIM : HEAD_DIM + 1]
        lanes = slice(i * TILE, i * TILE + score.shape[1])
        store(lanes, (mixed[:HEAD_DIM] * (1.0 / total)).astype(half), top + jnp.log(total))


def heads_forward(count, read, query_f, key_f, rows, store):
    ahead = scores_of(read(0, 0), read(0, 1), query_f, key_f, rows)
    for i in range(count):
        scores = ahead
        if i + 1 < count:
            ahead = scores_of(read(i + 1, 0), read(i + 1, 1), query_f, key_f, rows)
        mix(scores, read(i, 2), rows, functools.partial(store, i))


def project_kernel(n_a, per_step, rows, regions, me_ref, *refs):
    a_refs, refs = refs[:n_a], refs[n_a:]
    series_ref, qf_ref, kf_ref, qkv_ref, emb_ref, attn_ref, log_ref, w1, turned_ref, wqkv_t, *refs = refs
    raw, wqkv, qkv_s, emb_s, sem, sem_out = refs
    step, steps = pl.program_id(0), pl.num_programs(0)
    padded = qf_ref.shape[2]
    width = emb_s.shape[0]
    outs = [
        pltpu.make_async_copy(qkv_s, qkv_ref, sem_out.at[0]),
        pltpu.make_async_copy(emb_s, emb_ref, sem_out.at[1]),
    ]

    @pl.when(step == 0)
    def _():
        def place(piece, owner):
            return [
                (piece.at[:, pl.ds(j * width, width)], wqkv.at[pl.ds(pl.multiple_of(owner * 48 + j * 16, 16), 16)])
                for j in range(3)
            ] + [(piece.at[:, pl.ds(3 * width, 2 * LANES)], raw.at[rows_of(owner, 16)])]

        copies = piece_copies(me_ref[0], a_refs, sem, place)
        for copy in copies:
            copy.start()
        for copy in copies:
            copy.wait()
        turned_ref[...] = build_first(raw, w1)
        bias_q = across(w1[:, BIAS_AT + 1 : BIAS_AT + 2], padded)
        bias_v = across(w1[:, BIAS_AT + 2 : BIAS_AT + 3], padded)
        for r in range(regions):
            lanes = slice(r * padded, (r + 1) * padded)
            low = dot(w1[...], series_ref[:, lanes]).astype(half)
            emb_s[:, lanes] = low
            for part in range(3):
                value = dot(wqkv[part * width : (part + 1) * width], low)
                if part == 0:
                    value = (value + bias_q) * HEAD_DIM**-0.5
                elif part == 2:
                    value = value + bias_v
                qkv_s[part * width : (part + 1) * width, lanes] = value.astype(half)
        for copy in outs:
            copy.start()
        wqkv_t[...] = wqkv[...].T

    region = step // (HEADS // per_step)
    first = lax.rem(step, HEADS // per_step) * per_step
    lanes = pl.ds(pl.multiple_of(region * padded, LANES), padded)

    def read(i, part):
        at = pl.multiple_of((first + i) * HEAD_DIM, HEAD_DIM)
        return qkv_s[pl.ds(part * width + at, HEAD_DIM), lanes]

    def store(i, lanes, mixed, log):
        attn_ref[i * HEAD_DIM : (i + 1) * HEAD_DIM, lanes] = mixed
        log_ref[i, :, lanes] = log

    heads_forward(per_step, read, qf_ref[0], kf_ref[0], rows, store)

    @pl.when(step == steps - 1)
    def _():
        for copy in outs:
            copy.wait()


def head_blocks(padded, per_step, first=0):
    groups = HEADS // per_step

    def heads(part=0):
        return pl.BlockSpec(
            (per_step * HEAD_DIM, padded), lambda t: (part * groups + (t + first) % groups, (t + first) // groups)
        )

    feature = pl.BlockSpec((1, HEAD_DIM, padded), lambda t: ((t + first) // groups, 0, 0))
    log = pl.BlockSpec((per_step, 1, padded), lambda t: (t + first, 0, 0))
    return heads, feature, log


def project(me, a_bufs, series, query_f, key_f, rows, width, per_step, steps):
    regions, _, padded = query_f.shape
    tokens = regions * padded
    heads, feature, log = head_blocks(padded, per_step)
    return pl.pallas_call(
        functools.partial(project_kernel, len(a_bufs), per_step, rows, regions),
        grid=(steps,),
        in_specs=[SMEM] + [ANY] * len(a_bufs) + [VMEM, feature, feature],
        out_specs=[ANY, ANY, heads(), log, VMEM, VMEM, VMEM],
        out_shape=[
            jax.ShapeDtypeStruct((3 * width, tokens), half),
            jax.ShapeDtypeStruct((width, tokens), half),
            jax.ShapeDtypeStruct((width, tokens), half),
            jax.ShapeDtypeStruct((regions * HEADS, 1, padded), fp32),
            jax.ShapeDtypeStruct((width, LANES), half),
            jax.ShapeDtypeStruct((LANES, width), fp32),
            jax.ShapeDtypeStruct((width, 3 * width), half),
        ],
        scratch_shapes=[
            pltpu.VMEM((width, 2 * LANES), half),
            pltpu.VMEM((3 * width, width), half),
            pltpu.VMEM((3 * width, tokens), half),
            pltpu.VMEM((width, tokens), half),
            pltpu.SemaphoreType.DMA,
            pltpu.SemaphoreType.DMA((2,)),
        ],
        compiler_params=params(),
        cost_estimate=cost(2e10, 1.5e7),
    )(me, *a_bufs, series, query_f, key_f)


def attend_kernel(per_step, rows, q_ref, k_ref, v_ref, qf_ref, kf_ref, *refs):
    attn_ref, log_ref = refs[-2:]

    def read(i, part):
        return (q_ref, k_ref, v_ref)[part][i * HEAD_DIM : (i + 1) * HEAD_DIM, :]

    def store(i, lanes, mixed, log):
        attn_ref[i * HEAD_DIM : (i + 1) * HEAD_DIM, lanes] = mixed
        log_ref[i, :, lanes] = log

    heads_forward(per_step, read, qf_ref[0], kf_ref[0], rows, store)


def attend(qkv, attn, logs, query_f, key_f, rows, per_step, first):
    padded = query_f.shape[2]
    heads, feature, log = head_blocks(padded, per_step, first)
    return pl.pallas_call(
        functools.partial(attend_kernel, per_step, rows),
        grid=(logs.shape[0] // per_step - first,),
        in_specs=[heads(0), heads(1), heads(2), feature, feature, ANY, ANY],
        out_specs=[heads(), log],
        out_shape=[jax.ShapeDtypeStruct(attn.shape, half), jax.ShapeDtypeStruct(logs.shape, fp32)],
        input_output_aliases={5: 0, 6: 1},
        compiler_params=params(),
        cost_estimate=cost(1e10, 1e7),
    )(qkv, qkv, qkv, query_f, key_f, attn, logs)


NAMES = ("b3", "g0", "b4", "b5", "g1", "b6")
COLUMNS = {"b3": 99, "g0": 103, "b4": 100, "b5": 101, "g1": 104, "b6": 102}


def fold(value):
    total = value[:, :LANES]
    for s in range(LANES, value.shape[1], LANES):
        total = total + value[:, s : s + LANES]
    return total


def mean(value):
    return jnp.mean(value, axis=0, keepdims=True)


def feed_kernel(n_b, rows, regions, parts, me_ref, *refs):
    b_refs, refs = refs[:n_b], refs[n_b:]
    w1_hbm, turned_hbm, series_hbm, attn_ref, ct_ref, out_ref, gattn_ref, gres_ref, keep_ref, send_ref, small_hbm, *refs = refs
    w1_ref, turned_ref, series_ref, small_ref, *refs = refs
    w_out, w_out_t, w_up, w_up_t, w_down, w_down_t, up_b, col, attn_s, ct_s, *refs = refs
    act_s, slope_s, gdown_s, hid_s, gproj_s, gattn_s, flow, norm_s, lo_s, acc, acc_up, sem_in, sem_w, sem_out, sem_g = refs
    width, units = w_up_t.shape
    chunks = units // CHUNK
    padded = attn_s.shape[1] // regions
    count = len(parts)
    me = me_ref[0]
    lanes = [slice(s, s + n) for s, n in parts]

    loads = [
        (
            pltpu.make_async_copy(attn_ref.at[:, pl.ds(s, n)], attn_s.at[:, pl.ds(s, n)], sem_in.at[2 * i]),
            pltpu.make_async_copy(ct_ref.at[:, pl.ds(s, n)], ct_s.at[:, pl.ds(s, n)], sem_in.at[2 * i + 1]),
        )
        for i, (s, n) in enumerate(parts)
    ]
    short = [
        pltpu.make_async_copy(source, target, sem_w.at[3])
        for source, target in ((w1_hbm, w1_ref), (turned_hbm, turned_ref), (series_hbm, series_ref))
    ]
    for copy in short:
        copy.start()
    loads[0][0].start()
    groups = ([], [], [])
    at = 0
    owner_of = owners(me)
    for ref in b_refs:
        for i in range(ref.shape[0]):
            owner, piece = owner_of[at], ref.at[i]
            groups[0].append(pltpu.make_async_copy(piece.at[:, pl.ds(0, width)], w_out.at[rows_of(owner, 16)], sem_w.at[0]))
            for j in range(4):
                groups[1].append(
                    pltpu.make_async_copy(
                        piece.at[:, pl.ds((1 + j) * width, width)],
                        w_up.at[pl.ds(pl.multiple_of(owner * 64 + j * 16, 16), 16)],
                        sem_w.at[1],
                    )
                )
            groups[2].append(pltpu.make_async_copy(piece.at[:, pl.ds(5 * width, units)], w_down.at[rows_of(owner, 16)], sem_w.at[2]))
            at += 1
    for copy in groups[0]:
        copy.start()

    for copy in short:
        copy.wait()
    for i, name in enumerate(NAMES):
        col[i] = across(w1_ref[:, COLUMNS[name] : COLUMNS[name] + 1])
    for owner in range(PIECES):
        up_b[owner * 64 : owner * 64 + 64, :] = jnp.broadcast_to(
            turned_ref[:64, owner * 16 + 9 : owner * 16 + 10], (64, LANES)
        )

    def wide(value, size):
        return jnp.concatenate([value] * (size // LANES), axis=1)

    def column(r, name):
        return wide(col[NAMES.index(name)], parts[r][1])

    def add_to(r, name, value):
        i = NAMES.index(name)
        acc[i] = fold(value) if r == 0 else acc[i] + fold(value)

    rates = [None] * count
    outs = []

    def leave(source, target):
        copy = pltpu.make_async_copy(source, target, sem_out.at[len(outs)])
        copy.start()
        outs.append(copy)

    def enter(r):
        loads[r][0].wait()
        embed = dot(w1_ref[...], series_ref[:, lanes[r]])
        resid = embed + (dot(w_out[...], attn_s[:, lanes[r]]) + column(r, "b3"))
        center = resid - mean(resid)
        rates[r] = lax.rsqrt(mean(center * center) + norm_eps)
        norm = center * rates[r]
        norm_s[:, lanes[r]] = norm
        hidden = norm * column(r, "g0") + column(r, "b4")
        flow[:, lanes[r]] = hidden
        hid_s[:, lanes[r]] = hidden.astype(half)

    def up(r, c):
        part = slice(c * CHUNK, (c + 1) * CHUNK)
        upper = dot(w_up[part, :], hid_s[:, lanes[r]]) + wide(up_b[part, :], parts[r][1])
        square = upper * upper
        turned = 0.5 + 0.5 * jnp.tanh(upper * (gelu_coef + (gelu_coef * 0.044715) * square))
        act = upper * turned
        slope = turned + act * (1.0 - turned) * (2.0 * gelu_coef + (6.0 * gelu_coef * 0.044715) * square)
        slope_s[part, lanes[r]] = slope.astype(half)
        act_s[part, lanes[r]] = act.astype(half)

    def down(r):
        flow[:, lanes[r]] = flow[:, lanes[r]] + (dot(w_down[...], act_s[:, lanes[r]]) + column(r, "b5"))

    def turn(r):
        resid = flow[:, lanes[r]]
        center = resid - mean(resid)
        rate = lax.rsqrt(mean(center * center) + norm_eps)
        norm = center * rate
        lo_s[lanes[r], :] = (norm * column(r, "g1") + column(r, "b6")).astype(half).T
        loads[r][1].wait()
        grad = ct_s[:, lanes[r]].astype(fp32)
        add_to(r, "b6", grad)
        add_to(r, "g1", grad * norm)
        grad = grad * column(r, "g1")
        grad = rate * (grad - mean(grad) - norm * mean(grad * norm))
        add_to(r, "b5", grad)
        flow[:, lanes[r]] = grad
        gdown_s[:, lanes[r]] = grad.astype(half)

    def up_back(r, c):
        part = slice(c * CHUNK, (c + 1) * CHUNK)
        grad = slope_s[part, lanes[r]].astype(fp32) * dot(w_down_t[part, :], gdown_s[:, lanes[r]])
        acc_up[part, :] = fold(grad) if r == 0 else acc_up[part, :] + fold(grad)
        slope_s[part, lanes[r]] = grad.astype(half)

    def back(r):
        flow[:, lanes[r]] = flow[:, lanes[r]] + dot(w_up_t[...], slope_s[:, lanes[r]])

    def leave_norm(r):
        grad = flow[:, lanes[r]]
        norm = norm_s[:, lanes[r]]
        add_to(r, "b4", grad)
        add_to(r, "g0", grad * norm)
        grad = grad * column(r, "g0")
        grad = rates[r] * (grad - mean(grad) - norm * mean(grad * norm))
        add_to(r, "b3", grad)
        flow[:, lanes[r]] = grad
        low = grad.astype(half)
        gproj_s[:, lanes[r]] = low
        gattn_s[:, lanes[r]] = dot(w_out_t[...], low).astype(half)
        at = pl.ds(*parts[r])
        leave(flow.at[:, at], gres_ref.at[:, at])
        leave(gattn_s.at[:, at], gattn_ref.at[:, at])

    for copy in groups[0]:
        copy.wait()
    for group in groups[1:]:
        for copy in group:
            copy.start()
    for first, second in loads:
        if first is not loads[0][0]:
            first.start()
        second.start()
    enter(0)
    for copy in groups[1]:
        copy.wait()
    for r in range(count):
        up(r, 0)
        if r == 0:
            for copy in groups[2]:
                copy.wait()
            w_out_t[...] = w_out[...].T
            w_down_t[...] = w_down[...].T
            w_up_t[...] = w_up[...].T
        up(r, 1)
        if r + 1 < count:
            enter(r + 1)
        if r > 0:
            turn(r - 1)
        for c in range(2, chunks):
            up(r, c)
        down(r)
    for r in range(count):
        up_back(r, 0)
        up_back(r, 1)
        if r == 0:
            turn(count - 1)
            for region in range(regions):
                leave(lo_s.at[pl.ds(region * padded, rows)], out_ref.at[region])
        else:
            leave_norm(r - 1)
        for c in range(2, chunks):
            up_back(r, c)
        back(r)
    leave_norm(count - 1)
    targets = [(keep_ref if r < PIECES // 2 else send_ref).at[r % (PIECES // 2)] for r in range(PIECES)]
    copies = []

    def give(source, column, size):
        copies.append(pltpu.make_async_copy(source, target.at[:, pl.ds(column, size)], sem_g))
        copies[-1].start()

    w_up[...] = dot(slope_s[...], hid_s[...], 1, 1).astype(half)
    for owner, target in zip(owner_of, targets):
        for j in range(4):
            give(w_up.at[pl.ds(pl.multiple_of(owner * 64 + j * 16, 16), 16)], (1 + j) * width, width)
    w_out[...] = dot(gproj_s[...], attn_s[...], 1, 1).astype(half)
    w_down[...] = dot(gdown_s[...], act_s[...], 1, 1).astype(half)
    for owner, target in zip(owner_of, targets):
        give(w_out.at[rows_of(owner, 16)], 0, width)
        give(w_down.at[rows_of(owner, 16)], 5 * width, units)
    total = jnp.zeros((width, LANES), fp32)
    lane = lax.broadcasted_iota(jnp.int32, (width, LANES), 1)
    for i, name in enumerate(NAMES):
        total = total + jnp.where(lane == COLUMNS[name], jnp.sum(acc[i], axis=1, keepdims=True), 0.0)
    up_sum = jnp.sum(acc_up[...], axis=1, keepdims=True).reshape(PIECES, UP_COLUMNS, 16, 1)
    for c in range(UP_COLUMNS):
        total = total + jnp.where(lane == UP_AT + c, up_sum[:, c].reshape(width, 1), 0.0)
    small_ref[...] = total
    leave(small_ref, small_hbm)
    for copy in copies:
        copy.wait()
    for copy in outs:
        copy.wait()


def feed(me, b_bufs, w1, turned, series, attn, cotangent, regions, rows, units):
    width, tokens = attn.shape
    half_set = jax.ShapeDtypeStruct((PIECES // 2, 16, 5 * width + units), half)
    low_all = pltpu.VMEM((width, tokens), half)
    parts = ((0, tokens // 2 // TILE * TILE), (tokens // 2 // TILE * TILE, tokens - tokens // 2 // TILE * TILE))
    return pl.pallas_call(
        functools.partial(feed_kernel, len(b_bufs), rows, regions, parts),
        in_specs=[SMEM] + [ANY] * len(b_bufs) + [ANY] * 5,
        out_specs=[ANY] * 6,
        out_shape=[
            jax.ShapeDtypeStruct((regions, rows, width), half),
            jax.ShapeDtypeStruct((width, tokens), half),
            jax.ShapeDtypeStruct((width, tokens), fp32),
            half_set,
            half_set,
            jax.ShapeDtypeStruct((width, LANES), fp32),
        ],
        scratch_shapes=[
            pltpu.VMEM(w1.shape, half),
            pltpu.VMEM(turned.shape, fp32),
            pltpu.VMEM(series.shape, half),
            pltpu.VMEM((width, LANES), fp32),
            pltpu.VMEM((width, width), half),
            pltpu.VMEM((width, width), half),
            pltpu.VMEM((units, width), half),
            pltpu.VMEM((width, units), half),
            pltpu.VMEM((width, units), half),
            pltpu.VMEM((units, width), half),
            pltpu.VMEM((units, LANES), fp32),
            pltpu.VMEM((len(NAMES), width, LANES), fp32),
            low_all,
            low_all,
            pltpu.VMEM((units, tokens), half),
            pltpu.VMEM((units, tokens), half),
            low_all,
            low_all,
            low_all,
            low_all,
            pltpu.VMEM((width, tokens), fp32),
            pltpu.VMEM((width, tokens), fp32),
            pltpu.VMEM((tokens, width), half),
            pltpu.VMEM((len(NAMES), width, LANES), fp32),
            pltpu.VMEM((units, LANES), fp32),
            pltpu.SemaphoreType.DMA((2 * len(parts),)),
            pltpu.SemaphoreType.DMA((4,)),
            pltpu.SemaphoreType.DMA((regions + 2 * len(parts) + 1,)),
            pltpu.SemaphoreType.DMA,
        ],
        compiler_params=params(),
        cost_estimate=cost(4e10, 2e7),
    )(me, *b_bufs, w1, turned, series, attn, cotangent)


def heads_back(per_step, rows, refs, store):
    q_ref, k_ref, v_ref, attn_ref, gattn_ref, log_ref, qf_ref, kf_ref = refs
    padded = qf_ref.shape[2]
    query_f, key_f = qf_ref[0], kf_ref[0]
    blocks = [(s, min(TILE, rows - s)) for s in range(0, rows, TILE)]
    filler = jnp.zeros((13, padded), fp32)

    def in_three(row):
        first = row.astype(half).astype(fp32)
        left = row - first
        second = left.astype(half).astype(fp32)
        return jnp.concatenate([first, second, left - second, filler], axis=0).astype(half)

    for i in range(per_step):
        head = slice(i * HEAD_DIM, (i + 1) * HEAD_DIM)
        query, keys, values, grad = q_ref[head, :], k_ref[head, :], v_ref[head, :], gattn_ref[head, :]
        inner = jnp.sum(grad.astype(fp32) * attn_ref[head, :].astype(fp32), axis=0, keepdims=True)
        query_a = jnp.concatenate([query, in_three(-log_ref[i]), query_f[16:]], axis=0).T
        grad_a = jnp.concatenate([grad, in_three(-inner), jnp.zeros((48, padded), half)], axis=0).T
        keys_a = jnp.concatenate([keys, key_f], axis=0)
        values_a = jnp.concatenate([values, key_f], axis=0)
        grad_keys = grad_values = None
        grad_query = []
        for s, n in blocks:
            probs = jnp.exp(dot(query_a[s : s + n], keys_a))
            raw = (probs * dot(grad_a[s : s + n], values_a)).astype(half)
            more_v = dot(grad[:, s : s + n], probs.astype(half))
            more_k = dot(query[:, s : s + n], raw)
            grad_values = more_v if grad_values is None else grad_values + more_v
            grad_keys = more_k if grad_keys is None else grad_keys + more_k
            grad_query.append((dot(keys, raw, 1, 1) * HEAD_DIM**-0.5).astype(half))
        grad_query.append(jnp.zeros((HEAD_DIM, padded - rows), half))
        store(i, (jnp.concatenate(grad_query, axis=1), grad_keys.astype(half), grad_values.astype(half)))


def attend_back_kernel(per_step, rows, *refs):
    grad_ref = refs[8]

    def store(i, three):
        for part, value in enumerate(three):
            grad_ref[0, part, i * HEAD_DIM : (i + 1) * HEAD_DIM, :] = value

    heads_back(per_step, rows, refs[:8], store)


def finish_kernel(per_step, rows, counts, me_ref, *refs):
    ins, done_refs, refs = refs[:8], refs[8 : 8 + len(counts)], refs[8 + len(counts) :]
    first = sum(counts)
    emb_ref, gres_ref, series_ref, wqkv_t_ref, w1_ref, small_ref, keep_ref, send_ref, lbg_hbm, lbg_ref, *refs = refs
    grad_s, emb_s, gres_s, wqkv_t, g_qkv, g_one, sem, sem_out = refs
    step, steps = pl.program_id(0), pl.num_programs(0)
    width, tokens = emb_s.shape
    regions, lags, _ = lbg_ref.shape
    padded = tokens // regions
    groups = HEADS // per_step
    height = per_step * HEAD_DIM
    brought = [
        pltpu.make_async_copy(emb_ref, emb_s, sem),
        pltpu.make_async_copy(gres_ref, gres_s, sem),
        pltpu.make_async_copy(wqkv_t_ref, wqkv_t, sem),
    ]
    done = [ref.at[t] for ref in done_refs for t in range(ref.shape[0])]
    for t in range(first):
        for part in range(3):
            brought.append(
                pltpu.make_async_copy(
                    done[t].at[part],
                    grad_s.at[
                        pl.ds(part * width + (t % groups) * height, height), pl.ds(t // groups * padded, padded)
                    ],
                    sem,
                )
            )

    @pl.when(step == 0)
    def _():
        for copy in brought:
            copy.start()

    now = step + first
    lanes = pl.ds(pl.multiple_of(now // groups * padded, LANES), padded)
    rows_at = lax.rem(now, groups) * height

    def store(i, three):
        for part, value in enumerate(three):
            at = pl.multiple_of(part * width + rows_at + i * HEAD_DIM, HEAD_DIM)
            grad_s[pl.ds(at, HEAD_DIM), lanes] = value

    heads_back(per_step, rows, ins, store)

    @pl.when(step == steps - 1)
    def _():
        for copy in brought:
            copy.wait()
        owner_of = owners(me_ref[0])
        for part in range(3):
            at = slice(part * width, (part + 1) * width)
            g_qkv[at, :] = dot(grad_s[at, :], emb_s[...], 1, 1).astype(half)
        copies = []
        for r, owner in enumerate(owner_of):
            target = (keep_ref if r < PIECES // 2 else send_ref).at[r % (PIECES // 2)]
            for j in range(3):
                copies.append(
                    pltpu.make_async_copy(
                        g_qkv.at[pl.ds(pl.multiple_of(owner * 48 + j * 16, 16), 16)],
                        target.at[:, pl.ds(j * width, width)],
                        sem_out.at[0],
                    )
                )
        for copy in copies:
            copy.start()
        total = small_ref[...]
        lane = lax.broadcasted_iota(jnp.int32, total.shape, 1)
        for i, part in enumerate((0, 2)):
            bias = fold(grad_s[part * width : (part + 1) * width, :].astype(fp32))
            total = total + jnp.where(lane == BIAS_AT + 1 + i, jnp.sum(bias, axis=1, keepdims=True), 0.0)
        low = (gres_s[...] + dot(wqkv_t[...], grad_s[...])).astype(half)
        total = total + dot(low, series_ref[...], 1, 1)
        for r in range(regions):
            lbg_ref[r] = dot(w1_ref[...], low[:, r * padded : (r + 1) * padded], 0, 0)[:lags, :rows]
        lbg_out = pltpu.make_async_copy(lbg_ref, lbg_hbm, sem_out.at[2])
        lbg_out.start()
        g_one[...] = total.astype(half)
        more = []
        for r, owner in enumerate(owner_of):
            target = (keep_ref if r < PIECES // 2 else send_ref).at[r % (PIECES // 2)]
            more.append(
                pltpu.make_async_copy(
                    g_one.at[rows_of(owner, 16)], target.at[:, pl.ds(3 * width, LANES)], sem_out.at[1]
                )
            )
        for copy in more:
            copy.start()
        for copy in copies:
            copy.wait()
        for copy in more:
            copy.wait()
        lbg_out.wait()


def back_operands(qkv, attn, grad_attn, logs, query_f, key_f, per_step, first):
    heads, feature, log = head_blocks(query_f.shape[2], per_step, first)
    specs = [heads(0), heads(1), heads(2), heads(), heads(), log, feature, feature]
    return specs, (qkv, qkv, qkv, attn, grad_attn, logs, query_f, key_f)


def attend_back(qkv, attn, grad_attn, logs, query_f, key_f, rows, per_step, first, steps):
    padded = query_f.shape[2]
    specs, operands = back_operands(qkv, attn, grad_attn, logs, query_f, key_f, per_step, first)
    shape = (3, per_step * HEAD_DIM, padded)
    grad_spec = pl.BlockSpec((1, *shape), lambda t: (t, 0, 0, 0))
    grad_shape = jax.ShapeDtypeStruct((steps, *shape), half)
    return pl.pallas_call(
        functools.partial(attend_back_kernel, per_step, rows),
        grid=(steps,),
        in_specs=specs,
        out_specs=grad_spec,
        out_shape=grad_shape,
        compiler_params=params(56),
        cost_estimate=cost(2e10, 1e7),
    )(*operands)


def finish(me, qkv, attn, grad_attn, logs, query_f, key_f, done, embed_low, grad_resid, series, wqkv_t, w1, small, rows, lags, per_step):
    regions, _, padded = query_f.shape
    width, tokens = attn.shape
    counts = tuple(value.shape[0] for value in done)
    first = sum(counts)
    specs, operands = back_operands(qkv, attn, grad_attn, logs, query_f, key_f, per_step, first)
    half_set = jax.ShapeDtypeStruct((PIECES // 2, 16, 3 * width + LANES), half)
    return pl.pallas_call(
        functools.partial(finish_kernel, per_step, rows, counts),
        grid=(logs.shape[0] // per_step - first,),
        in_specs=[SMEM] + specs + [ANY] * len(done) + [ANY, ANY, VMEM, ANY, VMEM, VMEM],
        out_specs=[ANY, ANY, ANY],
        out_shape=[half_set, half_set, jax.ShapeDtypeStruct((regions, lags, rows), fp32)],
        scratch_shapes=[
            pltpu.VMEM((regions, lags, rows), fp32),
            pltpu.VMEM((3 * width, tokens), half),
            pltpu.VMEM((width, tokens), half),
            pltpu.VMEM((width, tokens), fp32),
            pltpu.VMEM((width, 3 * width), half),
            pltpu.VMEM((3 * width, width), half),
            pltpu.VMEM((width, LANES), half),
            pltpu.SemaphoreType.DMA,
            pltpu.SemaphoreType.DMA((3,)),
        ],
        compiler_params=params(57),
        cost_estimate=cost(4e10, 2e7),
    )(me, *operands, *done, embed_low, grad_resid, series, wqkv_t, w1, small)


def send(value, offset):
    return lax.ppermute(value, AXES, [(i, i ^ offset) for i in range(PIECES)])


def after(value, *others):
    return lax.optimization_barrier((value, *others))[0]


def along_z(piece):
    return jnp.stack([piece] + [send(piece, 2 * s) for s in range(1, 4)])


def along_plane(value):
    return [value] + [send(value, offset) for offset in (1, 16, 17)]


def along_core(plane):
    return plane + [send(part, 8) for part in plane]


def add(*terms):
    return sum(term.astype(fp32) for term in terms)


def quarters(low):
    return [low[4 * i : 4 * i + 4] for i in range(4)]


def add_core(keep, got):
    return [add(*pair).astype(half) for pair in zip(quarters(keep), quarters(got))]


def sum_plane(lows):
    return [lows[0]] + [send(low, offset) for low, offset in zip(lows[1:], (1, 16, 17))]


def add_plane(parts):
    return [add(*[part[s] for part in parts]).astype(half) for s in range(4)]


def sum_z(lows):
    return [lows[0]] + [send(lows[s], 2 * s) for s in range(1, 4)]


def stacked(value, width):
    return jnp.concatenate([value[:, s : s + width] for s in range(0, value.shape[1], width)], axis=0)


def unpack_one(packed, lags):
    up = packed[:, UP_AT : UP_AT + UP_COLUMNS].reshape(-1, 16, UP_COLUMNS).transpose(0, 2, 1).reshape(-1)
    return packed[:, :lags], packed[:, BIAS_AT:GAIN_AT].T, packed[:, GAIN_AT:UP_AT].T, up


def body(
    ours,
    lookback,
    bucket_size,
    variate_mask,
    w_embed,
    w_qkv,
    w_out,
    w_up,
    w_down,
    up_bias,
    biases,
    gains,
    cotangent,
):
    regions, rows, lags = lookback.shape
    width = w_qkv.shape[1]
    units = w_down.shape[1]
    padded = -(-rows // LANES) * LANES
    per_step = 4
    steps = regions * HEADS // per_step
    per_step_f = 2
    steps_f = regions * HEADS // per_step_f
    lookback_t = lookback.transpose(0, 2, 1)
    series, masked, query_f, key_f = prepare(bucket_size, variate_mask, lookback_t, cotangent, padded, 32)

    if ours:
        index = lax.axis_index(AXES).astype(jnp.int32)
        piece_a, piece_b = pack(w_embed, w_qkv, w_out, w_up, w_down, up_bias, biases, gains)
        z_a = after(along_z(piece_a), series)
        z_b = along_z(piece_b)
        plane_a = along_plane(z_a)
        plane_b = along_plane(after(z_b, z_a))
        a_bufs = along_core(plane_a)
    else:
        index = jnp.zeros((), jnp.int32)

        def whole(value, axis=0):
            return lax.all_gather(value, AXES, axis=axis, tiled=True)

        def cut(value, axis=0):
            shape = value.shape[:axis] + (PIECES, value.shape[axis] // PIECES) + value.shape[axis + 1 :]
            return jnp.moveaxis(value.reshape(shape), axis, 0)

        early = jnp.array(OFFSETS)
        short = jax.vmap(short_block)(cut(whole(biases, 1), 1), cut(whole(gains, 1), 1), cut(whole(up_bias)))
        a_bufs = [jax.vmap(first_piece)(cut(whole(w_embed)), short, cut(whole(w_qkv)))[early]]
        b_bufs = [jax.vmap(second_piece)(cut(whole(w_out)), cut(whole(w_up)), cut(whole(w_down)))[early]]
    me = index.reshape(1)

    qkv, embed_low, attn, logs, w1, turned, wqkv_t = project(
        me, a_bufs, series, query_f, key_f, rows, width, per_step_f, steps_f - 1
    )
    if ours:
        b_bufs = along_core(plane_b[:1]) + along_core([after(part, logs) for part in plane_b[1:]])
        b_bufs = [b_bufs[0], *b_bufs[2:5], b_bufs[1], *b_bufs[5:]]
    attn, logs = attend(qkv, attn, logs, query_f, key_f, rows, per_step_f, steps_f - 1)
    layer_out, grad_attn, grad_resid, keep_b, send_b, sums = feed(
        me, b_bufs, w1, turned, series, attn, masked, regions, rows, units
    )
    if ours:
        core_b = send(send_b, 8)
    done = [attend_back(qkv, attn, grad_attn, logs, query_f, key_f, rows, per_step, 0, steps - 2)]
    if ours:
        lows_b = add_core(keep_b, after(core_b, *done))
        parts_b = sum_plane(lows_b)
        grad_attn = after(grad_attn, *lows_b)
    keep_a, send_a, lookback_grad = finish(
        me, qkv, attn, grad_attn, logs, query_f, key_f, done, embed_low, grad_resid, series, wqkv_t, w1, sums, rows, lags, per_step
    )
    lookback_grad = lookback_grad.transpose(0, 2, 1)

    def parts_of(grad_a, grad_b):
        w_qkv_part = stacked(grad_a[:, : 3 * width], width)
        return w_qkv_part, grad_a[:, 3 * width :], grad_b[:, :width], stacked(grad_b[:, width : 5 * width], width), grad_b[:, 5 * width :]

    if ours:
        core_a = send(send_a, 8)
        parts_b = sum_z(add_plane([after(part, keep_a) for part in parts_b]))
        lows_a = add_core(keep_a, after(core_a, parts_b[0]))
        lows_a = add_plane(sum_plane(lows_a))
        grad_out, grad_up, grad_down = unpack_second([after(part, *lows_a) for part in parts_b], width, units)
        parts_a = sum_z(lows_a)
        grad_qkv, grad_embed, grad_up_bias, grad_biases, grad_gains = unpack_first(parts_a, width, lags)
    else:
        def shared(value, axis=0):
            return lax.psum_scatter(value, AXES, scatter_dimension=axis, tiled=True)

        order = jnp.argsort(jnp.array(OFFSETS, jnp.int32))
        grad_a = jnp.concatenate([keep_a, send_a], axis=0).astype(fp32)[order]
        grad_b = jnp.concatenate([keep_b, send_b], axis=0).astype(fp32)[order]
        whole_parts = [value.reshape(-1, value.shape[-1]) for value in jax.vmap(parts_of)(grad_a, grad_b)]
        grad_embed, grad_biases, grad_gains, grad_up_bias = unpack_one(whole_parts[1], lags)
        grad_qkv, grad_out, grad_up, grad_down = (shared(whole_parts[i]) for i in (0, 2, 3, 4))
        grad_embed, grad_up_bias = shared(grad_embed), shared(grad_up_bias)
        grad_biases, grad_gains = shared(grad_biases, 1), shared(grad_gains, 1)
    return (
        layer_out,
        lookback_grad,
        grad_embed,
        grad_qkv,
        grad_out,
        grad_up,
        grad_down,
        grad_up_bias,
        grad_biases,
        grad_gains,
    )


def solution(mesh):
    one = P(AXES)
    rows = P(AXES, None)
    blocks = P(AXES, None, None)
    columns = P(None, AXES)
    in_specs = (blocks, one, rows, rows, rows, rows, rows, rows, one, columns, columns, blocks)
    out_specs = (blocks, blocks, rows, rows, rows, rows, rows, one, columns, columns)
    ours = tuple(mesh.shape[axis] for axis in AXES) == (4, 8)
    return jax.shard_map(
        functools.partial(body, ours), mesh=mesh, in_specs=in_specs, out_specs=out_specs, check_vma=False
    )
```

```python
import functools

import jax
import jax.numpy as jnp
from jax import lax
from jax.experimental import pallas as pl
from jax.experimental.pallas import tpu as pltpu
from jax.sharding import PartitionSpec as P

HEADS = 8
HEAD_DIM = 64
PIECES = 32
LANES = 128
TILE = 256
CHUNK = 512
SPAN = 512
AXES = ("dp", "fsdp")

norm_eps = 1e-05
masked_score = -1e30
gelu_coef = 0.7978845608028654

half = jnp.bfloat16
fp32 = jnp.float32

OFFSETS = tuple(
    core * 8 + x * 16 + y + z * 2
    for core in range(2)
    for x in range(2)
    for y in range(2)
    for z in range(4)
)

BIAS_AT = 96
GAIN_AT = 103
UP_AT = 105
UP_COLUMNS = 4


def dot(left, right, left_dim=1, right_dim=0):
    return lax.dot_general(
        left, right, (((left_dim,), (right_dim,)), ((), ())), preferred_element_type=fp32
    )


def params(mebibytes=62):
    return pltpu.CompilerParams(vmem_limit_bytes=mebibytes * 2**20)


def cost(flops, moved):
    return pl.CostEstimate(flops=int(flops), bytes_accessed=int(moved), transcendentals=0)


VMEM = pl.BlockSpec(memory_space=pltpu.VMEM)
SMEM = pl.BlockSpec(memory_space=pltpu.SMEM)
ANY = pl.BlockSpec(memory_space=pl.ANY)


def piece_copies(me, refs, sem, place):
    copies = []
    at = 0
    for ref in refs:
        for i in range(ref.shape[0]):
            owner = jnp.bitwise_xor(me, OFFSETS[at])
            for source, target in place(ref.at[i], owner):
                copies.append(pltpu.make_async_copy(source, target, sem))
            at += 1
    return copies


def rows_of(owner, count):
    return pl.ds(pl.multiple_of(owner * count, 16), count)


def owners(me):
    return [jnp.bitwise_xor(me, offset) for offset in OFFSETS]


def across(column, lanes=LANES):
    return jnp.broadcast_to(column.astype(fp32), (column.shape[0], lanes))


def prepare_kernel(small, bucket_ref, mask_ref, lb_ref, ct_ref, series_ref, masked_ref, qf_ref, kf_ref):
    regions, rows = mask_ref.shape
    padded = qf_ref.shape[2]
    lags, width = lb_ref.shape[1], ct_ref.shape[2]
    last = rows // small - 1
    spare = padded - rows
    number = lax.broadcasted_iota(jnp.int32, (HEAD_DIM, padded), 0) - 16
    place = lax.broadcasted_iota(jnp.int32, (HEAD_DIM, padded), 1)
    counted = (number >= 0) & (number <= last)
    below = lax.broadcasted_iota(jnp.int32, (LANES - lags, padded), 0)
    for r in range(regions):
        lanes = slice(r * padded, (r + 1) * padded)
        valid = jnp.concatenate([mask_ref[r : r + 1, :].astype(fp32), jnp.zeros((1, spare), fp32)], axis=1)
        turned = jnp.concatenate([ct_ref[r].T, jnp.zeros((width, spare), half)], axis=1)
        masked_ref[:, lanes] = (turned.astype(fp32) * valid).astype(half)
        values = jnp.concatenate([lb_ref[r], jnp.zeros((lags, spare), half)], axis=1)
        series_ref[:lags, lanes] = values
        series_ref[lags:, lanes] = jnp.where(below == 0, 1.0, 0.0).astype(half)
        bucket = bucket_ref[r]
        window = jnp.floor((place.astype(fp32) + 0.5) / bucket.astype(fp32)).astype(jnp.int32)
        window = jnp.minimum(window, last)
        qf_ref[r] = (
            jnp.where(counted & (window != number), masked_score, 0.0) + jnp.where(number == last + 1, 1.0, 0.0)
        ).astype(half)
        kf_ref[r] = (
            jnp.where(counted & (window == number), 1.0, 0.0)
            + jnp.where((number >= -16) & (number < -13), 1.0, 0.0)
            + jnp.where(number == last + 1, jnp.where(valid > 0, 0.0, masked_score), 0.0)
        ).astype(half)


def prepare(bucket_size, variate_mask, lookback_t, cotangent, padded, small):
    regions, rows, width = cotangent.shape
    tokens = regions * padded
    feature = jax.ShapeDtypeStruct((regions, HEAD_DIM, padded), half)
    return pl.pallas_call(
        functools.partial(prepare_kernel, small),
        in_specs=[SMEM, VMEM, VMEM, VMEM],
        out_specs=[VMEM] * 4,
        out_shape=[
            jax.ShapeDtypeStruct((LANES, tokens), half),
            jax.ShapeDtypeStruct((width, tokens), half),
            feature,
            feature,
        ],
        compiler_params=params(),
        cost_estimate=cost(1e7, 8e6),
    )(bucket_size, variate_mask, lookback_t, cotangent)


def short_block(biases, gains, up_bias):
    width = biases.shape[1]
    up_bias = up_bias.reshape(1, -1)
    return jnp.concatenate(
        [
            jnp.concatenate([biases, jnp.zeros((7, LANES - width), biases.dtype)], axis=1),
            jnp.concatenate([gains, jnp.zeros((2, LANES - width), biases.dtype)], axis=1),
            jnp.concatenate([up_bias, jnp.zeros((1, LANES - up_bias.shape[1]), biases.dtype)], axis=1),
            jnp.zeros((6, LANES), biases.dtype),
        ],
        axis=0,
    )


def side_by_side(value):
    return [value[s : s + 16] for s in range(0, value.shape[0], 16)]


def first_piece(w_embed, short, w_qkv):
    spare = jnp.zeros((w_embed.shape[0], LANES - w_embed.shape[1]), half)
    return jnp.concatenate([*side_by_side(w_qkv), w_embed, spare, short], axis=1)


def second_piece(w_out, w_up, w_down):
    return jnp.concatenate([w_out, *side_by_side(w_up), w_down], axis=1)


def pack_kernel(embed_ref, qkv_ref, out_ref, up_ref, down_ref, up_bias_ref, bias_ref, gain_ref, first_ref, second_ref):
    width = qkv_ref.shape[1]
    for j in range(3):
        first_ref[:, j * width : (j + 1) * width] = qkv_ref[j * 16 : (j + 1) * 16, :]
    spare = jnp.zeros((16, LANES - embed_ref.shape[1]), half)
    first_ref[:, 3 * width : 3 * width + LANES] = jnp.concatenate([embed_ref[...], spare], axis=1)
    short = short_block(bias_ref[...].astype(fp32), gain_ref[...].astype(fp32), up_bias_ref[...].astype(fp32))
    first_ref[:, 3 * width + LANES :] = short.astype(half)
    second_ref[:, :width] = out_ref[...]
    for j in range(4):
        second_ref[:, (1 + j) * width : (2 + j) * width] = up_ref[j * 16 : (j + 1) * 16, :]
    second_ref[:, 5 * width :] = down_ref[...]


def pack(w_embed, w_qkv, w_out, w_up, w_down, up_bias, biases, gains):
    width, units = w_out.shape[1], w_down.shape[1]
    return pl.pallas_call(
        pack_kernel,
        in_specs=[VMEM] * 8,
        out_specs=[VMEM] * 2,
        out_shape=[
            jax.ShapeDtypeStruct((16, 3 * width + 2 * LANES), half),
            jax.ShapeDtypeStruct((16, 5 * width + units), half),
        ],
    )(w_embed, w_qkv, w_out, w_up, w_down, up_bias.reshape(1, -1), biases, gains)


def brought(refs, places, sem):
    copies = [pltpu.make_async_copy(ref, place, sem.at[i]) for i, (ref, place) in enumerate(zip(refs, places))]
    for copy in copies:
        copy.start()
    for copy in copies:
        copy.wait()
    return lambda columns: sum(place[:, columns].astype(fp32) for place in places)


def unpack_first_kernel(*refs):
    parts, (qkv_ref, embed_ref, up_ref, bias_ref, gain_ref), places, sem = refs[:4], refs[4:9], refs[9:13], refs[13]
    total = brought(parts, places, sem)(slice(None))
    width = qkv_ref.shape[1]
    for j in range(3):
        qkv_ref[j * 16 : (j + 1) * 16, :] = total[:, j * width : (j + 1) * width]
    rest = total[:, 3 * width :]
    embed_ref[...] = rest[:, : embed_ref.shape[1]]
    turned = rest.T
    bias_ref[...] = turned[BIAS_AT:GAIN_AT, :]
    gain_ref[...] = turned[GAIN_AT:UP_AT, :]
    up_ref[...] = jnp.concatenate([turned[UP_AT + c : UP_AT + c + 1, :] for c in range(UP_COLUMNS)], axis=1)


def unpack_first(parts, width, lags):
    qkv, embed, up, bias, gain = pl.pallas_call(
        unpack_first_kernel,
        in_specs=[ANY] * 4,
        out_specs=[VMEM] * 5,
        out_shape=[
            jax.ShapeDtypeStruct((48, width), fp32),
            jax.ShapeDtypeStruct((16, lags), fp32),
            jax.ShapeDtypeStruct((1, 16 * UP_COLUMNS), fp32),
            jax.ShapeDtypeStruct((7, 16), fp32),
            jax.ShapeDtypeStruct((2, 16), fp32),
        ],
        scratch_shapes=[pltpu.VMEM(part.shape, half) for part in parts] + [pltpu.SemaphoreType.DMA((4,))],
    )(*parts)
    return qkv, embed, up.reshape(-1), bias, gain


def unpack_second_kernel(*refs):
    parts, (out_ref, up_ref, down_ref), places, sem = refs[:4], refs[4:7], refs[7:11], refs[11]
    width = out_ref.shape[1]
    total = brought(parts, places, sem)
    out_ref[...] = total(slice(0, width))
    for j in range(4):
        up_ref[j * 16 : (j + 1) * 16, :] = total(slice((1 + j) * width, (2 + j) * width))
    down_ref[...] = total(slice(5 * width, None))


def unpack_second(parts, width, units):
    return pl.pallas_call(
        unpack_second_kernel,
        in_specs=[ANY] * 4,
        out_specs=[VMEM] * 3,
        out_shape=[
            jax.ShapeDtypeStruct((16, width), fp32),
            jax.ShapeDtypeStruct((64, width), fp32),
            jax.ShapeDtypeStruct((16, units), fp32),
        ],
        scratch_shapes=[pltpu.VMEM(part.shape, half) for part in parts] + [pltpu.SemaphoreType.DMA((4,))],
    )(*parts)


def build_first(raw, w1):
    turned = raw[:, LANES:].astype(fp32).T
    for owner in range(PIECES):
        at = slice(owner * 16, owner * 16 + 16)
        short = turned[:16, at]
        w1[at, :] = jnp.concatenate(
            [raw[at, :BIAS_AT].astype(fp32), short[:, :9], jnp.zeros((16, LANES - BIAS_AT - 9), fp32)], axis=1
        ).astype(half)
    return turned


def scores_of(query, keys, query_f, key_f, rows):
    padded = query_f.shape[1]
    keys_t = jnp.concatenate([keys, key_f], axis=0).T[:rows]
    query_a = jnp.concatenate([query, query_f], axis=0)
    return [dot(keys_t, query_a[:, s : min(s + TILE, padded)]) for s in range(0, padded, TILE)]


def mix(scores, values, rows, store):
    values_a = jnp.concatenate([values[:, :rows], jnp.ones((16, rows), half)], axis=0)
    for i, score in enumerate(scores):
        top = jnp.max(score, axis=0, keepdims=True)
        expo = jnp.exp(score - top).astype(half)
        mixed = dot(values_a, expo)
        total = mixed[HEAD_DIM : HEAD_DIM + 1]
        lanes = slice(i * TILE, i * TILE + score.shape[1])
        store(lanes, (mixed[:HEAD_DIM] * (1.0 / total)).astype(half), top + jnp.log(total))


def heads_forward(count, read, query_f, key_f, rows, store):
    ahead = scores_of(read(0, 0), read(0, 1), query_f, key_f, rows)
    for i in range(count):
        scores = ahead
        if i + 1 < count:
            ahead = scores_of(read(i + 1, 0), read(i + 1, 1), query_f, key_f, rows)
        mix(scores, read(i, 2), rows, functools.partial(store, i))


def project_kernel(n_a, per_step, rows, regions, me_ref, *refs):
    a_refs, refs = refs[:n_a], refs[n_a:]
    series_ref, qf_ref, kf_ref, qkv_ref, emb_ref, attn_ref, log_ref, w1, turned_ref, wqkv_t, *refs = refs
    raw, wqkv, qkv_s, emb_s, sem, sem_out = refs
    step, steps = pl.program_id(0), pl.num_programs(0)
    padded = qf_ref.shape[2]
    width = emb_s.shape[0]
    outs = [
        pltpu.make_async_copy(qkv_s, qkv_ref, sem_out.at[0]),
        pltpu.make_async_copy(emb_s, emb_ref, sem_out.at[1]),
    ]

    @pl.when(step == 0)
    def _():
        def place(piece, owner):
            return [
                (piece.at[:, pl.ds(j * width, width)], wqkv.at[pl.ds(pl.multiple_of(owner * 48 + j * 16, 16), 16)])
                for j in range(3)
            ] + [(piece.at[:, pl.ds(3 * width, 2 * LANES)], raw.at[rows_of(owner, 16)])]

        copies = piece_copies(me_ref[0], a_refs, sem, place)
        for copy in copies:
            copy.start()
        for copy in copies:
            copy.wait()
        turned_ref[...] = build_first(raw, w1)
        bias_q = across(w1[:, BIAS_AT + 1 : BIAS_AT + 2], padded)
        bias_v = across(w1[:, BIAS_AT + 2 : BIAS_AT + 3], padded)
        for r in range(regions):
            lanes = slice(r * padded, (r + 1) * padded)
            low = dot(w1[...], series_ref[:, lanes]).astype(half)
            emb_s[:, lanes] = low
            for part in range(3):
                value = dot(wqkv[part * width : (part + 1) * width], low)
                if part == 0:
                    value = (value + bias_q) * HEAD_DIM**-0.5
                elif part == 2:
                    value = value + bias_v
                qkv_s[part * width : (part + 1) * width, lanes] = value.astype(half)
        for copy in outs:
            copy.start()
        wqkv_t[...] = wqkv[...].T

    region = step // (HEADS // per_step)
    first = lax.rem(step, HEADS // per_step) * per_step
    lanes = pl.ds(pl.multiple_of(region * padded, LANES), padded)

    def read(i, part):
        at = pl.multiple_of((first + i) * HEAD_DIM, HEAD_DIM)
        return qkv_s[pl.ds(part * width + at, HEAD_DIM), lanes]

    def store(i, lanes, mixed, log):
        attn_ref[i * HEAD_DIM : (i + 1) * HEAD_DIM, lanes] = mixed
        log_ref[i, :, lanes] = log

    heads_forward(per_step, read, qf_ref[0], kf_ref[0], rows, store)

    @pl.when(step == steps - 1)
    def _():
        for copy in outs:
            copy.wait()


def head_blocks(padded, per_step, first=0):
    groups = HEADS // per_step

    def heads(part=0):
        return pl.BlockSpec(
            (per_step * HEAD_DIM, padded), lambda t: (part * groups + (t + first) % groups, (t + first) // groups)
        )

    feature = pl.BlockSpec((1, HEAD_DIM, padded), lambda t: ((t + first) // groups, 0, 0))
    log = pl.BlockSpec((per_step, 1, padded), lambda t: (t + first, 0, 0))
    return heads, feature, log


def project(me, a_bufs, series, query_f, key_f, rows, width, per_step, steps):
    regions, _, padded = query_f.shape
    tokens = regions * padded
    heads, feature, log = head_blocks(padded, per_step)
    return pl.pallas_call(
        functools.partial(project_kernel, len(a_bufs), per_step, rows, regions),
        grid=(steps,),
        in_specs=[SMEM] + [ANY] * len(a_bufs) + [VMEM, feature, feature],
        out_specs=[ANY, ANY, heads(), log, VMEM, VMEM, VMEM],
        out_shape=[
            jax.ShapeDtypeStruct((3 * width, tokens), half),
            jax.ShapeDtypeStruct((width, tokens), half),
            jax.ShapeDtypeStruct((width, tokens), half),
            jax.ShapeDtypeStruct((regions * HEADS, 1, padded), fp32),
            jax.ShapeDtypeStruct((width, LANES), half),
            jax.ShapeDtypeStruct((LANES, width), fp32),
            jax.ShapeDtypeStruct((width, 3 * width), half),
        ],
        scratch_shapes=[
            pltpu.VMEM((width, 2 * LANES), half),
            pltpu.VMEM((3 * width, width), half),
            pltpu.VMEM((3 * width, tokens), half),
            pltpu.VMEM((width, tokens), half),
            pltpu.SemaphoreType.DMA,
            pltpu.SemaphoreType.DMA((2,)),
        ],
        compiler_params=params(),
        cost_estimate=cost(2e10, 1.5e7),
    )(me, *a_bufs, series, query_f, key_f)


def attend_kernel(per_step, rows, q_ref, k_ref, v_ref, qf_ref, kf_ref, *refs):
    attn_ref, log_ref = refs[-2:]

    def read(i, part):
        return (q_ref, k_ref, v_ref)[part][i * HEAD_DIM : (i + 1) * HEAD_DIM, :]

    def store(i, lanes, mixed, log):
        attn_ref[i * HEAD_DIM : (i + 1) * HEAD_DIM, lanes] = mixed
        log_ref[i, :, lanes] = log

    heads_forward(per_step, read, qf_ref[0], kf_ref[0], rows, store)


def attend(qkv, attn, logs, query_f, key_f, rows, per_step, first):
    padded = query_f.shape[2]
    heads, feature, log = head_blocks(padded, per_step, first)
    return pl.pallas_call(
        functools.partial(attend_kernel, per_step, rows),
        grid=(logs.shape[0] // per_step - first,),
        in_specs=[heads(0), heads(1), heads(2), feature, feature, ANY, ANY],
        out_specs=[heads(), log],
        out_shape=[jax.ShapeDtypeStruct(attn.shape, half), jax.ShapeDtypeStruct(logs.shape, fp32)],
        input_output_aliases={5: 0, 6: 1},
        compiler_params=params(),
        cost_estimate=cost(1e10, 1e7),
    )(qkv, qkv, qkv, query_f, key_f, attn, logs)


NAMES = ("b3", "g0", "b4", "b5", "g1", "b6")
COLUMNS = {"b3": 99, "g0": 103, "b4": 100, "b5": 101, "g1": 104, "b6": 102}


def fold(value):
    total = value[:, :LANES]
    for s in range(LANES, value.shape[1], LANES):
        total = total + value[:, s : s + LANES]
    return total


def mean(value):
    return jnp.mean(value, axis=0, keepdims=True)


def feed_kernel(n_b, rows, regions, parts, me_ref, *refs):
    b_refs, refs = refs[:n_b], refs[n_b:]
    w1_hbm, turned_hbm, series_hbm, attn_ref, ct_ref, out_ref, gattn_ref, gres_ref, keep_ref, send_ref, small_hbm, *refs = refs
    w1_ref, turned_ref, series_ref, small_ref, *refs = refs
    w_out, w_out_t, w_up, w_up_t, w_down, w_down_t, up_b, col, attn_s, ct_s, *refs = refs
    act_s, slope_s, gdown_s, hid_s, gproj_s, gattn_s, flow, norm_s, lo_s, acc, acc_up, sem_in, sem_w, sem_out, sem_g = refs
    width, units = w_up_t.shape
    chunks = units // CHUNK
    padded = attn_s.shape[1] // regions
    count = len(parts)
    me = me_ref[0]
    lanes = [slice(s, s + n) for s, n in parts]

    loads = [
        (
            pltpu.make_async_copy(attn_ref.at[:, pl.ds(s, n)], attn_s.at[:, pl.ds(s, n)], sem_in.at[2 * i]),
            pltpu.make_async_copy(ct_ref.at[:, pl.ds(s, n)], ct_s.at[:, pl.ds(s, n)], sem_in.at[2 * i + 1]),
        )
        for i, (s, n) in enumerate(parts)
    ]
    short = [
        pltpu.make_async_copy(source, target, sem_w.at[3])
        for source, target in ((w1_hbm, w1_ref), (turned_hbm, turned_ref), (series_hbm, series_ref))
    ]
    for copy in short:
        copy.start()
    loads[0][0].start()
    groups = ([], [], [])
    at = 0
    owner_of = owners(me)
    for ref in b_refs:
        for i in range(ref.shape[0]):
            owner, piece = owner_of[at], ref.at[i]
            groups[0].append(pltpu.make_async_copy(piece.at[:, pl.ds(0, width)], w_out.at[rows_of(owner, 16)], sem_w.at[0]))
            for j in range(4):
                groups[1].append(
                    pltpu.make_async_copy(
                        piece.at[:, pl.ds((1 + j) * width, width)],
                        w_up.at[pl.ds(pl.multiple_of(owner * 64 + j * 16, 16), 16)],
                        sem_w.at[1],
                    )
                )
            groups[2].append(pltpu.make_async_copy(piece.at[:, pl.ds(5 * width, units)], w_down.at[rows_of(owner, 16)], sem_w.at[2]))
            at += 1
    for copy in groups[0]:
        copy.start()

    for copy in short:
        copy.wait()
    for i, name in enumerate(NAMES):
        col[i] = across(w1_ref[:, COLUMNS[name] : COLUMNS[name] + 1])
    for owner in range(PIECES):
        up_b[owner * 64 : owner * 64 + 64, :] = jnp.broadcast_to(
            turned_ref[:64, owner * 16 + 9 : owner * 16 + 10], (64, LANES)
        )

    def wide(value, size):
        return jnp.concatenate([value] * (size // LANES), axis=1)

    def column(r, name):
        return wide(col[NAMES.index(name)], parts[r][1])

    def add_to(r, name, value):
        i = NAMES.index(name)
        acc[i] = fold(value) if r == 0 else acc[i] + fold(value)

    rates = [None] * count
    outs = []

    def leave(source, target):
        copy = pltpu.make_async_copy(source, target, sem_out.at[len(outs)])
        copy.start()
        outs.append(copy)

    def enter(r):
        loads[r][0].wait()
        embed = dot(w1_ref[...], series_ref[:, lanes[r]])
        resid = embed + (dot(w_out[...], attn_s[:, lanes[r]]) + column(r, "b3"))
        center = resid - mean(resid)
        rates[r] = lax.rsqrt(mean(center * center) + norm_eps)
        norm = center * rates[r]
        norm_s[:, lanes[r]] = norm
        hidden = norm * column(r, "g0") + column(r, "b4")
        flow[:, lanes[r]] = hidden
        hid_s[:, lanes[r]] = hidden.astype(half)

    def up(r, c):
        part = slice(c * CHUNK, (c + 1) * CHUNK)
        upper = dot(w_up[part, :], hid_s[:, lanes[r]]) + wide(up_b[part, :], parts[r][1])
        square = upper * upper
        turned = 0.5 + 0.5 * jnp.tanh(upper * (gelu_coef + (gelu_coef * 0.044715) * square))
        act = upper * turned
        slope = turned + act * (1.0 - turned) * (2.0 * gelu_coef + (6.0 * gelu_coef * 0.044715) * square)
        slope_s[part, lanes[r]] = slope.astype(half)
        act_s[part, lanes[r]] = act.astype(half)

    def down(r):
        flow[:, lanes[r]] = flow[:, lanes[r]] + (dot(w_down[...], act_s[:, lanes[r]]) + column(r, "b5"))

    def turn(r):
        resid = flow[:, lanes[r]]
        center = resid - mean(resid)
        rate = lax.rsqrt(mean(center * center) + norm_eps)
        norm = center * rate
        lo_s[lanes[r], :] = (norm * column(r, "g1") + column(r, "b6")).astype(half).T
        loads[r][1].wait()
        grad = ct_s[:, lanes[r]].astype(fp32)
        add_to(r, "b6", grad)
        add_to(r, "g1", grad * norm)
        grad = grad * column(r, "g1")
        grad = rate * (grad - mean(grad) - norm * mean(grad * norm))
        add_to(r, "b5", grad)
        flow[:, lanes[r]] = grad
        gdown_s[:, lanes[r]] = grad.astype(half)

    def up_back(r, c):
        part = slice(c * CHUNK, (c + 1) * CHUNK)
        grad = slope_s[part, lanes[r]].astype(fp32) * dot(w_down_t[part, :], gdown_s[:, lanes[r]])
        acc_up[part, :] = fold(grad) if r == 0 else acc_up[part, :] + fold(grad)
        slope_s[part, lanes[r]] = grad.astype(half)

    def back(r):
        flow[:, lanes[r]] = flow[:, lanes[r]] + dot(w_up_t[...], slope_s[:, lanes[r]])

    def leave_norm(r):
        grad = flow[:, lanes[r]]
        norm = norm_s[:, lanes[r]]
        add_to(r, "b4", grad)
        add_to(r, "g0", grad * norm)
        grad = grad * column(r, "g0")
        grad = rates[r] * (grad - mean(grad) - norm * mean(grad * norm))
        add_to(r, "b3", grad)
        flow[:, lanes[r]] = grad
        low = grad.astype(half)
        gproj_s[:, lanes[r]] = low
        gattn_s[:, lanes[r]] = dot(w_out_t[...], low).astype(half)
        at = pl.ds(*parts[r])
        leave(flow.at[:, at], gres_ref.at[:, at])
        leave(gattn_s.at[:, at], gattn_ref.at[:, at])

    for copy in groups[0]:
        copy.wait()
    for group in groups[1:]:
        for copy in group:
            copy.start()
    for first, second in loads:
        if first is not loads[0][0]:
            first.start()
        second.start()
    enter(0)
    for copy in groups[1]:
        copy.wait()
    for r in range(count):
        up(r, 0)
        if r == 0:
            for copy in groups[2]:
                copy.wait()
            w_out_t[...] = w_out[...].T
            w_down_t[...] = w_down[...].T
            w_up_t[...] = w_up[...].T
        up(r, 1)
        if r + 1 < count:
            enter(r + 1)
        if r > 0:
            turn(r - 1)
        for c in range(2, chunks):
            up(r, c)
        down(r)
    for r in range(count):
        up_back(r, 0)
        up_back(r, 1)
        if r == 0:
            turn(count - 1)
            for region in range(regions):
                leave(lo_s.at[pl.ds(region * padded, rows)], out_ref.at[region])
        else:
            leave_norm(r - 1)
        for c in range(2, chunks):
            up_back(r, c)
        back(r)
    leave_norm(count - 1)
    targets = [(keep_ref if r < PIECES // 2 else send_ref).at[r % (PIECES // 2)] for r in range(PIECES)]
    copies = []

    def give(source, column, size):
        copies.append(pltpu.make_async_copy(source, target.at[:, pl.ds(column, size)], sem_g))
        copies[-1].start()

    w_up[...] = dot(slope_s[...], hid_s[...], 1, 1).astype(half)
    for owner, target in zip(owner_of, targets):
        for j in range(4):
            give(w_up.at[pl.ds(pl.multiple_of(owner * 64 + j * 16, 16), 16)], (1 + j) * width, width)
    w_out[...] = dot(gproj_s[...], attn_s[...], 1, 1).astype(half)
    w_down[...] = dot(gdown_s[...], act_s[...], 1, 1).astype(half)
    for owner, target in zip(owner_of, targets):
        give(w_out.at[rows_of(owner, 16)], 0, width)
        give(w_down.at[rows_of(owner, 16)], 5 * width, units)
    total = jnp.zeros((width, LANES), fp32)
    lane = lax.broadcasted_iota(jnp.int32, (width, LANES), 1)
    for i, name in enumerate(NAMES):
        total = total + jnp.where(lane == COLUMNS[name], jnp.sum(acc[i], axis=1, keepdims=True), 0.0)
    up_sum = jnp.sum(acc_up[...], axis=1, keepdims=True).reshape(PIECES, UP_COLUMNS, 16, 1)
    for c in range(UP_COLUMNS):
        total = total + jnp.where(lane == UP_AT + c, up_sum[:, c].reshape(width, 1), 0.0)
    small_ref[...] = total
    leave(small_ref, small_hbm)
    for copy in copies:
        copy.wait()
    for copy in outs:
        copy.wait()


def feed(me, b_bufs, w1, turned, series, attn, cotangent, regions, rows, units):
    width, tokens = attn.shape
    half_set = jax.ShapeDtypeStruct((PIECES // 2, 16, 5 * width + units), half)
    low_all = pltpu.VMEM((width, tokens), half)
    parts = ((0, tokens // 2 // TILE * TILE), (tokens // 2 // TILE * TILE, tokens - tokens // 2 // TILE * TILE))
    return pl.pallas_call(
        functools.partial(feed_kernel, len(b_bufs), rows, regions, parts),
        in_specs=[SMEM] + [ANY] * len(b_bufs) + [ANY] * 5,
        out_specs=[ANY] * 6,
        out_shape=[
            jax.ShapeDtypeStruct((regions, rows, width), half),
            jax.ShapeDtypeStruct((width, tokens), half),
            jax.ShapeDtypeStruct((width, tokens), fp32),
            half_set,
            half_set,
            jax.ShapeDtypeStruct((width, LANES), fp32),
        ],
        scratch_shapes=[
            pltpu.VMEM(w1.shape, half),
            pltpu.VMEM(turned.shape, fp32),
            pltpu.VMEM(series.shape, half),
            pltpu.VMEM((width, LANES), fp32),
            pltpu.VMEM((width, width), half),
            pltpu.VMEM((width, width), half),
            pltpu.VMEM((units, width), half),
            pltpu.VMEM((width, units), half),
            pltpu.VMEM((width, units), half),
            pltpu.VMEM((units, width), half),
            pltpu.VMEM((units, LANES), fp32),
            pltpu.VMEM((len(NAMES), width, LANES), fp32),
            low_all,
            low_all,
            pltpu.VMEM((units, tokens), half),
            pltpu.VMEM((units, tokens), half),
            low_all,
            low_all,
            low_all,
            low_all,
            pltpu.VMEM((width, tokens), fp32),
            pltpu.VMEM((width, tokens), fp32),
            pltpu.VMEM((tokens, width), half),
            pltpu.VMEM((len(NAMES), width, LANES), fp32),
            pltpu.VMEM((units, LANES), fp32),
            pltpu.SemaphoreType.DMA((2 * len(parts),)),
            pltpu.SemaphoreType.DMA((4,)),
            pltpu.SemaphoreType.DMA((regions + 2 * len(parts) + 1,)),
            pltpu.SemaphoreType.DMA,
        ],
        compiler_params=params(),
        cost_estimate=cost(4e10, 2e7),
    )(me, *b_bufs, w1, turned, series, attn, cotangent)


def heads_back(per_step, rows, refs, store):
    q_ref, k_ref, v_ref, attn_ref, gattn_ref, log_ref, qf_ref, kf_ref = refs
    padded = qf_ref.shape[2]
    query_f, key_f = qf_ref[0], kf_ref[0]
    blocks = [(s, min(TILE, rows - s)) for s in range(0, rows, TILE)]
    filler = jnp.zeros((13, padded), fp32)

    def in_three(row):
        first = row.astype(half).astype(fp32)
        left = row - first
        second = left.astype(half).astype(fp32)
        return jnp.concatenate([first, second, left - second, filler], axis=0).astype(half)

    for i in range(per_step):
        head = slice(i * HEAD_DIM, (i + 1) * HEAD_DIM)
        query, keys, values, grad = q_ref[head, :], k_ref[head, :], v_ref[head, :], gattn_ref[head, :]
        inner = jnp.sum(grad.astype(fp32) * attn_ref[head, :].astype(fp32), axis=0, keepdims=True)
        query_a = jnp.concatenate([query, in_three(-log_ref[i]), query_f[16:]], axis=0).T
        grad_a = jnp.concatenate([grad, in_three(-inner), jnp.zeros((48, padded), half)], axis=0).T
        keys_a = jnp.concatenate([keys, key_f], axis=0)
        values_a = jnp.concatenate([values, key_f], axis=0)
        grad_keys = grad_values = None
        grad_query = []
        for s, n in blocks:
            probs = jnp.exp(dot(query_a[s : s + n], keys_a))
            raw = (probs * dot(grad_a[s : s + n], values_a)).astype(half)
            more_v = dot(grad[:, s : s + n], probs.astype(half))
            more_k = dot(query[:, s : s + n], raw)
            grad_values = more_v if grad_values is None else grad_values + more_v
            grad_keys = more_k if grad_keys is None else grad_keys + more_k
            grad_query.append((dot(keys, raw, 1, 1) * HEAD_DIM**-0.5).astype(half))
        grad_query.append(jnp.zeros((HEAD_DIM, padded - rows), half))
        store(i, (jnp.concatenate(grad_query, axis=1), grad_keys.astype(half), grad_values.astype(half)))


def attend_back_kernel(per_step, rows, *refs):
    grad_ref = refs[8]

    def store(i, three):
        for part, value in enumerate(three):
            grad_ref[0, part, i * HEAD_DIM : (i + 1) * HEAD_DIM, :] = value

    heads_back(per_step, rows, refs[:8], store)


def finish_kernel(per_step, rows, counts, me_ref, *refs):
    ins, done_refs, refs = refs[:8], refs[8 : 8 + len(counts)], refs[8 + len(counts) :]
    first = sum(counts)
    emb_ref, gres_ref, series_ref, wqkv_t_ref, w1_ref, small_ref, keep_ref, send_ref, lbg_hbm, lbg_ref, *refs = refs
    grad_s, emb_s, gres_s, wqkv_t, g_qkv, g_one, sem, sem_out = refs
    step, steps = pl.program_id(0), pl.num_programs(0)
    width, tokens = emb_s.shape
    regions, lags, _ = lbg_ref.shape
    padded = tokens // regions
    groups = HEADS // per_step
    height = per_step * HEAD_DIM
    brought = [
        pltpu.make_async_copy(emb_ref, emb_s, sem),
        pltpu.make_async_copy(gres_ref, gres_s, sem),
        pltpu.make_async_copy(wqkv_t_ref, wqkv_t, sem),
    ]
    done = [ref.at[t] for ref in done_refs for t in range(ref.shape[0])]
    for t in range(first):
        for part in range(3):
            brought.append(
                pltpu.make_async_copy(
                    done[t].at[part],
                    grad_s.at[
                        pl.ds(part * width + (t % groups) * height, height), pl.ds(t // groups * padded, padded)
                    ],
                    sem,
                )
            )

    @pl.when(step == 0)
    def _():
        for copy in brought:
            copy.start()

    now = step + first
    lanes = pl.ds(pl.multiple_of(now // groups * padded, LANES), padded)
    rows_at = lax.rem(now, groups) * height

    def store(i, three):
        for part, value in enumerate(three):
            at = pl.multiple_of(part * width + rows_at + i * HEAD_DIM, HEAD_DIM)
            grad_s[pl.ds(at, HEAD_DIM), lanes] = value

    heads_back(per_step, rows, ins, store)

    @pl.when(step == steps - 1)
    def _():
        for copy in brought:
            copy.wait()
        owner_of = owners(me_ref[0])
        for part in range(3):
            at = slice(part * width, (part + 1) * width)
            g_qkv[at, :] = dot(grad_s[at, :], emb_s[...], 1, 1).astype(half)
        copies = []
        for r, owner in enumerate(owner_of):
            target = (keep_ref if r < PIECES // 2 else send_ref).at[r % (PIECES // 2)]
            for j in range(3):
                copies.append(
                    pltpu.make_async_copy(
                        g_qkv.at[pl.ds(pl.multiple_of(owner * 48 + j * 16, 16), 16)],
                        target.at[:, pl.ds(j * width, width)],
                        sem_out.at[0],
                    )
                )
        for copy in copies:
            copy.start()
        total = small_ref[...]
        lane = lax.broadcasted_iota(jnp.int32, total.shape, 1)
        for i, part in enumerate((0, 2)):
            bias = fold(grad_s[part * width : (part + 1) * width, :].astype(fp32))
            total = total + jnp.where(lane == BIAS_AT + 1 + i, jnp.sum(bias, axis=1, keepdims=True), 0.0)
        low = (gres_s[...] + dot(wqkv_t[...], grad_s[...])).astype(half)
        total = total + dot(low, series_ref[...], 1, 1)
        for r in range(regions):
            lbg_ref[r] = dot(w1_ref[...], low[:, r * padded : (r + 1) * padded], 0, 0)[:lags, :rows]
        lbg_out = pltpu.make_async_copy(lbg_ref, lbg_hbm, sem_out.at[2])
        lbg_out.start()
        g_one[...] = total.astype(half)
        more = []
        for r, owner in enumerate(owner_of):
            target = (keep_ref if r < PIECES // 2 else send_ref).at[r % (PIECES // 2)]
            more.append(
                pltpu.make_async_copy(
                    g_one.at[rows_of(owner, 16)], target.at[:, pl.ds(3 * width, LANES)], sem_out.at[1]
                )
            )
        for copy in more:
            copy.start()
        for copy in copies:
            copy.wait()
        for copy in more:
            copy.wait()
        lbg_out.wait()


def back_operands(qkv, attn, grad_attn, logs, query_f, key_f, per_step, first):
    heads, feature, log = head_blocks(query_f.shape[2], per_step, first)
    specs = [heads(0), heads(1), heads(2), heads(), heads(), log, feature, feature]
    return specs, (qkv, qkv, qkv, attn, grad_attn, logs, query_f, key_f)


def attend_back(qkv, attn, grad_attn, logs, query_f, key_f, rows, per_step, first, steps):
    padded = query_f.shape[2]
    specs, operands = back_operands(qkv, attn, grad_attn, logs, query_f, key_f, per_step, first)
    shape = (3, per_step * HEAD_DIM, padded)
    grad_spec = pl.BlockSpec((1, *shape), lambda t: (t, 0, 0, 0))
    grad_shape = jax.ShapeDtypeStruct((steps, *shape), half)
    return pl.pallas_call(
        functools.partial(attend_back_kernel, per_step, rows),
        grid=(steps,),
        in_specs=specs,
        out_specs=grad_spec,
        out_shape=grad_shape,
        compiler_params=params(56),
        cost_estimate=cost(2e10, 1e7),
    )(*operands)


def finish(me, qkv, attn, grad_attn, logs, query_f, key_f, done, embed_low, grad_resid, series, wqkv_t, w1, small, rows, lags, per_step):
    regions, _, padded = query_f.shape
    width, tokens = attn.shape
    counts = tuple(value.shape[0] for value in done)
    first = sum(counts)
    specs, operands = back_operands(qkv, attn, grad_attn, logs, query_f, key_f, per_step, first)
    half_set = jax.ShapeDtypeStruct((PIECES // 2, 16, 3 * width + LANES), half)
    return pl.pallas_call(
        functools.partial(finish_kernel, per_step, rows, counts),
        grid=(logs.shape[0] // per_step - first,),
        in_specs=[SMEM] + specs + [ANY] * len(done) + [ANY, ANY, VMEM, ANY, VMEM, VMEM],
        out_specs=[ANY, ANY, ANY],
        out_shape=[half_set, half_set, jax.ShapeDtypeStruct((regions, lags, rows), fp32)],
        scratch_shapes=[
            pltpu.VMEM((regions, lags, rows), fp32),
            pltpu.VMEM((3 * width, tokens), half),
            pltpu.VMEM((width, tokens), half),
            pltpu.VMEM((width, tokens), fp32),
            pltpu.VMEM((width, 3 * width), half),
            pltpu.VMEM((3 * width, width), half),
            pltpu.VMEM((width, LANES), half),
            pltpu.SemaphoreType.DMA,
            pltpu.SemaphoreType.DMA((3,)),
        ],
        compiler_params=params(54),
        cost_estimate=cost(4e10, 2e7),
    )(me, *operands, *done, embed_low, grad_resid, series, wqkv_t, w1, small)


def send(value, offset):
    return lax.ppermute(value, AXES, [(i, i ^ offset) for i in range(PIECES)])


def after(value, *others):
    return lax.optimization_barrier((value, *others))[0]


def along_z(piece):
    return jnp.stack([piece] + [send(piece, 2 * s) for s in range(1, 4)])


def along_plane(value):
    return [value] + [send(value, offset) for offset in (1, 16, 17)]


def along_core(plane):
    return plane + [send(part, 8) for part in plane]


def add(*terms):
    return sum(term.astype(fp32) for term in terms)


def quarters(low):
    return [low[4 * i : 4 * i + 4] for i in range(4)]


def add_core(keep, got):
    return [add(*pair).astype(half) for pair in zip(quarters(keep), quarters(got))]


def sum_plane(lows):
    return [lows[0]] + [send(low, offset) for low, offset in zip(lows[1:], (1, 16, 17))]


def add_plane(parts):
    return [add(*[part[s] for part in parts]).astype(half) for s in range(4)]


def sum_z(lows):
    return [lows[0]] + [send(lows[s], 2 * s) for s in range(1, 4)]


def stacked(value, width):
    return jnp.concatenate([value[:, s : s + width] for s in range(0, value.shape[1], width)], axis=0)


def unpack_one(packed, lags):
    up = packed[:, UP_AT : UP_AT + UP_COLUMNS].reshape(-1, 16, UP_COLUMNS).transpose(0, 2, 1).reshape(-1)
    return packed[:, :lags], packed[:, BIAS_AT:GAIN_AT].T, packed[:, GAIN_AT:UP_AT].T, up


def body(
    ours,
    lookback,
    bucket_size,
    variate_mask,
    w_embed,
    w_qkv,
    w_out,
    w_up,
    w_down,
    up_bias,
    biases,
    gains,
    cotangent,
):
    regions, rows, lags = lookback.shape
    width = w_qkv.shape[1]
    units = w_down.shape[1]
    padded = -(-rows // LANES) * LANES
    per_step = 4
    steps = regions * HEADS // per_step
    per_step_f = 2
    steps_f = regions * HEADS // per_step_f
    lookback_t = lookback.transpose(0, 2, 1)
    series, masked, query_f, key_f = prepare(bucket_size, variate_mask, lookback_t, cotangent, padded, 32)

    if ours:
        index = lax.axis_index(AXES).astype(jnp.int32)
        piece_a, piece_b = pack(w_embed, w_qkv, w_out, w_up, w_down, up_bias, biases, gains)
        z_a = after(along_z(piece_a), series)
        z_b = along_z(piece_b)
        plane_a = along_plane(z_a)
        plane_b = along_plane(after(z_b, z_a))
        a_bufs = along_core(plane_a)
    else:
        index = jnp.zeros((), jnp.int32)

        def whole(value, axis=0):
            return lax.all_gather(value, AXES, axis=axis, tiled=True)

        def cut(value, axis=0):
            shape = value.shape[:axis] + (PIECES, value.shape[axis] // PIECES) + value.shape[axis + 1 :]
            return jnp.moveaxis(value.reshape(shape), axis, 0)

        early = jnp.array(OFFSETS)
        short = jax.vmap(short_block)(cut(whole(biases, 1), 1), cut(whole(gains, 1), 1), cut(whole(up_bias)))
        a_bufs = [jax.vmap(first_piece)(cut(whole(w_embed)), short, cut(whole(w_qkv)))[early]]
        b_bufs = [jax.vmap(second_piece)(cut(whole(w_out)), cut(whole(w_up)), cut(whole(w_down)))[early]]
    me = index.reshape(1)

    qkv, embed_low, attn, logs, w1, turned, wqkv_t = project(
        me, a_bufs, series, query_f, key_f, rows, width, per_step_f, steps_f - 1
    )
    if ours:
        b_bufs = along_core(plane_b[:1]) + along_core([after(part, logs) for part in plane_b[1:]])
        b_bufs = [b_bufs[0], *b_bufs[2:5], b_bufs[1], *b_bufs[5:]]
    attn, logs = attend(qkv, attn, logs, query_f, key_f, rows, per_step_f, steps_f - 1)
    layer_out, grad_attn, grad_resid, keep_b, send_b, sums = feed(
        me, b_bufs, w1, turned, series, attn, masked, regions, rows, units
    )
    if ours:
        core_b = send(send_b, 8)
    done = [attend_back(qkv, attn, grad_attn, logs, query_f, key_f, rows, per_step, 0, steps - 2)]
    if ours:
        lows_b = add_core(keep_b, after(core_b, *done))
        parts_b = sum_plane(lows_b)
        grad_attn = after(grad_attn, *lows_b)
    keep_a, send_a, lookback_grad = finish(
        me, qkv, attn, grad_attn, logs, query_f, key_f, done, embed_low, grad_resid, series, wqkv_t, w1, sums, rows, lags, per_step
    )
    lookback_grad = lookback_grad.transpose(0, 2, 1)

    def parts_of(grad_a, grad_b):
        w_qkv_part = stacked(grad_a[:, : 3 * width], width)
        return w_qkv_part, grad_a[:, 3 * width :], grad_b[:, :width], stacked(grad_b[:, width : 5 * width], width), grad_b[:, 5 * width :]

    if ours:
        core_a = send(send_a, 8)
        parts_b = sum_z(add_plane([after(part, keep_a) for part in parts_b]))
        lows_a = add_core(keep_a, after(core_a, parts_b[0]))
        lows_a = add_plane(sum_plane(lows_a))
        grad_out, grad_up, grad_down = unpack_second([after(part, *lows_a) for part in parts_b], width, units)
        parts_a = sum_z(lows_a)
        grad_qkv, grad_embed, grad_up_bias, grad_biases, grad_gains = unpack_first(parts_a, width, lags)
    else:
        def shared(value, axis=0):
            return lax.psum_scatter(value, AXES, scatter_dimension=axis, tiled=True)

        order = jnp.argsort(jnp.array(OFFSETS, jnp.int32))
        grad_a = jnp.concatenate([keep_a, send_a], axis=0).astype(fp32)[order]
        grad_b = jnp.concatenate([keep_b, send_b], axis=0).astype(fp32)[order]
        whole_parts = [value.reshape(-1, value.shape[-1]) for value in jax.vmap(parts_of)(grad_a, grad_b)]
        grad_embed, grad_biases, grad_gains, grad_up_bias = unpack_one(whole_parts[1], lags)
        grad_qkv, grad_out, grad_up, grad_down = (shared(whole_parts[i]) for i in (0, 2, 3, 4))
        grad_embed, grad_up_bias = shared(grad_embed), shared(grad_up_bias)
        grad_biases, grad_gains = shared(grad_biases, 1), shared(grad_gains, 1)
    return (
        layer_out,
        lookback_grad,
        grad_embed,
        grad_qkv,
        grad_out,
        grad_up,
        grad_down,
        grad_up_bias,
        grad_biases,
        grad_gains,
    )


def solution(mesh):
    one = P(AXES)
    rows = P(AXES, None)
    blocks = P(AXES, None, None)
    columns = P(None, AXES)
    in_specs = (blocks, one, rows, rows, rows, rows, rows, rows, one, columns, columns, blocks)
    out_specs = (blocks, blocks, rows, rows, rows, rows, rows, one, columns, columns)
    ours = tuple(mesh.shape[axis] for axis in AXES) == (4, 8)
    return jax.shard_map(
        functools.partial(body, ours), mesh=mesh, in_specs=in_specs, out_specs=out_specs, check_vma=False
    )
```
